32 devices in a mesh: dp: 16 (over z, y, x), head: 2 (over core).
Axes of the slice: x: 2, y: 2, z: 4, core: 2. Of those that a mesh axis runs over, the one named last changes fastest.
Arguments:
- hidden_in: bfloat16 [32768, 768], P('dp'), may hold values from -6 to 6
- lengths: int32 [32, 8], P('dp'), may hold values from 1 to 512, 1024 in all within a row
- buckets: int32 [2047], replicated, may hold values from 0 to 31, as said below
- gain_attn: float32 [768], replicated, may hold values from 0.5 to 1.5
- gain_ffn: float32 [768], replicated, may hold values from 0.5 to 1.5
- w_query: bfloat16 [768, 768], P(None, 'head'), may hold values from -0.02734375 to 0.02734375
- w_key: bfloat16 [768, 768], P(None, 'head'), may hold values from -0.21875 to 0.21875
- w_value: bfloat16 [768, 768], P(None, 'head'), may hold values from -0.21875 to 0.21875
- w_attn_out: bfloat16 [768, 768], P('head'), may hold values from -0.875 to 0.875
- w_in: bfloat16 [768, 3072], P(None, 'head'), may hold values from -0.21875 to 0.21875
- w_ffn_out: bfloat16 [3072, 768], P('head'), may hold values from -0.109375 to 0.109375
- rel_bias: float32 [32, 12], P(None, 'head'), may hold values from -4 to 4
- out_grad: bfloat16 [32768, 768], P(('dp', 'head'))
- adapter_weights: float32 [2512], replicated, may hold values from -4 to 4
- first_moment: float32 [2512], replicated
- second_moment: float32 [2512], replicated, as said below
- ema_weights: float32 [2512], replicated, may hold values from -4 to 4
Outputs:
- layer_out: float32 [32768, 768], P(('dp', 'head'))
- grad_in: float32 [32768, 768], P(('dp', 'head'))
- new_weights: float32 [2512], replicated
- new_first: float32 [2512], replicated
- new_second: float32 [2512], replicated
- new_ema: float32 [2512], replicated
The draws below stay inside these ranges and needn't reach their ends.
Inputs may be any that keep to these rules, and one draw needn't show every extreme that they name: For keys before the query the bucket is below 16, for keys after it 32 / 2 or more, offset 0 has bucket 0; buckets never fall with distance on either side; the largest distance on each side has the highest bucket of that side. Each row's 8 lengths sum to 1024. `second_moment`: every entry is positive.
All inputs are finite; a program needn't handle non-finite values.
Results may differ from the reference program's by a relative error of at most 0.02.
Values may be sent and summed in bfloat16 or wider, within the bound.
No kernel may reach another device: no remote copies, remote signals or barrier semaphores. Data moves between devices by JAX's collectives and lax.ppermute only.
A program may use at most 320 MiB of HBM per device.

```python
import math
import jax
import jax.numpy as jnp
import numpy as np
from jax import lax

D = 768
H = 12
DH = 64
FF = 3072
NB = 32
KRON = 4
BOTTLE = 48
SEQ = 1024
QBLK = 512
DOCS = 8
MOST = 512
STEP = 10
ROWS = 32
TOKENS = 32768
P_SIZE = 2512


def moment_scales():
    root_tokens = math.sqrt(TOKENS)
    cot_size = 2.0
    bottle_size = 0.6 * cot_size * math.sqrt(KRON * D / BOTTLE)
    down_entry = 0.65 * bottle_size * root_tokens
    up_entry = 0.8 * cot_size * root_tokens
    down_factor = (KRON * D) ** (-0.5)
    up_factor = BOTTLE ** (-0.5)
    factors = [math.sqrt(D * BOTTLE) / KRON * (down_factor * down_entry + up_factor * up_entry), math.sqrt(KRON * BOTTLE) * down_factor * down_entry, down_entry, math.sqrt(KRON * D / BOTTLE) * up_entry, math.sqrt(KRON) * up_entry, bottle_size * root_tokens, cot_size * root_tokens]
    widths = [KRON * KRON * KRON, D, BOTTLE, BOTTLE, D, BOTTLE, D]
    edges = []
    running = 0
    for width in widths:
        running = running + width
        edges.append(running)
    index = jnp.arange(P_SIZE)
    scales = jnp.full((P_SIZE,), factors[6], jnp.float32)
    for place in range(5, -1, -1):
        scales = jnp.where(index < edges[place], factors[place], scales)
    return scales


def draw_buckets(key, part):
    key = jax.random.fold_in(key, 11)
    half_count = NB // 2
    distance = jnp.arange(SEQ, dtype=jnp.int32)
    picks = jax.random.randint(key, (2, SEQ), 0, distance[None, :] // 2 + 1)
    steps = jnp.where(distance[None, :] == 0, 0, (picks == 0).astype(jnp.int32))
    counted = jnp.minimum(jnp.cumsum(steps, axis=1), half_count - 1)
    counted = jnp.where(distance[None, :] == SEQ - 1, half_count - 1, counted)
    before = counted[0, ::-1][:SEQ - 1]
    after = jnp.where(distance == 0, 0, half_count + counted[1])
    return jnp.concatenate([before, after]).astype(jnp.int32)


def draw_out_grad(key, part):
    key = jax.random.fold_in(key, 23)
    ramp = jnp.arange(TOKENS, dtype=jnp.float32)[:, None] / (TOKENS - 1)
    noise = jax.random.normal(key, (TOKENS, D), jnp.float32)
    return (noise * (1.0 + 2.0 * ramp)).astype(jnp.bfloat16)


def draw_first_moment(key, part):
    key = jax.random.fold_in(key, 31)
    noise = jax.random.normal(key, (P_SIZE,), jnp.float32)
    return noise * moment_scales() * (0.1 / 0.9)


def draw_second_moment(key, part):
    key = jax.random.fold_in(key, 37)
    spread = jnp.exp(jax.random.uniform(key, (P_SIZE,), jnp.float32, 0.0, math.log(4.0)))
    scales = moment_scales()
    return scales * scales * (0.001 / 0.999) * spread


def levels(key, shape, split, least, high):
    factor_of, own = 1.0, jax.random.fold_in(key, 6)
    for dim, shards_of in split:
        heights = jnp.exp(jax.random.uniform(jax.random.fold_in(own, dim), (shards_of,), jnp.float32, least / len(split), high / len(split)))
        factor_of = factor_of * jnp.repeat(heights, shape[dim] // shards_of).reshape([-1 if axis == dim else 1 for axis in range(len(shape))])
    return factor_of


def split_up(number_of, total, bound, skew):
    loads = [(1 << 20) // math.isqrt(rank ** skew) + 1 for rank in range(2, number_of + 1)]
    rest, counts = total - bound - (number_of - 1), [1] * (number_of - 1)
    while rest > 0:
        movable = [i for i in range(number_of - 1) if counts[i] < bound]
        pool, budget = sum([loads[i] for i in movable]), rest
        for i in movable:
            addition = min(bound - counts[i], max(1, budget * loads[i] // pool), rest)
            counts[i] = counts[i] + addition
            rest = rest - addition
    return np.array([bound] + counts)


def ragged(key, count, total, bound, slope):
    if count == 2:
        one = jax.random.randint(key, (), max(1, total - bound), min(bound, total - 1) + 1)
        return jnp.stack([one, total - one])
    sizes = jnp.asarray(split_up(count, total, bound, slope), jnp.int32)
    pairs = (count - 1) // 2
    giver, taker = sizes[1:1 + 2 * pairs:2], sizes[2:2 + 2 * pairs:2]
    room = jnp.minimum(giver - 1, bound - taker)
    shifted = jax.random.randint(jax.random.fold_in(key, 1), (pairs,), 0, 1 << 20) % (room + 1)
    sizes = sizes.at[1:1 + 2 * pairs:2].set(giver - shifted).at[2:2 + 2 * pairs:2].set(taker + shifted)
    return sizes[jax.random.permutation(jax.random.fold_in(key, 2), count)]


def normal_values(key, dims, scale, limit, cuts=(), kind=jnp.bfloat16):
    loudness = levels(key, dims, cuts, -0.22, 0.18) if cuts else 1.0
    array = jax.random.normal(key, dims, jnp.float32) * scale * loudness
    return jnp.minimum(jnp.maximum(array, -limit), limit).astype(kind)


def setup_inputs(seed: int = 0) -> dict:
    key_list = jax.random.split(jax.random.key(seed), 18)
    hidden_in = normal_values(key_list[0], (TOKENS, D), 1.0, 6.0, ((0, 16),))
    lengths = jax.vmap(lambda own: ragged(own, DOCS, SEQ, MOST, 2))(jax.random.split(key_list[1], ROWS)).reshape((ROWS, DOCS)).astype(jnp.int32)
    buckets = draw_buckets(jax.random.fold_in(key_list[17], 71), 0)
    gain_attn = jnp.clip(1.0 + 0.1 * jax.random.normal(key_list[3], (D,), jnp.float32), 0.5, 1.5)
    gain_ffn = jnp.clip(1.0 + 0.1 * jax.random.normal(key_list[4], (D,), jnp.float32), 0.5, 1.5)
    w_query = normal_values(key_list[5], (D, D), (D * DH) ** -0.5, 0.02734375, ((1, 2),))
    w_key = normal_values(key_list[6], (D, D), D ** -0.5, 0.21875, ((1, 2),))
    w_value = normal_values(key_list[7], (D, D), D ** -0.5, 0.21875, ((1, 2),))
    w_attn_out = normal_values(key_list[8], (D, D), (D // 16) ** -0.5, 0.875, ((0, 2),))
    w_in = normal_values(key_list[9], (D, FF), D ** -0.5, 0.21875, ((1, 2),))
    w_ffn_out = normal_values(key_list[10], (FF, D), FF ** -0.5, 0.109375, ((0, 2),))
    rel_bias = normal_values(key_list[11], (NB, H), 1.0, 4.0, ((1, 2),), jnp.float32)
    out_grad = draw_out_grad(jax.random.fold_in(key_list[17], 71), 0)
    adapter_weights = normal_values(key_list[13], (P_SIZE,), 1.0, 4.0, (), jnp.float32)
    first_moment = draw_first_moment(jax.random.fold_in(key_list[17], 71), 0)
    second_moment = draw_second_moment(jax.random.fold_in(key_list[17], 71), 0)
    ema_weights = normal_values(key_list[16], (P_SIZE,), 1.0, 4.0, (), jnp.float32)
    return {"hidden_in": hidden_in, "lengths": lengths, "buckets": buckets, "gain_attn": gain_attn, "gain_ffn": gain_ffn, "w_query": w_query, "w_key": w_key, "w_value": w_value, "w_attn_out": w_attn_out, "w_in": w_in, "w_ffn_out": w_ffn_out, "rel_bias": rel_bias, "out_grad": out_grad, "adapter_weights": adapter_weights, "first_moment": first_moment, "second_moment": second_moment, "ema_weights": ema_weights}


@jax.custom_vjp
def low(v):
    return lax.optimization_barrier(v.astype(jnp.bfloat16)).astype(jnp.float32)

@jax.custom_vjp
def low_back(v):
    return v

def low_keep(v):
    return (low(v), None)

def low_pass(kept, grad):
    return (grad,)

def back_keep(v):
    return (v, None)

def back_low(kept, grad):
    return (low(grad),)
low.defvjp(low_keep, low_pass)
low_back.defvjp(back_keep, back_low)
highest = lax.Precision.HIGHEST
eps_norm = 1e-06
beta_one = 0.9
beta_two = 0.999
adam_eps = 1e-08
learn_rate = 0.6
weight_decay = 0.01
ema_decay = 0.9
masked_score = -1e+30

def both_ways(value):
    return low_back(low(value))

def product(left, right):
    return jnp.dot(left, right, precision=highest, preferred_element_type=jnp.float32)

def rms_scale(value, gain):
    return value * lax.rsqrt(lax.optimization_barrier(jnp.mean(value * value, axis=-1, keepdims=True)) + eps_norm) * gain

def segment_ids(row_lengths):
    doc_ends = jnp.cumsum(row_lengths.astype(jnp.int32))
    places = jnp.arange(SEQ, dtype=jnp.int32)
    return lax.optimization_barrier(jnp.sum((places[:, None] >= doc_ends[None, :]).astype(jnp.int32), axis=1))

def unpack(flat):
    widths = (KRON * KRON * KRON, D, BOTTLE, BOTTLE, D, BOTTLE, D)
    pieces = []
    first_item = 0
    for width in widths:
        pieces.append(flat[first_item:first_item + width])
        first_item = first_item + width
    kron_a = pieces[0].reshape(KRON, KRON, KRON)
    down_left = pieces[1].reshape(KRON, D // KRON)
    down_right = pieces[2].reshape(KRON, BOTTLE // KRON)
    up_left = pieces[3].reshape(KRON, BOTTLE // KRON)
    up_right = pieces[4].reshape(KRON, D // KRON)
    return (kron_a, down_left, down_right, up_left, up_right, pieces[5], pieces[6])

def adapter_matrices(flat):
    kron_a, down_left, down_right, up_left, up_right, bias_down, bias_up = unpack(flat)
    down_factor = (KRON * D) ** (-0.5)
    up_factor = BOTTLE ** (-0.5)
    down_mat = jnp.einsum('nab,np,nq->apbq', kron_a, down_left, down_right * down_factor, precision=highest).reshape(D, BOTTLE)
    up_mat = jnp.einsum('nba,nq,np->bqap', kron_a, up_left, up_right * up_factor, precision=highest).reshape(BOTTLE, D)
    return (down_mat, up_mat, bias_down, bias_up)

def forward_row(row_in, flat, same_doc, bias_full, frozen):
    query_proj, key_proj, value_proj, out_proj, in_proj, back_proj, gain_attn, gain_ffn = frozen
    normed = low(rms_scale(row_in, gain_attn))

    def heads_of(value):
        return value.reshape(SEQ, H, DH).transpose(1, 0, 2)
    queries = heads_of(both_ways(product(normed, query_proj)))
    keys_all = heads_of(both_ways(product(normed, key_proj)))
    values_all = heads_of(both_ways(product(normed, value_proj)))

    def attend(first_row):
        query_block = lax.dynamic_slice_in_dim(queries, first_row, QBLK, 1)
        bias_block = lax.dynamic_slice_in_dim(bias_full, first_row, QBLK, 1)
        mask_block = lax.dynamic_slice_in_dim(same_doc, first_row, QBLK, 0)
        scores = low_back(jnp.einsum('hqd,hkd->hqk', query_block, keys_all, precision=highest) + bias_block)
        scores = jnp.where(mask_block[None], scores, masked_score)
        row_peak = lax.optimization_barrier(jnp.max(scores, axis=-1, keepdims=True))
        expo = jnp.exp(scores - row_peak)
        prob_low = low(expo / lax.optimization_barrier(jnp.sum(expo, axis=-1, keepdims=True)))
        return jnp.einsum('hqk,hkd->hqd', prob_low, values_all, precision=highest)
    starts = jnp.arange(SEQ // QBLK, dtype=jnp.int32) * QBLK
    blocks = lax.map(jax.checkpoint(attend), starts)
    context = both_ways(blocks.transpose(0, 2, 1, 3).reshape(SEQ, D))
    residual = row_in + low_back(product(context, out_proj))
    ffn_normed = low(rms_scale(residual, gain_ffn))
    pre_act = low_back(product(ffn_normed, in_proj))
    hidden = low(jax.nn.gelu(pre_act))
    mixed = low_back(product(hidden, back_proj))
    down_mat, up_mat, bias_down, bias_up = adapter_matrices(flat)
    bottle_pre = low_back(product(low(mixed), low(down_mat)) + bias_down)
    bottle = low(jax.nn.gelu(bottle_pre))
    adapted = product(bottle, low(up_mat)) + bias_up
    return residual + mixed + adapted

def reference(hidden_in, lengths, buckets, gain_attn, gain_ffn, w_query, w_key, w_value, w_attn_out, w_in, w_ffn_out, rel_bias, out_grad, adapter_weights, first_moment, second_moment, ema_weights):
    frozen = tuple((weight.astype(jnp.float32) for weight in (w_query, w_key, w_value, w_attn_out, w_in, w_ffn_out))) + (gain_attn, gain_ffn)
    places = jnp.arange(SEQ, dtype=jnp.int32)
    offsets = places[None, :] - places[:, None] + SEQ - 1
    per_head = jnp.transpose(rel_bias[buckets], (1, 0))
    bias_full = jnp.take(per_head, offsets, axis=1)
    rows_in = hidden_in.astype(jnp.float32).reshape(-1, SEQ, D)
    rows_grad = out_grad.astype(jnp.float32).reshape(-1, SEQ, D)

    def one_row(grad_total, items):
        row_in, row_grad, row_lengths = items
        doc_ids = segment_ids(row_lengths)
        same_doc = doc_ids[:, None] == doc_ids[None, :]
        row_out, pull_back = jax.vjp(lambda value, flat: forward_row(value, flat, same_doc, bias_full, frozen), row_in, adapter_weights)
        input_grad, flat_grad = pull_back(row_grad)
        return (grad_total + flat_grad, (row_out, input_grad))
    adapter_grad, (outs_rows, grads_rows) = lax.scan(one_row, jnp.zeros_like(adapter_weights), (rows_in, rows_grad, lengths))
    new_first = beta_one * first_moment + (1.0 - beta_one) * adapter_grad
    new_second = beta_two * second_moment + (1.0 - beta_two) * adapter_grad * adapter_grad
    first_hat = new_first / (1.0 - beta_one ** STEP)
    second_hat = new_second / (1.0 - beta_two ** STEP)
    new_weights = adapter_weights - learn_rate * (first_hat / (jnp.sqrt(second_hat) + adam_eps) + weight_decay * adapter_weights)
    new_ema = ema_decay * ema_weights + (1.0 - ema_decay) * new_weights
    return (outs_rows.reshape(-1, D), grads_rows.reshape(-1, D), new_weights, new_first, new_second, new_ema)
```

```python
import functools

import jax
import jax.numpy as jnp
from jax import lax
from jax.experimental import pallas as pl
from jax.experimental.pallas import tpu as pltpu
from jax.sharding import PartitionSpec as P

D = 768
DH = 64
KRON = 4
BOTTLE = 48
SEQ = 1024
MOST = 512
STEP = 10
QB = 256
KB = 256
NQ = SEQ // QB
PAIR = 2 * DH
FCHUNK = 512
REACH = QB + MOST - 128
SPREAD = REACH + MOST + QB
CODES = SPREAD + 128
VMEM_BYTES = 60 * 2**20

eps_norm = 1e-06
beta_one = 0.9
beta_two = 0.999
adam_eps = 1e-08
learn_rate = 0.6
weight_decay = 0.01
ema_decay = 0.9
masked_score = -1e30
highest = lax.Precision.HIGHEST
f32 = jnp.float32
bf16 = jnp.bfloat16


def nn(left, right):
    return lax.dot_general(left, right, (((1,), (0,)), ((), ())), preferred_element_type=f32)


def nt(left, right):
    return lax.dot_general(left, right, (((1,), (1,)), ((), ())), preferred_element_type=f32)


def tn(left, right):
    return lax.dot_general(left, right, (((0,), (0,)), ((), ())), preferred_element_type=f32)


def row_plan(len_ref, own):
    docs = len_ref.shape[1]
    sizes = [len_ref[own, doc] for doc in range(docs)]
    longest, chosen = sizes[0], jnp.int32(0)
    for doc in range(1, docs):
        longer = sizes[doc] > longest
        chosen = jnp.where(longer, doc, chosen)
        longest = jnp.maximum(longest, sizes[doc])
    start = jnp.int32(0)
    for doc in range(docs):
        start = start + jnp.where(doc < chosen, sizes[doc], 0)
    ends, total = [], jnp.int32(0)
    for doc in range(docs):
        total = total + len_ref[own, lax.rem(chosen + doc, docs)]
        ends.append(total)
    return start, ends


def key_span(ends, first_row, last_row):
    begin, finish = jnp.int32(0), jnp.int32(SEQ)
    for end in ends:
        begin = jnp.where(end <= first_row, end, begin)
    for end in reversed(ends):
        finish = jnp.where(end > last_row, end, finish)
    return lax.div(begin, KB), lax.div(finish + (KB - 1), KB)


def to_packed(value, start):
    return pltpu.roll(value, lax.rem(SEQ - start, SEQ), 0)


def to_given(value, start):
    return pltpu.roll(value, start, 0)


def one_head(pair, half):
    lane = lax.broadcasted_iota(jnp.int32, pair.shape, 1)
    keep = lane < DH if half == 0 else lane >= DH
    return jnp.where(keep, pair, jnp.zeros_like(pair))


def attention_kernel(
    leading,
    own_ref,
    len_ref,
    x_ref,
    gain_ref,
    wq_ref,
    wk_ref,
    wv_ref,
    codes_ref,
    table_ref,
    *rest,
):
    if leading:
        prob_ref, q_ref, k_ref, v_ref, ctx_ref, packed_ref, vt_ref, bias_ref, dk_ref, dq_ref = rest
    else:
        prob_ref, q_ref, k_ref, v_ref, ctx_ref, vt_ref, bias_ref, dk_ref, dq_ref = rest[5:]
    heads = table_ref.shape[1]
    step = pl.program_id(0)
    start, ends = row_plan(len_ref, own_ref[0])

    @pl.when(step == 0)
    def _prepare():
        if leading:
            inputs = to_packed(x_ref[...].astype(f32), start)
            packed_ref[...] = inputs.astype(bf16)
        else:
            inputs = x_ref[...].astype(f32)
        scale = lax.rsqrt(jnp.mean(inputs * inputs, axis=1, keepdims=True) + eps_norm)
        normed = (inputs * scale * gain_ref[...]).astype(bf16)
        q_ref[...] = nn(normed, wq_ref[...]).astype(bf16)
        k_ref[...] = nn(normed, wk_ref[...]).astype(bf16)
        values = nn(normed, wv_ref[...]).astype(bf16)
        v_ref[...] = values
        vt_ref[...] = values.T
        row = lax.broadcasted_iota(jnp.int32, dk_ref.shape, 0)
        dk_ref[...] = sum((row >= end).astype(jnp.int32) for end in ends)
        lane = lax.broadcasted_iota(jnp.int32, dq_ref.shape, 1)
        dq_ref[...] = sum((lane >= end).astype(jnp.int32) for end in ends)
        bucket = lax.broadcasted_iota(jnp.int32, (table_ref.shape[0], CODES), 0)
        chosen = (bucket == codes_ref[...]).astype(f32)
        per_head = lax.dot_general(
            table_ref[...], chosen, (((0,), (0,)), ((), ())), precision=highest, preferred_element_type=f32
        )
        for head in range(heads):
            spread = jnp.broadcast_to(per_head[head : head + 1, :], (128, CODES))
            spread = pltpu.roll(spread, CODES - 127, 1, stride=1, stride_axis=0)
            bias_ref[head] = spread[:, :SPREAD]

    first_row = step * QB
    begin, finish = key_span(ends, first_row, first_row + QB - 1)

    def attend(count):
        rows = count * KB
        first_key = pl.multiple_of(begin * KB, KB)
        key_rows = pl.ds(first_key, rows)
        query_rows = pl.ds(pl.multiple_of(first_row, QB), QB)
        doc_key = jnp.concatenate([dk_ref[key_rows, :]] * (QB // 128), axis=1)
        same = doc_key == dq_ref[0:1, query_rows]
        for head in range(heads):
            lanes = slice(head // 2 * PAIR, head // 2 * PAIR + PAIR)
            band = slice(head * DH, head * DH + DH)
            queries = one_head(q_ref[query_rows, lanes], head % 2)
            scores = nt(k_ref[key_rows, lanes], queries)
            bias = jnp.concatenate(
                [
                    bias_ref[
                        head,
                        :,
                        pl.ds(pl.multiple_of(first_row - first_key + (REACH - part * 128), 128), QB),
                    ]
                    for part in range(rows // 128)
                ],
                axis=0,
            )
            scores = jnp.where(same, scores + bias, masked_score)
            expo = jnp.exp(scores - jnp.max(scores, axis=0, keepdims=True))
            prob = (expo * (1.0 / jnp.sum(expo, axis=0, keepdims=True))).astype(bf16)
            prob_ref[0, head, 0, 0:rows, :] = prob
            ctx_ref[band, query_rows] = nn(vt_ref[band, key_rows], prob).astype(bf16)

    for count in range(QB // KB, SEQ // KB + 1):
        pl.when(finish - begin == count)(functools.partial(attend, count))


def attention_forward(leading, own, lengths, x, gain, weights, codes, table, kept=None):
    width = weights[0].shape[1]
    heads = table.shape[1]
    group = 0 if leading else 1

    def whole(*shape):
        return pl.BlockSpec(shape, lambda i, *_: (0,) * len(shape))

    def side(*shape):
        return pl.BlockSpec(shape, lambda i, *_: (0, group))

    in_specs = [
        pl.BlockSpec((SEQ, D), lambda i, own_ref, len_ref: (own_ref[0], 0)) if leading else whole(SEQ, D),
        whole(1, D),
        whole(D, width),
        whole(D, width),
        whole(D, width),
        whole(1, CODES),
        whole(*table.shape),
    ]
    out_specs = [
        pl.BlockSpec((1, heads, 1, SEQ, QB), lambda i, *_: (group, 0, i, 0, 0)),
        side(SEQ, width),
        side(SEQ, width),
        side(SEQ, width),
        pl.BlockSpec((width, SEQ), lambda i, *_: (group, 0)),
    ]
    out_shape = [
        jax.ShapeDtypeStruct((2, heads, NQ, SEQ, QB), bf16),
        jax.ShapeDtypeStruct((SEQ, 2 * width), bf16),
        jax.ShapeDtypeStruct((SEQ, 2 * width), bf16),
        jax.ShapeDtypeStruct((SEQ, 2 * width), bf16),
        jax.ShapeDtypeStruct((2 * width, SEQ), bf16),
    ]
    aliases = {}
    extra = ()
    if leading:
        out_specs.append(whole(SEQ, D))
        out_shape.append(jax.ShapeDtypeStruct((SEQ, D), bf16))
    else:
        in_specs += [pl.BlockSpec(memory_space=pl.ANY)] * 5
        aliases = {9 + place: place for place in range(5)}
        extra = tuple(kept)
    return pl.pallas_call(
        functools.partial(attention_kernel, leading),
        grid_spec=pltpu.PrefetchScalarGridSpec(
            num_scalar_prefetch=2,
            grid=(NQ,),
            in_specs=in_specs,
            out_specs=out_specs,
            scratch_shapes=[
                pltpu.VMEM((width, SEQ), bf16),
                pltpu.VMEM((heads, 128, SPREAD), f32),
                pltpu.VMEM((SEQ, 128), jnp.int32),
                pltpu.VMEM((8, SEQ), jnp.int32),
            ],
        ),
        out_shape=out_shape,
        input_output_aliases=aliases,
        compiler_params=pltpu.CompilerParams(vmem_limit_bytes=VMEM_BYTES),
        name="attention_forward_own" if leading else "attention_forward_other",
    )(own, lengths, x, gain, *weights, codes, table, *extra)


root_two_over_pi = 0.7978845608028654
cubic = 0.044715


def gelu_both(value):
    square = value * value
    slow = jnp.tanh(value * (root_two_over_pi + (root_two_over_pi * cubic) * square))
    half = 0.5 * value
    act = half + half * slow
    slope = (0.5 + 0.5 * slow) + half * (1.0 - slow * slow) * (
        root_two_over_pi + (3.0 * root_two_over_pi * cubic) * square
    )
    return act, slope


def middle_kernel(
    own_ref,
    len_ref,
    ctx_hbm,
    x_hbm,
    grad_hbm,
    wo_own,
    wo_other,
    win_own,
    win_other,
    wout_own,
    wout_other,
    gain_ref,
    down_ref,
    up_ref,
    bias_down_ref,
    bias_up_ref,
    out_hbm,
    res_grad_hbm,
    dctx_ref,
    delta_ref,
    adapter_ref,
    ctx_ref,
    x_ref,
    grad_ref,
    wo_ref,
    win_ref,
    wout_ref,
    slope_ref,
    res_ref,
    out_ref,
    res_grad_ref,
    sems,
):
    start, _ = row_plan(len_ref, own_ref[0])
    half = wo_own.shape[0]
    hidden = win_own.shape[1]
    copies = [
        pltpu.make_async_copy(ctx_hbm, ctx_ref, sems.at[0]),
        pltpu.make_async_copy(wo_own, wo_ref.at[0:half, :], sems.at[1]),
        pltpu.make_async_copy(wo_other, wo_ref.at[half : 2 * half, :], sems.at[2]),
        pltpu.make_async_copy(x_hbm, x_ref, sems.at[3]),
        pltpu.make_async_copy(win_own, win_ref.at[:, 0:hidden], sems.at[4]),
        pltpu.make_async_copy(wout_own, wout_ref.at[0:hidden, :], sems.at[5]),
        pltpu.make_async_copy(win_other, win_ref.at[:, hidden : 2 * hidden], sems.at[6]),
        pltpu.make_async_copy(wout_other, wout_ref.at[hidden : 2 * hidden, :], sems.at[7]),
        pltpu.make_async_copy(grad_hbm, grad_ref, sems.at[8]),
    ]
    for copy in copies:
        copy.start()
    for copy in copies[:4]:
        copy.wait()
    residual = x_ref[...].astype(f32) + tn(ctx_ref[...], wo_ref[...])
    res_ref[...] = residual
    scale = lax.rsqrt(jnp.mean(residual * residual, axis=1, keepdims=True) + eps_norm)
    low = (residual * scale * gain_ref[...]).astype(bf16)
    for copy in copies[4:]:
        copy.wait()
    chunks = 2 * hidden // FCHUNK
    mixed = jnp.zeros((SEQ, D), f32)
    for chunk in range(chunks):
        cols = slice(chunk * FCHUNK, chunk * FCHUNK + FCHUNK)
        act, slope = gelu_both(nn(low, win_ref[:, cols]))
        slope_ref[:, cols] = slope.astype(bf16)
        mixed = mixed + nn(act.astype(bf16), wout_ref[cols, :])
    out_grad = to_packed(grad_ref[...].astype(f32), start)
    out_grad_low = out_grad.astype(bf16)
    down, up = down_ref[...], up_ref[...]
    mixed_low = mixed.astype(bf16)
    bottle, bottle_slope = gelu_both(nt(mixed_low, down) + bias_down_ref[...])
    bottle_low = bottle.astype(bf16)
    layer_out = res_ref[...] + mixed + nn(bottle_low, up) + bias_up_ref[...]
    out_ref[...] = to_given(layer_out, start)
    out_copy = pltpu.make_async_copy(out_ref, out_hbm, sems.at[9])
    out_copy.start()
    bottle_grad_wide = nt(out_grad_low, up) * bottle_slope
    bottle_grad = bottle_grad_wide.astype(bf16)
    adapter_ref[0, 0:BOTTLE, :] = tn(bottle_low, out_grad_low)
    adapter_ref[1, 0:BOTTLE, :] = tn(bottle_grad, mixed_low)
    adapter_ref[0, BOTTLE : BOTTLE + 8, :] = jnp.broadcast_to(
        jnp.sum(out_grad, axis=0, keepdims=True), (8, D)
    )
    adapter_ref[1, BOTTLE : BOTTLE + 8, 0:BOTTLE] = jnp.broadcast_to(
        jnp.sum(bottle_grad.astype(f32), axis=0, keepdims=True), (8, BOTTLE)
    )
    mixed_grad = (out_grad + nn(bottle_grad, down)).astype(bf16)
    normed_grad = jnp.zeros((SEQ, D), f32)
    for chunk in range(chunks):
        cols = slice(chunk * FCHUNK, chunk * FCHUNK + FCHUNK)
        pre_grad = (nt(mixed_grad, wout_ref[cols, :]) * slope_ref[:, cols].astype(f32)).astype(bf16)
        normed_grad = normed_grad + nt(pre_grad, win_ref[:, cols])
    residual = res_ref[...]
    weighted = normed_grad * gain_ref[...]
    inner = jnp.mean(residual * weighted, axis=1, keepdims=True)
    res_grad = out_grad + scale * weighted - residual * (scale * scale * scale * inner)
    res_grad_ref[...] = res_grad
    res_copy = pltpu.make_async_copy(res_grad_ref, res_grad_hbm, sems.at[10])
    res_copy.start()
    dctx = nt(res_grad.astype(bf16), wo_ref[...]).astype(bf16)
    dctx_ref[...] = dctx
    product = dctx.T.astype(f32) * ctx_ref[...].astype(f32)
    delta_ref[0 : D // DH, :] = jnp.sum(product.reshape(D // DH, DH, SEQ), axis=1)
    out_copy.wait()
    res_copy.wait()


def middle(own, lengths, ctx, x, out_grad, frozen, gain, down, up, bias_down, bias_up):
    any_space = pl.BlockSpec(memory_space=pl.ANY)
    vmem = pl.BlockSpec(memory_space=pltpu.VMEM)
    smem = pl.BlockSpec(memory_space=pltpu.SMEM)
    hidden = 2 * frozen[2].shape[1]
    return pl.pallas_call(
        middle_kernel,
        in_specs=[smem, smem] + [any_space] * 9 + [vmem] * 5,
        out_specs=[any_space, any_space, vmem, vmem, vmem],
        out_shape=[
            jax.ShapeDtypeStruct((SEQ, D), f32),
            jax.ShapeDtypeStruct((SEQ, D), f32),
            jax.ShapeDtypeStruct((SEQ, D), bf16),
            jax.ShapeDtypeStruct((16, SEQ), f32),
            jax.ShapeDtypeStruct((2, BOTTLE + 8, D), f32),
        ],
        scratch_shapes=[
            pltpu.VMEM((D, SEQ), bf16),
            pltpu.VMEM((SEQ, D), bf16),
            pltpu.VMEM((SEQ, D), bf16),
            pltpu.VMEM((D, D), bf16),
            pltpu.VMEM((D, hidden), bf16),
            pltpu.VMEM((hidden, D), bf16),
            pltpu.VMEM((SEQ, hidden), bf16),
            pltpu.VMEM((SEQ, D), f32),
            pltpu.VMEM((SEQ, D), f32),
            pltpu.VMEM((SEQ, D), f32),
            pltpu.SemaphoreType.DMA((11,)),
        ],
        compiler_params=pltpu.CompilerParams(vmem_limit_bytes=VMEM_BYTES),
        name="feed_forward_both_ways",
    )(own, lengths, ctx, x, out_grad, *frozen, gain, down, up, bias_down, bias_up)


def backward_kernel(
    own_ref,
    len_ref,
    prob_ref,
    q_ref,
    k_ref,
    v_ref,
    dctx_ref,
    delta_ref,
    gain_ref,
    x_hbm,
    res_grad_hbm,
    wq_own,
    wk_own,
    wv_own,
    wq_other,
    wk_other,
    wv_other,
    out_ref,
    kt_ref,
    dqt_ref,
    dk_ref,
    dv_ref,
    grads_ref,
    weights_ref,
    x_ref,
    res_grad_ref,
    sems,
):
    group, step = pl.program_id(0), pl.program_id(1)
    width = q_ref.shape[1]
    heads = width // DH
    start, ends = row_plan(len_ref, own_ref[0])
    sources = (wq_own, wq_other, wk_own, wk_other, wv_own, wv_other)
    copies = [
        pltpu.make_async_copy(source, weights_ref.at[:, place * width : place * width + width], sems.at[place])
        for place, source in enumerate(sources)
    ]
    copies.append(pltpu.make_async_copy(x_hbm, x_ref, sems.at[6]))
    copies.append(pltpu.make_async_copy(res_grad_hbm, res_grad_ref, sems.at[7]))

    @pl.when((group == 0) & (step == 0))
    def _fetch():
        for copy in copies:
            copy.start()

    @pl.when(step == 0)
    def _prepare():
        kt_ref[...] = k_ref[...].T
        dk_ref[...] = jnp.zeros_like(dk_ref)
        dv_ref[...] = jnp.zeros_like(dv_ref)

    first_row = step * QB
    begin, finish = key_span(ends, first_row, first_row + QB - 1)

    def attend(count):
        rows = count * KB
        key_rows = pl.ds(pl.multiple_of(begin * KB, KB), rows)
        query_rows = pl.ds(pl.multiple_of(first_row, QB), QB)
        for pair in range(heads // 2):
            lanes = slice(pair * PAIR, pair * PAIR + PAIR)
            dk = dv = None
            for half in range(2):
                head = 2 * pair + half
                band = slice(head * DH, head * DH + DH)
                prob = prob_ref[0, head, 0, 0:rows, :]
                grad = one_head(dctx_ref[query_rows, lanes], half)
                queries = one_head(q_ref[query_rows, lanes], half)
                prob_grad = nt(v_ref[key_rows, lanes], grad)
                delta = delta_ref[pl.ds(group * heads + head, 1), query_rows]
                score_grad = (prob.astype(f32) * (prob_grad - delta)).astype(bf16)
                dv_part = nn(prob, grad)
                dk_part = nn(score_grad, queries)
                dv = dv_part if dv is None else dv + dv_part
                dk = dk_part if dk is None else dk + dk_part
                dqt_ref[band, query_rows] = nn(kt_ref[band, key_rows], score_grad).astype(bf16)
            dk_ref[key_rows, lanes] += dk
            dv_ref[key_rows, lanes] += dv

    for count in range(QB // KB, SEQ // KB + 1):
        pl.when(finish - begin == count)(functools.partial(attend, count))

    for side in range(2):

        @pl.when((step == NQ - 1) & (group == side))
        def _collect():
            grads_ref[:, side * width : side * width + width] = dqt_ref[...].T
            grads_ref[:, (2 + side) * width : (3 + side) * width] = dk_ref[...].astype(bf16)
            grads_ref[:, (4 + side) * width : (5 + side) * width] = dv_ref[...].astype(bf16)

    @pl.when((step == NQ - 1) & (group == 1))
    def _finish():
        for copy in copies:
            copy.wait()
        normed_grad = nt(grads_ref[...], weights_ref[...])
        inputs = x_ref[...].astype(f32)
        scale = lax.rsqrt(jnp.mean(inputs * inputs, axis=1, keepdims=True) + eps_norm)
        weighted = normed_grad * gain_ref[...]
        inner = jnp.mean(inputs * weighted, axis=1, keepdims=True)
        grad_in = res_grad_ref[...] + scale * weighted - inputs * (scale * scale * scale * inner)
        out_ref[...] = to_given(grad_in, start)


def attention_backward(own, lengths, prob, q, k, v, dctx, delta, gain, x, res_grad, weights):
    width = weights[0].shape[1]
    heads = width // DH

    def side():
        return pl.BlockSpec((SEQ, width), lambda g, i, *_: (0, g))

    def whole(*shape):
        return pl.BlockSpec(shape, lambda g, i, *_: (0,) * len(shape))

    return pl.pallas_call(
        backward_kernel,
        grid_spec=pltpu.PrefetchScalarGridSpec(
            num_scalar_prefetch=2,
            grid=(2, NQ),
            in_specs=[
                pl.BlockSpec((1, heads, 1, SEQ, QB), lambda g, i, *_: (g, 0, i, 0, 0)),
                side(),
                side(),
                side(),
                side(),
                whole(*delta.shape),
                whole(1, D),
            ]
            + [pl.BlockSpec(memory_space=pl.ANY)] * 8,
            out_specs=[whole(SEQ, D)],
            scratch_shapes=[
                pltpu.VMEM((width, SEQ), bf16),
                pltpu.VMEM((width, SEQ), bf16),
                pltpu.VMEM((SEQ, width), f32),
                pltpu.VMEM((SEQ, width), f32),
                pltpu.VMEM((SEQ, 6 * width), bf16),
                pltpu.VMEM((D, 6 * width), bf16),
                pltpu.VMEM((SEQ, D), bf16),
                pltpu.VMEM((SEQ, D), f32),
                pltpu.SemaphoreType.DMA((8,)),
            ],
        ),
        out_shape=[jax.ShapeDtypeStruct((SEQ, D), f32)],
        compiler_params=pltpu.CompilerParams(vmem_limit_bytes=VMEM_BYTES),
        name="attention_backward",
    )(own, lengths, prob, q, k, v, dctx, delta, gain, x, res_grad, *weights)[0]


def unpack(flat):
    widths = (KRON * KRON * KRON, D, BOTTLE, BOTTLE, D, BOTTLE, D)
    pieces = []
    first_item = 0
    for width in widths:
        pieces.append(flat[first_item : first_item + width])
        first_item = first_item + width
    kron_a = pieces[0].reshape(KRON, KRON, KRON)
    down_left = pieces[1].reshape(KRON, D // KRON)
    down_right = pieces[2].reshape(KRON, BOTTLE // KRON)
    up_left = pieces[3].reshape(KRON, BOTTLE // KRON)
    up_right = pieces[4].reshape(KRON, D // KRON)
    return (kron_a, down_left, down_right, up_left, up_right, pieces[5], pieces[6])


def adapter_matrices(flat):
    kron_a, down_left, down_right, up_left, up_right, bias_down, bias_up = unpack(flat)
    down_factor = (KRON * D) ** (-0.5)
    up_factor = BOTTLE ** (-0.5)
    down_mat = jnp.einsum(
        "nab,np,nq->bqap", kron_a, down_left, down_right * down_factor, precision=highest
    ).reshape(BOTTLE, D)
    up_mat = jnp.einsum(
        "nba,nq,np->bqap", kron_a, up_left, up_right * up_factor, precision=highest
    ).reshape(BOTTLE, D)
    return (down_mat, up_mat, bias_down, bias_up)


def sum_everywhere(value):
    for axis in ("head", "dp"):
        size = lax.axis_size(axis)
        step = 1
        while step < size:
            value = value + lax.ppermute(value, axis, [(place, place ^ step) for place in range(size)])
            step = 2 * step
    return value


def on_device(
    hidden_in,
    lengths,
    buckets,
    gain_attn,
    gain_ffn,
    w_query,
    w_key,
    w_value,
    w_attn_out,
    w_in,
    w_ffn_out,
    rel_bias,
    out_grad,
    adapter_weights,
    first_moment,
    second_moment,
    ema_weights,
):
    swap = [(0, 1), (1, 0)]
    own = lax.axis_index("head").astype(jnp.int32).reshape(1)

    def other(value):
        return lax.ppermute(value, "head", swap)

    own_qkv = (w_query, w_key, w_value)
    other_qkv = tuple(other(weight) for weight in own_qkv)
    other_bias = other(rel_bias)
    other_rest = tuple(other(weight) for weight in (w_attn_out, w_in, w_ffn_out))
    last = REACH + 127 + SEQ - 1
    codes = buckets[max(last - CODES + 1, 0) : last + 1][::-1]
    codes = jnp.pad(codes, (0, CODES - codes.shape[0])).reshape(1, CODES)
    gain_a, gain_f = gain_attn.reshape(1, D), gain_ffn.reshape(1, D)
    mats, adapter_pull = jax.vjp(adapter_matrices, adapter_weights)
    down_mat, up_mat, bias_down, bias_up = mats

    *kept, packed = attention_forward(
        True, own, lengths, hidden_in, gain_a, own_qkv, codes, rel_bias
    )
    prob, q, k, v, ctx = attention_forward(
        False, own, lengths, packed, gain_a, other_qkv, codes, other_bias, kept
    )
    frozen = tuple(piece for pair in zip((w_attn_out, w_in, w_ffn_out), other_rest) for piece in pair)
    layer_out, res_grad, dctx, delta, adapter = middle(
        own,
        lengths,
        ctx,
        packed,
        out_grad,
        frozen,
        gain_f,
        down_mat.astype(bf16),
        up_mat.astype(bf16),
        bias_down.reshape(1, BOTTLE),
        bias_up.reshape(1, D),
    )
    local_grad = adapter_pull(
        (adapter[1, :BOTTLE], adapter[0, :BOTTLE], adapter[1, BOTTLE, :BOTTLE], adapter[0, BOTTLE])
    )[0]
    total_grad = sum_everywhere(local_grad)
    grad_in = attention_backward(
        own, lengths, prob, q, k, v, dctx, delta, gain_a, packed, res_grad, own_qkv + other_qkv
    )
    new_first = beta_one * first_moment + (1.0 - beta_one) * total_grad
    new_second = beta_two * second_moment + (1.0 - beta_two) * total_grad * total_grad
    first_hat = new_first / (1.0 - beta_one**STEP)
    second_hat = new_second / (1.0 - beta_two**STEP)
    new_weights = adapter_weights - learn_rate * (
        first_hat / (jnp.sqrt(second_hat) + adam_eps) + weight_decay * adapter_weights
    )
    new_ema = ema_decay * ema_weights + (1.0 - ema_decay) * new_weights
    return (layer_out, grad_in, new_weights, new_first, new_second, new_ema)


def solution(mesh):
    placed = (
        P("dp", None),
        P("dp", None),
        P(),
        P(),
        P(),
        P(None, "head"),
        P(None, "head"),
        P(None, "head"),
        P("head", None),
        P(None, "head"),
        P("head", None),
        P(None, "head"),
        P(("dp", "head"), None),
        P(),
        P(),
        P(),
        P(),
    )
    return jax.shard_map(
        on_device,
        mesh=mesh,
        in_specs=placed,
        out_specs=(P(("dp", "head"), None), P(("dp", "head"), None), P(), P(), P(), P()),
        check_vma=False,
    )
```

```python
import functools

import jax
import jax.numpy as jnp
from jax import lax
from jax.experimental import pallas as pl
from jax.experimental.pallas import tpu as pltpu
from jax.sharding import PartitionSpec as P

D = 768
DH = 64
KRON = 4
BOTTLE = 48
SEQ = 1024
MOST = 512
STEP = 10
QB = 256
KB = 256
NQ = SEQ // QB
PAIR = 2 * DH
FCHUNK = 512
REACH = QB + MOST - 128
SPREAD = REACH + MOST + QB
CODES = SPREAD + 128
VMEM_BYTES = 127 * 2**19

eps_norm = 1e-06
beta_one = 0.9
beta_two = 0.999
adam_eps = 1e-08
learn_rate = 0.6
weight_decay = 0.01
ema_decay = 0.9
masked_score = -1e30
log2_e = 1.4426950408889634
highest = lax.Precision.HIGHEST
f32 = jnp.float32
bf16 = jnp.bfloat16


def nn(left, right):
    return lax.dot_general(left, right, (((1,), (0,)), ((), ())), preferred_element_type=f32)


def nt(left, right):
    return lax.dot_general(left, right, (((1,), (1,)), ((), ())), preferred_element_type=f32)


def tn(left, right):
    return lax.dot_general(left, right, (((0,), (0,)), ((), ())), preferred_element_type=f32)


def row_plan(len_ref, own):
    docs = len_ref.shape[1]
    sizes = [len_ref[own, doc] for doc in range(docs)]
    longest, chosen = sizes[0], jnp.int32(0)
    for doc in range(1, docs):
        longer = sizes[doc] > longest
        chosen = jnp.where(longer, doc, chosen)
        longest = jnp.maximum(longest, sizes[doc])
    start = jnp.int32(0)
    for doc in range(docs):
        start = start + jnp.where(doc < chosen, sizes[doc], 0)
    ends, total = [], jnp.int32(0)
    for doc in range(docs):
        total = total + len_ref[own, lax.rem(chosen + doc, docs)]
        ends.append(total)
    return start, ends


def key_span(ends, first_row, last_row):
    begin, finish = jnp.int32(0), jnp.int32(SEQ)
    for end in ends:
        begin = jnp.where(end <= first_row, end, begin)
    for end in reversed(ends):
        finish = jnp.where(end > last_row, end, finish)
    return lax.div(begin, KB), lax.div(finish + (KB - 1), KB)


def rotate_rows(source_ref, target_ref, shift):
    groups = SEQ // 8
    fine, coarse = shift & 7, shift >> 3
    back = (8 - fine) & 7
    keep = lax.broadcasted_iota(jnp.int32, (8, target_ref.shape[1]), 0) < 8 - fine

    def turned(group):
        rows = source_ref[pl.ds(pl.multiple_of((group & (groups - 1)) * 8, 16), 16), :].astype(f32)
        return pltpu.roll(rows[0:8], back, 0), pltpu.roll(rows[8:16], back, 0)

    def some(part, carry):
        first, second = carry
        for pair in range(4):
            group = part * 8 + pair * 2
            third, fourth = turned(group + 2)
            for place, left, right in ((0, first, second), (1, second, third)):
                to = ((group + place - coarse) & (groups - 1)) * 8
                target_ref[pl.ds(pl.multiple_of(to, 8), 8), :] = jnp.where(keep, left, right)
            first, second = third, fourth
        return first, second

    lax.fori_loop(0, groups // 8, some, turned(jnp.int32(0)))


def one_head(pair, half):
    lane = lax.broadcasted_iota(jnp.int32, pair.shape, 1)
    keep = lane < DH if half == 0 else lane >= DH
    return jnp.where(keep, pair, jnp.zeros_like(pair))


def flip_lanes(value):
    tiles = value.shape[1] // 128
    row = lax.broadcasted_iota(jnp.int32, (128, 128), 0)
    lane = lax.broadcasted_iota(jnp.int32, (128, 128), 1)
    stacked = jnp.concatenate([value[:, tile * 128 : tile * 128 + 128] for tile in range(tiles)], axis=0)
    flipped = exact(stacked, (row + lane == 127).astype(f32))
    return jnp.concatenate([flipped[tile * 8 : tile * 8 + 8, :] for tile in reversed(range(tiles))], axis=1)


def exact(left, right):
    return lax.dot_general(
        left, right, (((1,), (0,)), ((), ())), precision=highest, preferred_element_type=f32
    )


def bias_bands(buckets_ref, table_ref, bias_ref):
    heads = table_ref.shape[0]
    top = REACH + 128 + SEQ - 1
    codes = buckets_ref[...].reshape(1, 2 * SEQ - 1)[:, top - CODES + 1 : top + 1]
    bucket = lax.broadcasted_iota(jnp.int32, (table_ref.shape[1], CODES), 0)
    per_head = exact(table_ref[...] * log2_e, (bucket == codes).astype(f32))
    per_head = flip_lanes(jnp.concatenate([per_head, jnp.zeros((8 - heads, CODES), f32)], axis=0))
    for head in range(heads):
        spread = jnp.broadcast_to(per_head[head : head + 1, :], (128, CODES))
        spread = pltpu.roll(spread, CODES - 128, 1, stride=1, stride_axis=0)
        bias_ref[head] = spread[:, :SPREAD]


def attention_kernel(leading, *refs):
    own_ref, len_ref, x_hbm, wq_hbm, wk_hbm, wv_hbm = refs[:6]
    gain_ref, buckets_ref, table_ref = refs[6:9]
    if leading:
        prob_hbm, q_hbm, k_hbm, v_hbm, ctx_hbm, shrink_hbm, packed_hbm = refs[9:16]
    else:
        prob_hbm, q_hbm, k_hbm, v_hbm, ctx_hbm, shrink_hbm = refs[15:21]
    (
        x_ref,
        w_ref,
        q_ref,
        k_ref,
        v_ref,
        vt_ref,
        ctx_ref,
        shrink_ref,
        bias_ref,
        dk_ref,
        dq_ref,
        prob_ref,
        turned_ref,
        prob_sems,
        sems,
    ) = refs[-15:]
    heads = table_ref.shape[0]
    width = heads * DH
    group = 0 if leading else 1
    columns = slice(group * width, group * width + width)
    if leading:
        x_hbm = x_hbm.at[pl.ds(pl.multiple_of(own_ref[0] * SEQ, SEQ), SEQ), :]
    loads = [pltpu.make_async_copy(x_hbm, x_ref, sems.at[0])]
    for place, source in enumerate((wq_hbm, wk_hbm, wv_hbm)):
        target = w_ref.at[:, place * width : place * width + width]
        loads.append(pltpu.make_async_copy(source, target, sems.at[1 + place]))
    for load in loads:
        load.start()
    start, ends = row_plan(len_ref, own_ref[0])
    row = lax.broadcasted_iota(jnp.int32, dk_ref.shape, 0)
    dk_ref[...] = sum((row >= end).astype(jnp.int32) for end in ends)
    lane = lax.broadcasted_iota(jnp.int32, dq_ref.shape, 1)
    dq_ref[...] = sum((lane >= end).astype(jnp.int32) for end in ends)
    bias_bands(buckets_ref, table_ref, bias_ref)
    stores = []

    def store(source, target, place):
        copy = pltpu.make_async_copy(source, target, sems.at[place])
        copy.start()
        stores.append(copy)

    loads[0].wait()
    if not leading:
        inputs = x_ref[...].astype(f32)
    if leading:
        rotate_rows(x_ref, turned_ref, start)
        inputs = turned_ref[...]
        x_ref[...] = inputs.astype(bf16)
        store(x_ref, packed_hbm, 4)
    scale = lax.rsqrt(jnp.mean(inputs * inputs, axis=1, keepdims=True) + eps_norm)
    normed = (inputs * scale * gain_ref[...].reshape(1, D)).astype(bf16)
    for load in loads[1:]:
        load.wait()
    queries_all = nn(normed, w_ref[:, 0:width])
    q_ref[...] = (queries_all * log2_e).astype(bf16)
    k_ref[...] = nn(normed, w_ref[:, width : 2 * width]).astype(bf16)
    values = nn(normed, w_ref[:, 2 * width : 3 * width]).astype(bf16)
    v_ref[...] = values
    vt_ref[...] = values.T
    store(q_ref, q_hbm.at[:, columns], 5)
    store(k_ref, k_hbm.at[:, columns], 6)
    store(v_ref, v_hbm.at[:, columns], 7)

    def prob_copy(step, count):
        slot, rows = lax.rem(step, 2), count * KB
        return pltpu.make_async_copy(
            prob_ref.at[slot, :, 0:rows, :], prob_hbm.at[group, :, step, 0:rows, :], prob_sems.at[slot]
        )

    def with_span(step, action):
        begin, finish = key_span(ends, step * QB, step * QB + QB - 1)
        for count in range(QB // KB, SEQ // KB + 1):
            pl.when(finish - begin == count)(functools.partial(action, step, begin, count))

    def drain(step, begin, count):
        prob_copy(step, count).wait()

    def attend(step, begin, count):
        rows = count * KB
        slot = lax.rem(step, 2)
        first_row, first_key = step * QB, pl.multiple_of(begin * KB, KB)
        key_rows = pl.ds(first_key, rows)
        query_rows = pl.ds(pl.multiple_of(first_row, QB), QB)
        doc_key = jnp.concatenate([dk_ref[key_rows, :]] * (QB // 128), axis=1)
        same = doc_key == dq_ref[0:1, query_rows]
        scores = []
        for head in range(heads):
            lanes = slice(head // 2 * PAIR, head // 2 * PAIR + PAIR)
            scores.append(nt(k_ref[key_rows, lanes], one_head(q_ref[query_rows, lanes], head % 2)))
        totals = []
        for head in range(heads):
            bias = jnp.concatenate(
                [
                    bias_ref[
                        head,
                        :,
                        pl.ds(pl.multiple_of(first_row - first_key + (REACH - part * 128), 128), QB),
                    ]
                    for part in range(rows // 128)
                ],
                axis=0,
            )
            score = jnp.where(same, scores[head] + bias, masked_score)
            expo = jnp.exp2(score - jnp.max(score, axis=0, keepdims=True))
            totals.append(1.0 / jnp.sum(expo, axis=0, keepdims=True))
            prob_ref[slot, head, 0:rows, :] = expo.astype(bf16)
        prob_copy(step, count).start()
        for head in range(heads):
            band = slice(head * DH, head * DH + DH)
            context = nn(vt_ref[band, key_rows], prob_ref[slot, head, 0:rows, :])
            ctx_ref[band, query_rows] = (context * totals[head]).astype(bf16)
            shrink_ref[head : head + 1, query_rows] = totals[head]

    def one_block(step, carry):
        @pl.when(step >= 2)
        def _drain():
            with_span(step - 2, drain)

        with_span(step, attend)
        return carry

    lax.fori_loop(0, NQ, one_block, 0)
    store(ctx_ref, ctx_hbm.at[columns, :], 8)
    store(shrink_ref, shrink_hbm.at[group], 9)
    with_span(NQ - 2, drain)
    with_span(NQ - 1, drain)
    for copy in stores:
        copy.wait()


def attention_forward(leading, own, lengths, x, gain, weights, buckets, table, kept=()):
    heads = table.shape[0]
    width = heads * DH
    any_space = pl.BlockSpec(memory_space=pl.ANY)
    vmem = pl.BlockSpec(memory_space=pltpu.VMEM)
    smem = pl.BlockSpec(memory_space=pltpu.SMEM)
    out_shape = [
        jax.ShapeDtypeStruct((2, heads, NQ, SEQ, QB), bf16),
        jax.ShapeDtypeStruct((SEQ, 2 * width), bf16),
        jax.ShapeDtypeStruct((SEQ, 2 * width), bf16),
        jax.ShapeDtypeStruct((SEQ, 2 * width), bf16),
        jax.ShapeDtypeStruct((2 * width, SEQ), bf16),
        jax.ShapeDtypeStruct((2, 8, SEQ), f32),
    ]
    if leading:
        out_shape.append(jax.ShapeDtypeStruct((SEQ, D), bf16))
    return pl.pallas_call(
        functools.partial(attention_kernel, leading),
        in_specs=[smem, smem] + [any_space] * 4 + [vmem] * 3 + [any_space] * len(kept),
        out_specs=[any_space] * len(out_shape),
        out_shape=out_shape,
        scratch_shapes=[
            pltpu.VMEM((SEQ, D), bf16),
            pltpu.VMEM((D, 3 * width), bf16),
            pltpu.VMEM((SEQ, width), bf16),
            pltpu.VMEM((SEQ, width), bf16),
            pltpu.VMEM((SEQ, width), bf16),
            pltpu.VMEM((width, SEQ), bf16),
            pltpu.VMEM((width, SEQ), bf16),
            pltpu.VMEM((8, SEQ), f32),
            pltpu.VMEM((heads, 128, SPREAD), f32),
            pltpu.VMEM((SEQ, 128), jnp.int32),
            pltpu.VMEM((8, SEQ), jnp.int32),
            pltpu.VMEM((2, heads, SEQ, QB), bf16),
            pltpu.VMEM((SEQ if leading else 8, D), f32),
            pltpu.SemaphoreType.DMA((2,)),
            pltpu.SemaphoreType.DMA((10,)),
        ],
        input_output_aliases={9 + place: place for place in range(len(kept))},
        compiler_params=pltpu.CompilerParams(vmem_limit_bytes=VMEM_BYTES),
        cost_estimate=pl.CostEstimate(flops=15 * 10**9, bytes_accessed=16 * 10**6, transcendentals=4 * 10**6),
        name="attention_forward_own" if leading else "attention_forward_other",
    )(own, lengths, x, *weights, gain, buckets, table, *kept)


root_two_over_pi = 0.7978845608028654
cubic = 0.044715


def gelu_both(value):
    square = value * value
    slow = jnp.tanh(value * (root_two_over_pi + (root_two_over_pi * cubic) * square))
    half = 0.5 * value
    act = half + half * slow
    slope = (0.5 + 0.5 * slow) + half * (1.0 - slow * slow) * (
        root_two_over_pi + (3.0 * root_two_over_pi * cubic) * square
    )
    return act, slope


def block_of(index, width, blocks):
    return sum((index >= width * place).astype(jnp.int32) for place in range(1, blocks))


class Kronecker:
    def __init__(self, core, small, large, factor, swapped):
        terms, rows = KRON, KRON * KRON
        sub, leaf = BOTTLE // KRON, D // KRON
        self.factor = factor
        row = lax.broadcasted_iota(jnp.int32, (rows, rows * KRON), 0)
        item = lax.broadcasted_iota(jnp.int32, (rows, rows * KRON), 1)
        item_of = lax.broadcasted_iota(jnp.int32, (rows * KRON, BOTTLE), 0)
        lane_block = block_of(lax.broadcasted_iota(jnp.int32, (rows * KRON, BOTTLE), 1), sub, KRON)
        if swapped:
            self.holds = ((item >> 4) == (row >> 2)) & ((item & 3) == (row & 3))
            pick = ((item_of >> 2) & 3) == lane_block
        else:
            self.holds = (item >> 2) == row
            pick = (item_of & 3) == lane_block
        self.pick = pick.astype(f32)
        self.core = exact(jnp.where(self.holds, jnp.broadcast_to(core, self.holds.shape), 0.0), self.pick)
        self.small = jnp.concatenate(
            [
                jnp.broadcast_to(
                    jnp.concatenate([small[:, n * sub : n * sub + sub]] * KRON, axis=1), (KRON, BOTTLE)
                )
                for n in range(terms)
            ],
            axis=0,
        )
        large = jnp.concatenate(
            [
                jnp.broadcast_to(
                    jnp.concatenate([large[:, n * leaf : n * leaf + leaf]] * KRON, axis=1), (KRON, D)
                )
                for n in range(terms)
            ],
            axis=0,
        )
        row = lax.broadcasted_iota(jnp.int32, (rows, D), 0)
        lane = lax.broadcasted_iota(jnp.int32, (rows, D), 1)
        self.diagonal = (row & 3) == block_of(lane, leaf, KRON)
        self.large = jnp.where(self.diagonal, large, 0.0)
        self.mix = self.core * self.small

    def matrix(self):
        return exact(self.mix.T, self.large) * self.factor

    def gradient(self, grad):
        sub, leaf = BOTTLE // KRON, D // KRON
        inner = self.factor * lax.dot_general(
            self.large, grad, (((1,), (1,)), ((), ())), precision=highest, preferred_element_type=f32
        )
        core = lax.dot_general(
            self.small * inner, self.pick, (((1,), (1,)), ((), ())), precision=highest, preferred_element_type=f32
        )
        core = jnp.sum(jnp.where(self.holds, core, 0.0), axis=0, keepdims=True)
        by_term = self.core * inner
        outer = self.factor * jnp.where(self.diagonal, exact(self.mix, grad), 0.0)
        small, large = [], []
        for n in range(KRON):
            row = jnp.sum(by_term[n * KRON : n * KRON + KRON, :], axis=0, keepdims=True)
            small.append(sum(row[:, b * sub : b * sub + sub] for b in range(KRON)))
            row = jnp.sum(outer[n * KRON : n * KRON + KRON, :], axis=0, keepdims=True)
            large.append(sum(row[:, a * leaf : a * leaf + leaf] for a in range(KRON)))
        return core, jnp.concatenate(small, axis=1), jnp.concatenate(large, axis=1)


def both_adapters(flat):
    widths = (KRON * KRON * KRON, D, BOTTLE, BOTTLE, D, BOTTLE, D)
    pieces, place = [], 0
    for width in widths:
        pieces.append(flat[:, place : place + width])
        place = place + width
    core, down_left, down_right, up_left, up_right, bias_down, bias_up = pieces
    down = Kronecker(core, down_right, down_left, (KRON * D) ** (-0.5), False)
    up = Kronecker(core, up_left, up_right, BOTTLE ** (-0.5), True)
    return down, up, bias_down, bias_up


def feed_forward_kernel(
    own_ref,
    len_ref,
    prob_hbm,
    q_hbm,
    k_hbm,
    v_hbm,
    ctx_hbm,
    shrink_hbm,
    x_hbm,
    grad_hbm,
    wo_own,
    wo_other,
    win_own,
    win_other,
    wout_own,
    wout_other,
    wq_own,
    wk_own,
    wv_own,
    wq_other,
    wk_other,
    wv_other,
    gain_attn_ref,
    gain_ffn_ref,
    flat_ref,
    out_hbm,
    grad_in_hbm,
    flat_grad_ref,
    ctx_ref,
    x_ref,
    grad_ref,
    wo_ref,
    win_ref,
    wout_ref,
    slope_ref,
    res_ref,
    res_grad_ref,
    delta_ref,
    shrink_ref,
    dqt_ref,
    sums_ref,
    prob_ref,
    prob_sems,
    sems,
):
    start, ends = row_plan(len_ref, own_ref[0])
    half = wo_own.shape[0]
    hidden = win_own.shape[1]
    heads = half // DH
    chunks = 2 * hidden // FCHUNK
    side = hidden // FCHUNK

    def load(source, target, place):
        return pltpu.make_async_copy(source, target, sems.at[place])

    first = [
        load(ctx_hbm, ctx_ref, 0),
        load(wo_own, wo_ref.at[0:half, :], 1),
        load(wo_other, wo_ref.at[half : 2 * half, :], 2),
        load(x_hbm, x_ref, 3),
    ]
    win_loads, wout_loads = [], []
    for chunk in range(chunks):
        source = win_own if chunk < side else win_other
        place = chunk % side * FCHUNK
        cols = slice(chunk * FCHUNK, chunk * FCHUNK + FCHUNK)
        win_loads.append(load(source.at[:, place : place + FCHUNK], win_ref.at[:, cols], 4 + chunk))
        source = wout_own if chunk < side else wout_other
        wout_loads.append(load(source.at[place : place + FCHUNK, :], wout_ref.at[cols, :], 4 + chunks + chunk))
    base = 4 + 2 * chunks
    grad_load = load(grad_hbm, grad_ref, base)
    v_ref, k_ref, q_ref = (wout_ref.at[place * SEQ : place * SEQ + SEQ, :] for place in range(3))
    late = [
        load(v_hbm, v_ref, base + 1),
        load(k_hbm, k_ref, base + 3),
        load(q_hbm, q_ref, base + 2),
    ]
    shrink_load = load(shrink_hbm, shrink_ref, base + 4)
    out_copy = load(res_grad_ref, out_hbm, base + 5)
    grad_in_copy = load(res_ref, grad_in_hbm, base + 6)
    qkv_loads = [
        load(source, win_ref.at[:, place * half : place * half + half], 4 + place)
        for place, source in enumerate((wq_own, wq_other, wk_own, wk_other, wv_own, wv_other))
    ]
    for copy in first:
        copy.start()
    for chunk in range(chunks):
        win_loads[chunk].start()
        wout_loads[chunk].start()
    grad_load.start()
    shrink_load.start()

    def prob_copy(it, count):
        slot, rows = lax.rem(it, 2), count * KB
        return pltpu.make_async_copy(
            prob_hbm.at[lax.div(it, NQ), :, lax.rem(it, NQ), 0:rows, :],
            prob_ref.at[slot, :, 0:rows, :],
            prob_sems.at[slot],
        )

    def with_span(it, action):
        first_row = lax.rem(it, NQ) * QB
        begin, finish = key_span(ends, first_row, first_row + QB - 1)
        for count in range(QB // KB, SEQ // KB + 1):
            pl.when(finish - begin == count)(functools.partial(action, it, begin, count))

    def fetch(it, begin, count):
        prob_copy(it, count).start()

    with_span(jnp.int32(0), fetch)
    flat = flat_ref[...].reshape(1, flat_ref.shape[0])
    down_maker, up_maker, bias_down, bias_up = both_adapters(flat)
    down, up = down_maker.matrix().astype(bf16), up_maker.matrix().astype(bf16)
    gain = gain_ffn_ref[...].reshape(1, D)
    for copy in first:
        copy.wait()
    residual = x_ref[...].astype(f32) + tn(ctx_ref[...], wo_ref[...])
    res_ref[...] = residual
    scale = lax.rsqrt(jnp.mean(residual * residual, axis=1, keepdims=True) + eps_norm)
    low = (residual * scale * gain).astype(bf16)

    def cols_of(chunk):
        return slice(chunk * FCHUNK, chunk * FCHUNK + FCHUNK)

    previous = None
    win_loads[0].wait()
    pre = nn(low, win_ref[:, cols_of(0)])
    for chunk in range(chunks):
        if chunk + 1 < chunks:
            win_loads[chunk + 1].wait()
            ahead = nn(low, win_ref[:, cols_of(chunk + 1)])
        if previous is not None:
            wout_loads[chunk - 1].wait()
            part = nn(previous, wout_ref[cols_of(chunk - 1), :])
            if chunk == 1:
                sums_ref[...] = part
            else:
                sums_ref[...] += part
        act, slope = gelu_both(pre)
        slope_ref[:, cols_of(chunk)] = slope.astype(bf16)
        previous, pre = act.astype(bf16), ahead
    wout_loads[chunks - 1].wait()
    mixed = sums_ref[...] + nn(previous, wout_ref[cols_of(chunks - 1), :])
    grad_load.wait()
    rotate_rows(grad_ref, res_grad_ref, start)
    out_grad_low = res_grad_ref[...].astype(bf16)
    grad_ref[...] = out_grad_low
    mixed_low = mixed.astype(bf16)
    bottle, bottle_slope = gelu_both(nt(mixed_low, down) + bias_down)
    bottle_low = bottle.astype(bf16)
    sums_ref[...] = res_ref[...] + mixed + nn(bottle_low, up) + bias_up
    rotate_rows(sums_ref, res_grad_ref, SEQ - start)
    out_copy.start()
    bottle_grad = (nt(out_grad_low, up) * bottle_slope).astype(bf16)
    mixed_grad = (out_grad_low.astype(f32) + nn(bottle_grad, down)).astype(bf16)
    up_grad = tn(bottle_low, out_grad_low)
    down_grad = tn(bottle_grad, mixed_low)
    core_down, right_down, left_down = down_maker.gradient(down_grad)
    core_up, left_up, right_up = up_maker.gradient(up_grad)
    flat_grad = jnp.concatenate(
        [
            core_down + core_up,
            left_down,
            right_down,
            left_up,
            right_up,
            jnp.sum(bottle_grad.astype(f32), axis=0, keepdims=True),
            jnp.sum(out_grad_low.astype(f32), axis=0, keepdims=True),
        ],
        axis=1,
    )
    flat_grad_ref[...] = flat_grad.reshape(flat_grad_ref.shape[0])
    pre = nt(mixed_grad, wout_ref[cols_of(0), :])
    for chunk in range(chunks):
        if chunk + 1 < chunks:
            ahead = nt(mixed_grad, wout_ref[cols_of(chunk + 1), :])
        pre_grad = (pre * slope_ref[:, cols_of(chunk)].astype(f32)).astype(bf16)
        part = nt(pre_grad, win_ref[:, cols_of(chunk)])
        if chunk == 0:
            sums_ref[...] = part
        else:
            sums_ref[...] += part
        pre = ahead
    for copy in late + qkv_loads:
        copy.start()
    residual = res_ref[...]
    weighted = sums_ref[...] * gain
    inner = jnp.mean(residual * weighted, axis=1, keepdims=True)
    res_grad = grad_ref[...].astype(f32) + scale * weighted - residual * (scale * scale * scale * inner)
    out_copy.wait()
    res_grad_ref[...] = res_grad
    shrink_load.wait()
    shrink = jnp.concatenate([shrink_ref[0, 0:heads, :], shrink_ref[1, 0:heads, :]], axis=0)
    shrink_top = shrink.astype(bf16)
    shrink_rest = (shrink - shrink_top.astype(f32)).astype(bf16)
    head_row = lax.broadcasted_iota(jnp.int32, (2 * heads, D), 0)
    head_lane = lax.broadcasted_iota(jnp.int32, (2 * heads, D), 1) >> 6
    spread = (head_row == head_lane).astype(bf16)
    shrink_wide = tn(shrink_top, spread) + tn(shrink_rest, spread)
    dctx = (nt(res_grad.astype(bf16), wo_ref[...]) * shrink_wide).astype(bf16)
    grad_ref[...] = dctx
    product = dctx.T.astype(f32) * ctx_ref[...].astype(f32)
    delta_ref[0 : 2 * heads, :] = jnp.sum(product.reshape(2 * heads, DH, SEQ), axis=1)
    for copy in late:
        copy.wait()
    kt_ref, dctx_ref = ctx_ref, grad_ref
    kt_ref[...] = k_ref[...].T

    def attend(it, begin, count):
        rows = count * KB
        slot, group = lax.rem(it, 2), lax.div(it, NQ)
        key_rows = pl.ds(pl.multiple_of(begin * KB, KB), rows)
        query_rows = pl.ds(pl.multiple_of(lax.rem(it, NQ) * QB, QB), QB)
        prob_copy(it, count).wait()

        def lanes(pair):
            return pl.ds(pl.multiple_of(group * half + pair * PAIR, PAIR), PAIR)

        together = heads if count <= 2 else 2
        for lead in range(0, heads, together):
            members = range(lead, lead + together)
            grads, prob_grads, score_grads = {}, {}, {}
            for head in members:
                grads[head] = one_head(dctx_ref[query_rows, lanes(head // 2)], head % 2)
                prob_grads[head] = nt(v_ref[key_rows, lanes(head // 2)], grads[head])
            for head in members:
                delta = delta_ref[pl.ds(group * heads + head, 1), query_rows]
                prob = prob_ref[slot, head, 0:rows, :].astype(f32)
                score_grads[head] = (prob * (prob_grads[head] - delta)).astype(bf16)
            for pair in range(lead // 2, (lead + together) // 2):
                dk = dv = None
                for head in (2 * pair, 2 * pair + 1):
                    band = pl.ds(pl.multiple_of(group * half + head * DH, DH), DH)
                    queries = one_head(q_ref[query_rows, lanes(pair)], head % 2)
                    dv_part = nn(prob_ref[slot, head, 0:rows, :], grads[head])
                    dk_part = nn(score_grads[head], queries)
                    dv = dv_part if dv is None else dv + dv_part
                    dk = dk_part if dk is None else dk + dk_part
                    dqt_ref[band, query_rows] = nn(kt_ref[band, key_rows], score_grads[head]).astype(bf16)
                sums_ref[key_rows, pair * PAIR : pair * PAIR + PAIR] += dk
                sums_ref[key_rows, half + pair * PAIR : half + pair * PAIR + PAIR] += dv

    def one_block(it, carry):
        @pl.when(it + 1 < 2 * NQ)
        def _ahead():
            with_span(it + 1, fetch)

        @pl.when(lax.rem(it, NQ) == 0)
        def _clear():
            sums_ref[...] = jnp.zeros_like(sums_ref)

        with_span(it, attend)
        for group in range(2):

            @pl.when(it == group * NQ + NQ - 1)
            def _collect():
                place = (2 + group) * half
                slope_ref[:, place : place + half] = (sums_ref[:, 0:half] * (1.0 / log2_e)).astype(bf16)
                place = (4 + group) * half
                slope_ref[:, place : place + half] = sums_ref[:, half : 2 * half].astype(bf16)

        return carry

    lax.fori_loop(0, 2 * NQ, one_block, 0)
    slope_ref[:, 0 : 2 * half] = dqt_ref[...].T
    for copy in qkv_loads:
        copy.wait()
    normed_grad = nt(slope_ref[:, 0 : 6 * half], win_ref[:, 0 : 6 * half])
    inputs = x_ref[...].astype(f32)
    scale = lax.rsqrt(jnp.mean(inputs * inputs, axis=1, keepdims=True) + eps_norm)
    weighted = normed_grad * gain_attn_ref[...].reshape(1, D)
    inner = jnp.mean(inputs * weighted, axis=1, keepdims=True)
    sums_ref[...] = res_grad_ref[...] + scale * weighted - inputs * (scale * scale * scale * inner)
    rotate_rows(sums_ref, res_ref, SEQ - start)
    grad_in_copy.start()
    grad_in_copy.wait()


def feed_forward_and_back(own, lengths, kept, x, out_grad, frozen, weights, gain_attn, gain_ffn, flat):
    any_space = pl.BlockSpec(memory_space=pl.ANY)
    vmem = pl.BlockSpec(memory_space=pltpu.VMEM)
    smem = pl.BlockSpec(memory_space=pltpu.SMEM)
    hidden = 2 * frozen[2].shape[1]
    heads = kept[0].shape[1]
    half = heads * DH
    return pl.pallas_call(
        feed_forward_kernel,
        in_specs=[smem, smem] + [any_space] * 20 + [vmem] * 3,
        out_specs=[any_space, any_space, vmem],
        out_shape=[
            jax.ShapeDtypeStruct((SEQ, D), f32),
            jax.ShapeDtypeStruct((SEQ, D), f32),
            jax.ShapeDtypeStruct(flat.shape, f32),
        ],
        scratch_shapes=[
            pltpu.VMEM((D, SEQ), bf16),
            pltpu.VMEM((SEQ, D), bf16),
            pltpu.VMEM((SEQ, D), bf16),
            pltpu.VMEM((D, D), bf16),
            pltpu.VMEM((D, hidden), bf16),
            pltpu.VMEM((hidden, D), bf16),
            pltpu.VMEM((SEQ, hidden), bf16),
            pltpu.VMEM((SEQ, D), f32),
            pltpu.VMEM((SEQ, D), f32),
            pltpu.VMEM((16, SEQ), f32),
            pltpu.VMEM((2, 8, SEQ), f32),
            pltpu.VMEM((D, SEQ), bf16),
            pltpu.VMEM((SEQ, D), f32),
            pltpu.VMEM((2, heads, SEQ, QB), bf16),
            pltpu.SemaphoreType.DMA((2,)),
            pltpu.SemaphoreType.DMA((2 * (hidden // FCHUNK) + 11,)),
        ],
        compiler_params=pltpu.CompilerParams(vmem_limit_bytes=VMEM_BYTES),
        cost_estimate=pl.CostEstimate(flops=60 * 10**9, bytes_accessed=40 * 10**6, transcendentals=4 * 10**6),
        name="feed_forward_and_back",
    )(own, lengths, *kept, x, out_grad, *frozen, *weights, gain_attn, gain_ffn, flat)


def sum_everywhere(value):
    for axis in ("head", "dp"):
        size = lax.axis_size(axis)
        step = 1
        while step < size:
            value = value + lax.ppermute(value, axis, [(place, place ^ step) for place in range(size)])
            step = 2 * step
    return value


def on_device(
    hidden_in,
    lengths,
    buckets,
    gain_attn,
    gain_ffn,
    w_query,
    w_key,
    w_value,
    w_attn_out,
    w_in,
    w_ffn_out,
    rel_bias,
    out_grad,
    adapter_weights,
    first_moment,
    second_moment,
    ema_weights,
):
    swap = [(0, 1), (1, 0)]
    own = lax.axis_index("head").astype(jnp.int32).reshape(1)

    def other(value):
        return lax.ppermute(value, "head", swap)

    table = rel_bias.T
    own_qkv = (w_query, w_key, w_value)
    other_qkv = tuple(other(weight) for weight in own_qkv)
    other_table = other(table)
    rest = (w_attn_out, w_in, w_ffn_out)
    frozen = tuple(piece for weight in rest for piece in (weight, other(weight)))
    *kept, packed = attention_forward(
        True, own, lengths, hidden_in, gain_attn, own_qkv, buckets, table
    )
    kept = attention_forward(
        False, own, lengths, packed, gain_attn, other_qkv, buckets, other_table, kept
    )
    layer_out, grad_in, local_grad = feed_forward_and_back(
        own, lengths, kept, packed, out_grad, frozen, own_qkv + other_qkv, gain_attn, gain_ffn, adapter_weights
    )
    total_grad = sum_everywhere(local_grad)
    new_first = beta_one * first_moment + (1.0 - beta_one) * total_grad
    new_second = beta_two * second_moment + (1.0 - beta_two) * total_grad * total_grad
    first_hat = new_first / (1.0 - beta_one**STEP)
    second_hat = new_second / (1.0 - beta_two**STEP)
    new_weights = adapter_weights - learn_rate * (
        first_hat / (jnp.sqrt(second_hat) + adam_eps) + weight_decay * adapter_weights
    )
    new_ema = ema_decay * ema_weights + (1.0 - ema_decay) * new_weights
    return (layer_out, grad_in, new_weights, new_first, new_second, new_ema)


def solution(mesh):
    placed = (
        P("dp", None),
        P("dp", None),
        P(),
        P(),
        P(),
        P(None, "head"),
        P(None, "head"),
        P(None, "head"),
        P("head", None),
        P(None, "head"),
        P("head", None),
        P(None, "head"),
        P(("dp", "head"), None),
        P(),
        P(),
        P(),
        P(),
    )
    return jax.shard_map(
        on_device,
        mesh=mesh,
        in_specs=placed,
        out_specs=(P(("dp", "head"), None), P(("dp", "head"), None), P(), P(), P(), P()),
        check_vma=False,
    )
```

```python
import functools

import jax
import jax.numpy as jnp
from jax import lax
from jax.experimental import pallas as pl
from jax.experimental.pallas import tpu as pltpu
from jax.sharding import PartitionSpec as P

D = 768
DH = 64
KRON = 4
BOTTLE = 48
SEQ = 1024
MOST = 512
STEP = 10
QB = 256
KB = 256
NQ = SEQ // QB
PAIR = 2 * DH
FCHUNK = 512
REACH = QB + MOST - 128
SPREAD = REACH + MOST + QB
CODES = SPREAD + 128
VMEM_BYTES = 127 * 2**19

eps_norm = 1e-06
beta_one = 0.9
beta_two = 0.999
adam_eps = 1e-08
learn_rate = 0.6
weight_decay = 0.01
ema_decay = 0.9
masked_score = -1e30
log2_e = 1.4426950408889634
highest = lax.Precision.HIGHEST
f32 = jnp.float32
bf16 = jnp.bfloat16


def nn(left, right):
    return lax.dot_general(left, right, (((1,), (0,)), ((), ())), preferred_element_type=f32)


def nt(left, right):
    return lax.dot_general(left, right, (((1,), (1,)), ((), ())), preferred_element_type=f32)


def tn(left, right):
    return lax.dot_general(left, right, (((0,), (0,)), ((), ())), preferred_element_type=f32)


def row_plan(len_ref, own):
    docs = len_ref.shape[1]
    sizes = [len_ref[own, doc] for doc in range(docs)]
    longest, chosen = sizes[0], jnp.int32(0)
    for doc in range(1, docs):
        longer = sizes[doc] > longest
        chosen = jnp.where(longer, doc, chosen)
        longest = jnp.maximum(longest, sizes[doc])
    start = jnp.int32(0)
    for doc in range(docs):
        start = start + jnp.where(doc < chosen, sizes[doc], 0)
    ends, total = [], jnp.int32(0)
    for doc in range(docs):
        total = total + len_ref[own, lax.rem(chosen + doc, docs)]
        ends.append(total)
    return start, ends


def key_span(ends, first_row, last_row):
    begin, finish = jnp.int32(0), jnp.int32(SEQ)
    for end in ends:
        begin = jnp.where(end <= first_row, end, begin)
    for end in reversed(ends):
        finish = jnp.where(end > last_row, end, finish)
    return lax.div(begin, KB), lax.div(finish + (KB - 1), KB)


def rotate_rows(source_ref, target_ref, shift):
    groups = SEQ // 8
    fine, coarse = shift & 7, shift >> 3
    back = (8 - fine) & 7
    keep = lax.broadcasted_iota(jnp.int32, (8, target_ref.shape[1]), 0) < 8 - fine

    def turned(group):
        rows = source_ref[pl.ds(pl.multiple_of((group & (groups - 1)) * 8, 16), 16), :].astype(f32)
        return pltpu.roll(rows[0:8], back, 0), pltpu.roll(rows[8:16], back, 0)

    def some(part, carry):
        first, second = carry
        for pair in range(4):
            group = part * 8 + pair * 2
            third, fourth = turned(group + 2)
            for place, left, right in ((0, first, second), (1, second, third)):
                to = ((group + place - coarse) & (groups - 1)) * 8
                target_ref[pl.ds(pl.multiple_of(to, 8), 8), :] = jnp.where(keep, left, right)
            first, second = third, fourth
        return first, second

    lax.fori_loop(0, groups // 8, some, turned(jnp.int32(0)))


def one_head(pair, half):
    lane = lax.broadcasted_iota(jnp.int32, pair.shape, 1)
    keep = lane < DH if half == 0 else lane >= DH
    return jnp.where(keep, pair, jnp.zeros_like(pair))


def flip_lanes(value):
    tiles = value.shape[1] // 128
    row = lax.broadcasted_iota(jnp.int32, (128, 128), 0)
    lane = lax.broadcasted_iota(jnp.int32, (128, 128), 1)
    stacked = jnp.concatenate([value[:, tile * 128 : tile * 128 + 128] for tile in range(tiles)], axis=0)
    flipped = exact(stacked, (row + lane == 127).astype(f32))
    return jnp.concatenate([flipped[tile * 8 : tile * 8 + 8, :] for tile in reversed(range(tiles))], axis=1)


def exact(left, right):
    return lax.dot_general(
        left, right, (((1,), (0,)), ((), ())), precision=highest, preferred_element_type=f32
    )


def bias_bands(buckets_ref, table_ref, bias_ref):
    heads = table_ref.shape[0]
    top = REACH + 128 + SEQ - 1
    codes = buckets_ref[...].reshape(1, 2 * SEQ - 1)[:, top - CODES + 1 : top + 1]
    bucket = lax.broadcasted_iota(jnp.int32, (table_ref.shape[1], CODES), 0)
    per_head = exact(table_ref[...] * log2_e, (bucket == codes).astype(f32))
    per_head = flip_lanes(jnp.concatenate([per_head, jnp.zeros((8 - heads, CODES), f32)], axis=0))
    for head in range(heads):
        spread = jnp.broadcast_to(per_head[head : head + 1, :], (128, CODES))
        spread = pltpu.roll(spread, CODES - 128, 1, stride=1, stride_axis=0)
        bias_ref[head] = spread[:, :SPREAD]


def attention_kernel(leading, *refs):
    own_ref, len_ref, x_hbm, wq_hbm, wk_hbm, wv_hbm = refs[:6]
    gain_ref, buckets_ref, table_ref = refs[6:9]
    if leading:
        prob_hbm, q_hbm, k_hbm, v_hbm, ctx_hbm, shrink_hbm, packed_hbm = refs[9:16]
    else:
        prob_hbm, q_hbm, k_hbm, v_hbm, ctx_hbm, shrink_hbm = refs[15:21]
    (
        x_ref,
        w_ref,
        q_ref,
        k_ref,
        v_ref,
        vt_ref,
        ctx_ref,
        shrink_ref,
        bias_ref,
        dk_ref,
        dq_ref,
        prob_ref,
        turned_ref,
        prob_sems,
        ctx_sems,
        sems,
    ) = refs[-16:]
    heads = table_ref.shape[0]
    width = heads * DH
    group = 0 if leading else 1
    columns = slice(group * width, group * width + width)
    if leading:
        x_hbm = x_hbm.at[pl.ds(pl.multiple_of(own_ref[0] * SEQ, SEQ), SEQ), :]
    loads = [pltpu.make_async_copy(x_hbm, x_ref, sems.at[0])]
    for place, source in enumerate((wq_hbm, wk_hbm, wv_hbm)):
        target = w_ref.at[:, place * width : place * width + width]
        loads.append(pltpu.make_async_copy(source, target, sems.at[1 + place]))
    for load in loads:
        load.start()
    start, ends = row_plan(len_ref, own_ref[0])
    row = lax.broadcasted_iota(jnp.int32, dk_ref.shape, 0)
    dk_ref[...] = sum((row >= end).astype(jnp.int32) for end in ends)
    lane = lax.broadcasted_iota(jnp.int32, dq_ref.shape, 1)
    dq_ref[...] = sum((lane >= end).astype(jnp.int32) for end in ends)
    bias_bands(buckets_ref, table_ref, bias_ref)
    stores = []

    def store(source, target, place):
        copy = pltpu.make_async_copy(source, target, sems.at[place])
        copy.start()
        stores.append(copy)

    loads[0].wait()
    if not leading:
        inputs = x_ref[...].astype(f32)
    if leading:
        rotate_rows(x_ref, turned_ref, start)
        inputs = turned_ref[...]
        x_ref[...] = inputs.astype(bf16)
        store(x_ref, packed_hbm, 4)
    scale = lax.rsqrt(jnp.mean(inputs * inputs, axis=1, keepdims=True) + eps_norm)
    normed = (inputs * scale * gain_ref[...].reshape(1, D)).astype(bf16)
    for load in loads[1:]:
        load.wait()
    projected = nn(normed, w_ref[...])
    q_ref[...] = (projected[:, 0:width] * log2_e).astype(bf16)
    k_ref[...] = projected[:, width : 2 * width].astype(bf16)
    values = projected[:, 2 * width : 3 * width].astype(bf16)
    v_ref[...] = values
    vt_ref[...] = values.T
    store(q_ref, q_hbm.at[:, columns], 5)
    store(k_ref, k_hbm.at[:, columns], 6)
    store(v_ref, v_hbm.at[:, columns], 7)

    def prob_copy(step, count):
        slot, rows = lax.rem(step, 2), count * KB
        return pltpu.make_async_copy(
            prob_ref.at[slot, :, 0:rows, :], prob_hbm.at[group, :, step, 0:rows, :], prob_sems.at[slot]
        )

    def with_span(step, action):
        begin, finish = key_span(ends, step * QB, step * QB + QB - 1)
        for count in range(QB // KB, SEQ // KB + 1):
            pl.when(finish - begin == count)(functools.partial(action, step, begin, count))

    def ctx_copy(step):
        query_rows = pl.ds(pl.multiple_of(step * QB, QB), QB)
        return pltpu.make_async_copy(
            ctx_ref.at[:, query_rows], ctx_hbm.at[columns, query_rows], ctx_sems.at[step]
        )

    def drain(step, begin, count):
        prob_copy(step, count).wait()

    def attend(step, begin, count):
        rows = count * KB
        slot = lax.rem(step, 2)
        first_row, first_key = step * QB, pl.multiple_of(begin * KB, KB)
        key_rows = pl.ds(first_key, rows)
        query_rows = pl.ds(pl.multiple_of(first_row, QB), QB)
        doc_key = jnp.concatenate([dk_ref[key_rows, :]] * (QB // 128), axis=1)
        same = doc_key == dq_ref[0:1, query_rows]
        scores = []
        for head in range(heads):
            lanes = slice(head // 2 * PAIR, head // 2 * PAIR + PAIR)
            scores.append(nt(k_ref[key_rows, lanes], one_head(q_ref[query_rows, lanes], head % 2)))
        totals = []
        for head in range(heads):
            bias = jnp.concatenate(
                [
                    bias_ref[
                        head,
                        :,
                        pl.ds(pl.multiple_of(first_row - first_key + (REACH - part * 128), 128), QB),
                    ]
                    for part in range(rows // 128)
                ],
                axis=0,
            )
            score = jnp.where(same, scores[head] + bias, masked_score)
            expo = jnp.exp2(score - jnp.max(score, axis=0, keepdims=True))
            totals.append(1.0 / jnp.sum(expo, axis=0, keepdims=True))
            prob_ref[slot, head, 0:rows, :] = expo.astype(bf16)
        for head in range(heads):
            band = slice(head * DH, head * DH + DH)
            context = nn(vt_ref[band, key_rows], prob_ref[slot, head, 0:rows, :])
            ctx_ref[band, query_rows] = (context * totals[head]).astype(bf16)
            shrink_ref[head : head + 1, query_rows] = totals[head]
        prob_copy(step, count).start()
        ctx_copy(step).start()

    def one_block(step, carry):
        @pl.when(step >= 2)
        def _drain():
            with_span(step - 2, drain)

        with_span(step, attend)
        return carry

    lax.fori_loop(0, NQ, one_block, 0)
    store(shrink_ref, shrink_hbm.at[group], 8)
    for step in range(NQ):
        ctx_copy(step).wait()
    with_span(NQ - 2, drain)
    with_span(NQ - 1, drain)
    for copy in stores:
        copy.wait()


def attention_forward(leading, own, lengths, x, gain, weights, buckets, table, kept=()):
    heads = table.shape[0]
    width = heads * DH
    any_space = pl.BlockSpec(memory_space=pl.ANY)
    vmem = pl.BlockSpec(memory_space=pltpu.VMEM)
    smem = pl.BlockSpec(memory_space=pltpu.SMEM)
    out_shape = [
        jax.ShapeDtypeStruct((2, heads, NQ, SEQ, QB), bf16),
        jax.ShapeDtypeStruct((SEQ, 2 * width), bf16),
        jax.ShapeDtypeStruct((SEQ, 2 * width), bf16),
        jax.ShapeDtypeStruct((SEQ, 2 * width), bf16),
        jax.ShapeDtypeStruct((2 * width, SEQ), bf16),
        jax.ShapeDtypeStruct((2, 8, SEQ), f32),
    ]
    if leading:
        out_shape.append(jax.ShapeDtypeStruct((SEQ, D), bf16))
    return pl.pallas_call(
        functools.partial(attention_kernel, leading),
        in_specs=[smem, smem] + [any_space] * 4 + [vmem] * 3 + [any_space] * len(kept),
        out_specs=[any_space] * len(out_shape),
        out_shape=out_shape,
        scratch_shapes=[
            pltpu.VMEM((SEQ, D), bf16),
            pltpu.VMEM((D, 3 * width), bf16),
            pltpu.VMEM((SEQ, width), bf16),
            pltpu.VMEM((SEQ, width), bf16),
            pltpu.VMEM((SEQ, width), bf16),
            pltpu.VMEM((width, SEQ), bf16),
            pltpu.VMEM((width, SEQ), bf16),
            pltpu.VMEM((8, SEQ), f32),
            pltpu.VMEM((heads, 128, SPREAD), f32),
            pltpu.VMEM((SEQ, 128), jnp.int32),
            pltpu.VMEM((8, SEQ), jnp.int32),
            pltpu.VMEM((2, heads, SEQ, QB), bf16),
            pltpu.VMEM((SEQ if leading else 8, D), f32),
            pltpu.SemaphoreType.DMA((2,)),
            pltpu.SemaphoreType.DMA((NQ,)),
            pltpu.SemaphoreType.DMA((9,)),
        ],
        input_output_aliases={9 + place: place for place in range(len(kept))},
        compiler_params=pltpu.CompilerParams(vmem_limit_bytes=VMEM_BYTES),
        cost_estimate=pl.CostEstimate(flops=15 * 10**9, bytes_accessed=16 * 10**6, transcendentals=4 * 10**6),
        name="attention_forward_own" if leading else "attention_forward_other",
    )(own, lengths, x, *weights, gain, buckets, table, *kept)


root_two_over_pi = 0.7978845608028654
cubic = 0.044715


def gelu_both(value):
    square = value * value
    slow = jnp.tanh(value * (root_two_over_pi + (root_two_over_pi * cubic) * square))
    half = 0.5 * value
    act = half + half * slow
    slope = (0.5 + 0.5 * slow) + half * (1.0 - slow * slow) * (
        root_two_over_pi + (3.0 * root_two_over_pi * cubic) * square
    )
    return act, slope


def block_of(index, width, blocks):
    return sum((index >= width * place).astype(jnp.int32) for place in range(1, blocks))


class Kronecker:
    def __init__(self, core, small, large, factor, swapped):
        terms, rows = KRON, KRON * KRON
        sub, leaf = BOTTLE // KRON, D // KRON
        self.factor = factor
        row = lax.broadcasted_iota(jnp.int32, (rows, rows * KRON), 0)
        item = lax.broadcasted_iota(jnp.int32, (rows, rows * KRON), 1)
        item_of = lax.broadcasted_iota(jnp.int32, (rows * KRON, BOTTLE), 0)
        lane_block = block_of(lax.broadcasted_iota(jnp.int32, (rows * KRON, BOTTLE), 1), sub, KRON)
        if swapped:
            self.holds = ((item >> 4) == (row >> 2)) & ((item & 3) == (row & 3))
            pick = ((item_of >> 2) & 3) == lane_block
        else:
            self.holds = (item >> 2) == row
            pick = (item_of & 3) == lane_block
        self.pick = pick.astype(f32)
        self.core = exact(jnp.where(self.holds, jnp.broadcast_to(core, self.holds.shape), 0.0), self.pick)
        self.small = jnp.concatenate(
            [
                jnp.broadcast_to(
                    jnp.concatenate([small[:, n * sub : n * sub + sub]] * KRON, axis=1), (KRON, BOTTLE)
                )
                for n in range(terms)
            ],
            axis=0,
        )
        large = jnp.concatenate(
            [
                jnp.broadcast_to(
                    jnp.concatenate([large[:, n * leaf : n * leaf + leaf]] * KRON, axis=1), (KRON, D)
                )
                for n in range(terms)
            ],
            axis=0,
        )
        row = lax.broadcasted_iota(jnp.int32, (rows, D), 0)
        lane = lax.broadcasted_iota(jnp.int32, (rows, D), 1)
        self.diagonal = (row & 3) == block_of(lane, leaf, KRON)
        self.large = jnp.where(self.diagonal, large, 0.0)
        self.mix = self.core * self.small

    def matrix(self):
        return exact(self.mix.T, self.large) * self.factor

    def gradient(self, grad):
        sub, leaf = BOTTLE // KRON, D // KRON
        inner = self.factor * lax.dot_general(
            self.large, grad, (((1,), (1,)), ((), ())), precision=highest, preferred_element_type=f32
        )
        core = lax.dot_general(
            self.small * inner, self.pick, (((1,), (1,)), ((), ())), precision=highest, preferred_element_type=f32
        )
        core = jnp.sum(jnp.where(self.holds, core, 0.0), axis=0, keepdims=True)
        by_term = self.core * inner
        outer = self.factor * jnp.where(self.diagonal, exact(self.mix, grad), 0.0)
        small, large = [], []
        for n in range(KRON):
            row = jnp.sum(by_term[n * KRON : n * KRON + KRON, :], axis=0, keepdims=True)
            small.append(sum(row[:, b * sub : b * sub + sub] for b in range(KRON)))
            row = jnp.sum(outer[n * KRON : n * KRON + KRON, :], axis=0, keepdims=True)
            large.append(sum(row[:, a * leaf : a * leaf + leaf] for a in range(KRON)))
        return core, jnp.concatenate(small, axis=1), jnp.concatenate(large, axis=1)


def both_adapters(flat):
    widths = (KRON * KRON * KRON, D, BOTTLE, BOTTLE, D, BOTTLE, D)
    pieces, place = [], 0
    for width in widths:
        pieces.append(flat[:, place : place + width])
        place = place + width
    core, down_left, down_right, up_left, up_right, bias_down, bias_up = pieces
    down = Kronecker(core, down_right, down_left, (KRON * D) ** (-0.5), False)
    up = Kronecker(core, up_left, up_right, BOTTLE ** (-0.5), True)
    return down, up, bias_down, bias_up


def feed_forward_kernel(
    own_ref,
    len_ref,
    prob_hbm,
    q_hbm,
    k_hbm,
    v_hbm,
    ctx_hbm,
    shrink_hbm,
    x_hbm,
    grad_hbm,
    wo_own,
    wo_other,
    win_own,
    win_other,
    wout_own,
    wout_other,
    wq_own,
    wk_own,
    wv_own,
    wq_other,
    wk_other,
    wv_other,
    gain_attn_ref,
    gain_ffn_ref,
    flat_ref,
    out_hbm,
    grad_in_hbm,
    flat_grad_ref,
    ctx_ref,
    x_ref,
    grad_ref,
    wo_ref,
    win_ref,
    wout_ref,
    slope_ref,
    res_ref,
    res_grad_ref,
    delta_ref,
    shrink_ref,
    dqt_ref,
    sums_ref,
    prob_ref,
    prob_sems,
    sems,
):
    start, ends = row_plan(len_ref, own_ref[0])
    half = wo_own.shape[0]
    hidden = win_own.shape[1]
    heads = half // DH
    chunks = 2 * hidden // FCHUNK
    side = hidden // FCHUNK

    def load(source, target, place):
        return pltpu.make_async_copy(source, target, sems.at[place])

    first = [
        load(ctx_hbm, ctx_ref, 0),
        load(wo_own, wo_ref.at[0:half, :], 1),
        load(wo_other, wo_ref.at[half : 2 * half, :], 2),
        load(x_hbm, x_ref, 3),
    ]
    win_loads, wout_loads = [], []
    for chunk in range(chunks):
        source = win_own if chunk < side else win_other
        place = chunk % side * FCHUNK
        cols = slice(chunk * FCHUNK, chunk * FCHUNK + FCHUNK)
        win_loads.append(load(source.at[:, place : place + FCHUNK], win_ref.at[:, cols], 4 + chunk))
        source = wout_own if chunk < side else wout_other
        wout_loads.append(load(source.at[place : place + FCHUNK, :], wout_ref.at[cols, :], 4 + chunks + chunk))
    base = 4 + 2 * chunks
    grad_load = load(grad_hbm, grad_ref, base)
    v_ref, k_ref, q_ref = (wout_ref.at[place * SEQ : place * SEQ + SEQ, :] for place in range(3))
    late = [
        load(v_hbm, v_ref, base + 1),
        load(k_hbm, k_ref, base + 3),
        load(q_hbm, q_ref, base + 2),
    ]
    shrink_load = load(shrink_hbm, shrink_ref, base + 4)
    out_copy = load(res_grad_ref, out_hbm, base + 5)
    grad_in_copy = load(res_ref, grad_in_hbm, base + 6)
    qkv_loads = [
        load(source, win_ref.at[:, place * half : place * half + half], 4 + place)
        for place, source in enumerate((wq_own, wq_other, wk_own, wk_other, wv_own, wv_other))
    ]
    for copy in first:
        copy.start()
    for chunk in range(chunks):
        win_loads[chunk].start()
        wout_loads[chunk].start()
    grad_load.start()
    shrink_load.start()

    def prob_copy(it, count):
        slot, rows = lax.rem(it, 2), count * KB
        return pltpu.make_async_copy(
            prob_hbm.at[lax.div(it, NQ), :, lax.rem(it, NQ), 0:rows, :],
            prob_ref.at[slot, :, 0:rows, :],
            prob_sems.at[slot],
        )

    def with_span(it, action):
        first_row = lax.rem(it, NQ) * QB
        begin, finish = key_span(ends, first_row, first_row + QB - 1)
        for count in range(QB // KB, SEQ // KB + 1):
            pl.when(finish - begin == count)(functools.partial(action, it, begin, count))

    def fetch(it, begin, count):
        prob_copy(it, count).start()

    with_span(jnp.int32(0), fetch)
    flat = flat_ref[...].reshape(1, flat_ref.shape[0])
    down_maker, up_maker, bias_down, bias_up = both_adapters(flat)
    down, up = down_maker.matrix().astype(bf16), up_maker.matrix().astype(bf16)
    gain = gain_ffn_ref[...].reshape(1, D)
    for copy in first:
        copy.wait()
    residual = x_ref[...].astype(f32) + tn(ctx_ref[...], wo_ref[...])
    res_ref[...] = residual
    scale = lax.rsqrt(jnp.mean(residual * residual, axis=1, keepdims=True) + eps_norm)
    low = (residual * scale * gain).astype(bf16)

    def cols_of(chunk):
        return slice(chunk * FCHUNK, chunk * FCHUNK + FCHUNK)

    previous = None
    for copy in win_loads + wout_loads:
        copy.wait()
    pre = nn(low, win_ref[:, cols_of(0)])
    for chunk in range(chunks):
        if chunk + 1 < chunks:
            ahead = nn(low, win_ref[:, cols_of(chunk + 1)])
        if previous is not None:
            part = nn(previous, wout_ref[cols_of(chunk - 1), :])
            if chunk == 1:
                sums_ref[...] = part
            else:
                sums_ref[...] += part
        act, slope = gelu_both(pre)
        slope_ref[:, cols_of(chunk)] = slope.astype(bf16)
        previous, pre = act.astype(bf16), ahead
    mixed = sums_ref[...] + nn(previous, wout_ref[cols_of(chunks - 1), :])
    grad_load.wait()
    rotate_rows(grad_ref, res_grad_ref, start)
    out_grad_low = res_grad_ref[...].astype(bf16)
    grad_ref[...] = out_grad_low
    mixed_low = mixed.astype(bf16)
    bottle, bottle_slope = gelu_both(nt(mixed_low, down) + bias_down)
    bottle_low = bottle.astype(bf16)
    sums_ref[...] = res_ref[...] + mixed + nn(bottle_low, up) + bias_up
    rotate_rows(sums_ref, res_grad_ref, SEQ - start)
    out_copy.start()
    bottle_grad = (nt(out_grad_low, up) * bottle_slope).astype(bf16)
    mixed_grad = (out_grad_low.astype(f32) + nn(bottle_grad, down)).astype(bf16)
    up_grad = tn(bottle_low, out_grad_low)
    down_grad = tn(bottle_grad, mixed_low)
    pre = nt(mixed_grad, wout_ref[cols_of(0), :])
    for chunk in range(chunks):
        if chunk + 1 < chunks:
            ahead = nt(mixed_grad, wout_ref[cols_of(chunk + 1), :])
        if chunk == 2:
            core_down, right_down, left_down = down_maker.gradient(down_grad)
            core_up, left_up, right_up = up_maker.gradient(up_grad)
            flat_grad = jnp.concatenate(
                [
                    core_down + core_up,
                    left_down,
                    right_down,
                    left_up,
                    right_up,
                    jnp.sum(bottle_grad.astype(f32), axis=0, keepdims=True),
                    jnp.sum(out_grad_low.astype(f32), axis=0, keepdims=True),
                ],
                axis=1,
            )
            flat_grad_ref[...] = flat_grad.reshape(flat_grad_ref.shape[0])
        pre_grad = (pre * slope_ref[:, cols_of(chunk)].astype(f32)).astype(bf16)
        part = nt(pre_grad, win_ref[:, cols_of(chunk)])
        if chunk == 0:
            sums_ref[...] = part
        else:
            sums_ref[...] += part
        pre = ahead
    for copy in late + qkv_loads:
        copy.start()
    residual = res_ref[...]
    weighted = sums_ref[...] * gain
    inner = jnp.mean(residual * weighted, axis=1, keepdims=True)
    res_grad = grad_ref[...].astype(f32) + scale * weighted - residual * (scale * scale * scale * inner)
    out_copy.wait()
    res_grad_ref[...] = res_grad
    shrink_load.wait()
    shrink = jnp.concatenate([shrink_ref[0, 0:heads, :], shrink_ref[1, 0:heads, :]], axis=0)
    shrink_top = shrink.astype(bf16)
    shrink_rest = (shrink - shrink_top.astype(f32)).astype(bf16)
    head_row = lax.broadcasted_iota(jnp.int32, (2 * heads, D), 0)
    head_lane = lax.broadcasted_iota(jnp.int32, (2 * heads, D), 1) >> 6
    spread = (head_row == head_lane).astype(bf16)
    shrink_wide = tn(shrink_top, spread) + tn(shrink_rest, spread)
    dctx = (nt(res_grad.astype(bf16), wo_ref[...]) * shrink_wide).astype(bf16)
    grad_ref[...] = dctx
    product = dctx.T.astype(f32) * ctx_ref[...].astype(f32)
    delta_ref[0 : 2 * heads, :] = jnp.sum(product.reshape(2 * heads, DH, SEQ), axis=1)
    for copy in late:
        copy.wait()
    kt_ref, dctx_ref = ctx_ref, grad_ref
    kt_ref[...] = k_ref[...].T

    def attend(it, begin, count):
        rows = count * KB
        slot, group = lax.rem(it, 2), lax.div(it, NQ)
        key_rows = pl.ds(pl.multiple_of(begin * KB, KB), rows)
        query_rows = pl.ds(pl.multiple_of(lax.rem(it, NQ) * QB, QB), QB)
        prob_copy(it, count).wait()

        def lanes(pair):
            return pl.ds(pl.multiple_of(group * half + pair * PAIR, PAIR), PAIR)

        together = heads if count <= 2 else 2
        for lead in range(0, heads, together):
            members = range(lead, lead + together)
            grads, prob_grads, score_grads = {}, {}, {}
            for head in members:
                grads[head] = one_head(dctx_ref[query_rows, lanes(head // 2)], head % 2)
                prob_grads[head] = nt(v_ref[key_rows, lanes(head // 2)], grads[head])
            for head in members:
                delta = delta_ref[pl.ds(group * heads + head, 1), query_rows]
                prob = prob_ref[slot, head, 0:rows, :].astype(f32)
                score_grads[head] = (prob * (prob_grads[head] - delta)).astype(bf16)
            for pair in range(lead // 2, (lead + together) // 2):
                dk = dv = None
                for head in (2 * pair, 2 * pair + 1):
                    band = pl.ds(pl.multiple_of(group * half + head * DH, DH), DH)
                    queries = one_head(q_ref[query_rows, lanes(pair)], head % 2)
                    dv_part = nn(prob_ref[slot, head, 0:rows, :], grads[head])
                    dk_part = nn(score_grads[head], queries)
                    dv = dv_part if dv is None else dv + dv_part
                    dk = dk_part if dk is None else dk + dk_part
                    dqt_ref[band, query_rows] = nn(kt_ref[band, key_rows], score_grads[head]).astype(bf16)
                sums_ref[key_rows, pair * PAIR : pair * PAIR + PAIR] += dk
                sums_ref[key_rows, half + pair * PAIR : half + pair * PAIR + PAIR] += dv

    def one_block(it, carry):
        @pl.when(it + 1 < 2 * NQ)
        def _ahead():
            with_span(it + 1, fetch)

        @pl.when(lax.rem(it, NQ) == 0)
        def _clear():
            sums_ref[...] = jnp.zeros_like(sums_ref)

        with_span(it, attend)
        for group in range(2):

            @pl.when(it == group * NQ + NQ - 1)
            def _collect():
                place = (2 + group) * half
                slope_ref[:, place : place + half] = (sums_ref[:, 0:half] * (1.0 / log2_e)).astype(bf16)
                place = (4 + group) * half
                slope_ref[:, place : place + half] = sums_ref[:, half : 2 * half].astype(bf16)

        return carry

    lax.fori_loop(0, 2 * NQ, one_block, 0)
    slope_ref[:, 0 : 2 * half] = dqt_ref[...].T
    for copy in qkv_loads:
        copy.wait()
    normed_grad = nt(slope_ref[:, 0 : 6 * half], win_ref[:, 0 : 6 * half])
    inputs = x_ref[...].astype(f32)
    scale = lax.rsqrt(jnp.mean(inputs * inputs, axis=1, keepdims=True) + eps_norm)
    weighted = normed_grad * gain_attn_ref[...].reshape(1, D)
    inner = jnp.mean(inputs * weighted, axis=1, keepdims=True)
    sums_ref[...] = res_grad_ref[...] + scale * weighted - inputs * (scale * scale * scale * inner)
    rotate_rows(sums_ref, res_ref, SEQ - start)
    grad_in_copy.start()
    grad_in_copy.wait()


def feed_forward_and_back(own, lengths, kept, x, out_grad, frozen, weights, gain_attn, gain_ffn, flat):
    any_space = pl.BlockSpec(memory_space=pl.ANY)
    vmem = pl.BlockSpec(memory_space=pltpu.VMEM)
    smem = pl.BlockSpec(memory_space=pltpu.SMEM)
    hidden = 2 * frozen[2].shape[1]
    heads = kept[0].shape[1]
    half = heads * DH
    return pl.pallas_call(
        feed_forward_kernel,
        in_specs=[smem, smem] + [any_space] * 20 + [vmem] * 3,
        out_specs=[any_space, any_space, vmem],
        out_shape=[
            jax.ShapeDtypeStruct((SEQ, D), f32),
            jax.ShapeDtypeStruct((SEQ, D), f32),
            jax.ShapeDtypeStruct(flat.shape, f32),
        ],
        scratch_shapes=[
            pltpu.VMEM((D, SEQ), bf16),
            pltpu.VMEM((SEQ, D), bf16),
            pltpu.VMEM((SEQ, D), bf16),
            pltpu.VMEM((D, D), bf16),
            pltpu.VMEM((D, hidden), bf16),
            pltpu.VMEM((hidden, D), bf16),
            pltpu.VMEM((SEQ, hidden), bf16),
            pltpu.VMEM((SEQ, D), f32),
            pltpu.VMEM((SEQ, D), f32),
            pltpu.VMEM((16, SEQ), f32),
            pltpu.VMEM((2, 8, SEQ), f32),
            pltpu.VMEM((D, SEQ), bf16),
            pltpu.VMEM((SEQ, D), f32),
            pltpu.VMEM((2, heads, SEQ, QB), bf16),
            pltpu.SemaphoreType.DMA((2,)),
            pltpu.SemaphoreType.DMA((2 * (hidden // FCHUNK) + 11,)),
        ],
        compiler_params=pltpu.CompilerParams(vmem_limit_bytes=VMEM_BYTES),
        cost_estimate=pl.CostEstimate(flops=60 * 10**9, bytes_accessed=40 * 10**6, transcendentals=4 * 10**6),
        name="feed_forward_and_back",
    )(own, lengths, *kept, x, out_grad, *frozen, *weights, gain_attn, gain_ffn, flat)


def sum_everywhere(value):
    for axis in ("head", "dp"):
        size = lax.axis_size(axis)
        step = 1
        while step < size:
            value = value + lax.ppermute(value, axis, [(place, place ^ step) for place in range(size)])
            step = 2 * step
    return value


def on_device(
    hidden_in,
    lengths,
    buckets,
    gain_attn,
    gain_ffn,
    w_query,
    w_key,
    w_value,
    w_attn_out,
    w_in,
    w_ffn_out,
    rel_bias,
    out_grad,
    adapter_weights,
    first_moment,
    second_moment,
    ema_weights,
):
    swap = [(0, 1), (1, 0)]
    own = lax.axis_index("head").astype(jnp.int32).reshape(1)

    def other(value):
        return lax.ppermute(value, "head", swap)

    table = rel_bias.T
    own_qkv = (w_query, w_key, w_value)
    other_qkv = tuple(other(weight) for weight in own_qkv)
    other_table = other(table)
    rest = (w_attn_out, w_in, w_ffn_out)
    frozen = tuple(piece for weight in rest for piece in (weight, other(weight)))
    *kept, packed = attention_forward(
        True, own, lengths, hidden_in, gain_attn, own_qkv, buckets, table
    )
    kept = attention_forward(
        False, own, lengths, packed, gain_attn, other_qkv, buckets, other_table, kept
    )
    layer_out, grad_in, local_grad = feed_forward_and_back(
        own, lengths, kept, packed, out_grad, frozen, own_qkv + other_qkv, gain_attn, gain_ffn, adapter_weights
    )
    total_grad = sum_everywhere(local_grad)
    new_first = beta_one * first_moment + (1.0 - beta_one) * total_grad
    new_second = beta_two * second_moment + (1.0 - beta_two) * total_grad * total_grad
    first_hat = new_first / (1.0 - beta_one**STEP)
    second_hat = new_second / (1.0 - beta_two**STEP)
    new_weights = adapter_weights - learn_rate * (
        first_hat / (jnp.sqrt(second_hat) + adam_eps) + weight_decay * adapter_weights
    )
    new_ema = ema_decay * ema_weights + (1.0 - ema_decay) * new_weights
    return (layer_out, grad_in, new_weights, new_first, new_second, new_ema)


def solution(mesh):
    placed = (
        P("dp", None),
        P("dp", None),
        P(),
        P(),
        P(),
        P(None, "head"),
        P(None, "head"),
        P(None, "head"),
        P("head", None),
        P(None, "head"),
        P("head", None),
        P(None, "head"),
        P(("dp", "head"), None),
        P(),
        P(),
        P(),
        P(),
    )
    return jax.shard_map(
        on_device,
        mesh=mesh,
        in_specs=placed,
        out_specs=(P(("dp", "head"), None), P(("dp", "head"), None), P(), P(), P(), P()),
        check_vma=False,
    )
```

```python
import functools

import jax
import jax.numpy as jnp
from jax import lax
from jax.experimental import pallas as pl
from jax.experimental.pallas import tpu as pltpu
from jax.sharding import PartitionSpec as P

D = 768
DH = 64
KRON = 4
BOTTLE = 48
SEQ = 1024
MOST = 512
STEP = 10
QB = 256
KB = 256
NQ = SEQ // QB
PAIR = 2 * DH
FCHUNK = 1024
REACH = QB + MOST - 128
SPREAD = REACH + MOST + QB
CODES = SPREAD + 128
VMEM_BYTES = 127 * 2**19

eps_norm = 1e-06
beta_one = 0.9
beta_two = 0.999
adam_eps = 1e-08
learn_rate = 0.6
weight_decay = 0.01
ema_decay = 0.9
masked_score = -1e30
log2_e = 1.4426950408889634
highest = lax.Precision.HIGHEST
f32 = jnp.float32
bf16 = jnp.bfloat16


def nn(left, right):
    return lax.dot_general(left, right, (((1,), (0,)), ((), ())), preferred_element_type=f32)


def nt(left, right):
    return lax.dot_general(left, right, (((1,), (1,)), ((), ())), preferred_element_type=f32)


def tn(left, right):
    return lax.dot_general(left, right, (((0,), (0,)), ((), ())), preferred_element_type=f32)


def row_plan(len_ref, own):
    docs = len_ref.shape[1]
    sizes = [len_ref[own, doc] for doc in range(docs)]
    longest, chosen = sizes[0], jnp.int32(0)
    for doc in range(1, docs):
        longer = sizes[doc] > longest
        chosen = jnp.where(longer, doc, chosen)
        longest = jnp.maximum(longest, sizes[doc])
    start = jnp.int32(0)
    for doc in range(docs):
        start = start + jnp.where(doc < chosen, sizes[doc], 0)
    ends, total = [], jnp.int32(0)
    for doc in range(docs):
        total = total + len_ref[own, lax.rem(chosen + doc, docs)]
        ends.append(total)
    return start, ends


def key_span(ends, first_row, last_row):
    begin, finish = jnp.int32(0), jnp.int32(SEQ)
    for end in ends:
        begin = jnp.where(end <= first_row, end, begin)
    for end in reversed(ends):
        finish = jnp.where(end > last_row, end, finish)
    return lax.div(begin, KB), lax.div(finish + (KB - 1), KB)


def rotate_rows(source_ref, target_ref, shift):
    groups = SEQ // 8
    fine, coarse = shift & 7, shift >> 3
    back = (8 - fine) & 7
    keep = lax.broadcasted_iota(jnp.int32, (8, target_ref.shape[1]), 0) < 8 - fine

    def turned(group):
        rows = source_ref[pl.ds(pl.multiple_of((group & (groups - 1)) * 8, 16), 16), :].astype(f32)
        return pltpu.roll(rows[0:8], back, 0), pltpu.roll(rows[8:16], back, 0)

    def some(part, carry):
        first, second = carry
        for pair in range(4):
            group = part * 8 + pair * 2
            third, fourth = turned(group + 2)
            for place, left, right in ((0, first, second), (1, second, third)):
                to = ((group + place - coarse) & (groups - 1)) * 8
                target_ref[pl.ds(pl.multiple_of(to, 8), 8), :] = jnp.where(keep, left, right)
            first, second = third, fourth
        return first, second

    lax.fori_loop(0, groups // 8, some, turned(jnp.int32(0)))


def rotate_pieces(source_ref, target_ref, shift, pieces, ready):
    groups = SEQ // 8
    fine, coarse = shift & 7, shift >> 3
    back = (8 - fine) & 7
    keep = lax.broadcasted_iota(jnp.int32, (8, target_ref.shape[1]), 0) < 8 - fine

    def turned(group):
        rows = source_ref[pl.ds(pl.multiple_of(((group + coarse) & (groups - 1)) * 8, 8), 8), :]
        return pltpu.roll(rows, back, 0)

    def some(part, before):
        for place in range(8):
            group = part * 8 + place
            after = turned(group + 1)
            target_ref[pl.ds(pl.multiple_of(group * 8, 8), 8), :] = jnp.where(keep, before, after)
            before = after
        return before

    steps = groups // 8 // pieces
    carry = turned(jnp.int32(0))
    for piece in range(pieces):
        carry = lax.fori_loop(piece * steps, piece * steps + steps, some, carry)
        ready(piece)


def one_head(pair, half):
    lane = lax.broadcasted_iota(jnp.int32, pair.shape, 1)
    keep = lane < DH if half == 0 else lane >= DH
    return jnp.where(keep, pair, jnp.zeros_like(pair))


def flip_lanes(value):
    tiles = value.shape[1] // 128
    row = lax.broadcasted_iota(jnp.int32, (128, 128), 0)
    lane = lax.broadcasted_iota(jnp.int32, (128, 128), 1)
    stacked = jnp.concatenate([value[:, tile * 128 : tile * 128 + 128] for tile in range(tiles)], axis=0)
    flipped = exact(stacked, (row + lane == 127).astype(f32))
    return jnp.concatenate([flipped[tile * 8 : tile * 8 + 8, :] for tile in reversed(range(tiles))], axis=1)


def exact(left, right):
    return lax.dot_general(
        left, right, (((1,), (0,)), ((), ())), precision=highest, preferred_element_type=f32
    )


def bias_bands(buckets_ref, table_ref, bias_ref, lead):
    heads = table_ref.shape[0]
    top = REACH + 128 + SEQ - 1
    codes = buckets_ref[...].reshape(1, 2 * SEQ - 1)[:, top - CODES + 1 : top + 1]
    bucket = lax.broadcasted_iota(jnp.int32, (table_ref.shape[1], CODES), 0)
    per_head = exact(table_ref[...] * log2_e, (bucket == codes).astype(f32))
    per_head = flip_lanes(jnp.concatenate([per_head, jnp.zeros((8 - heads, CODES), f32)], axis=0))
    for head in range(heads):
        spread = jnp.broadcast_to(per_head[head : head + 1, :], (128, CODES))
        spread = pltpu.roll(spread, CODES - 128, 1, stride=1, stride_axis=0)
        bias_ref[lead + head] = spread[:, :SPREAD]


def places(first, width):
    return pl.ds(pl.multiple_of(first, width), width)


def key_window(ends, first_row, last_row):
    begin, finish = key_span(ends, first_row, last_row)
    wide = finish - begin > MOST // KB
    return jnp.where(wide, 0, jnp.minimum(begin, (SEQ - MOST) // KB)), wide


def pack_kernel(own_ref, len_ref, x_hbm, grad_hbm, packed_hbm, packed_grad_hbm, x_ref, grad_ref, turned_ref, sems):
    start, _ = row_plan(len_ref, own_ref[0])
    rows = pl.ds(pl.multiple_of(own_ref[0] * SEQ, SEQ), SEQ)
    loads = [
        pltpu.make_async_copy(x_hbm.at[rows, :], x_ref, sems.at[0]),
        pltpu.make_async_copy(grad_hbm, grad_ref, sems.at[1]),
    ]
    stores = [
        pltpu.make_async_copy(x_ref, packed_hbm, sems.at[2]),
        pltpu.make_async_copy(grad_ref, packed_grad_hbm, sems.at[3]),
    ]
    for load in loads:
        load.start()
    for load, store, ref in zip(loads, stores, (x_ref, grad_ref)):
        load.wait()
        rotate_rows(ref, turned_ref, start)
        ref[...] = turned_ref[...].astype(bf16)
        store.start()
    for store in stores:
        store.wait()


def pack(own, lengths, x, out_grad):
    any_space = pl.BlockSpec(memory_space=pl.ANY)
    smem = pl.BlockSpec(memory_space=pltpu.SMEM)
    return pl.pallas_call(
        pack_kernel,
        in_specs=[smem, smem, any_space, any_space],
        out_specs=[any_space, any_space],
        out_shape=[jax.ShapeDtypeStruct((SEQ, D), bf16)] * 2,
        scratch_shapes=[
            pltpu.VMEM((SEQ, D), bf16),
            pltpu.VMEM((SEQ, D), bf16),
            pltpu.VMEM((SEQ, D), f32),
            pltpu.SemaphoreType.DMA((4,)),
        ],
        compiler_params=pltpu.CompilerParams(vmem_limit_bytes=VMEM_BYTES),
        cost_estimate=pl.CostEstimate(flops=3 * 10**9, bytes_accessed=6 * 10**6, transcendentals=0),
        name="pack_rows",
    )(own, lengths, x, out_grad)


def attention_kernel(
    own_ref,
    len_ref,
    x_hbm,
    wq_own,
    wk_own,
    wv_own,
    wq_other,
    wk_other,
    wv_other,
    table_hbm,
    gain_ref,
    buckets_ref,
    table_own,
    prob_hbm,
    q_hbm,
    k_hbm,
    v_hbm,
    ctx_hbm,
    shrink_hbm,
    x_ref,
    w_ref,
    qkv_ref,
    vt_ref,
    ctx_ref,
    shrink_ref,
    table_other,
    bias_ref,
    dk_ref,
    dq_ref,
    prob_ref,
    prob_sems,
    ctx_sems,
    sems,
):
    heads = table_own.shape[0]
    half = heads * DH
    sources = (wq_own, wq_other, wk_own, wk_other, wv_own, wv_other)
    loads = [pltpu.make_async_copy(x_hbm, x_ref, sems.at[0])]
    for place, source in enumerate(sources):
        target = w_ref.at[:, place * half : place * half + half]
        loads.append(pltpu.make_async_copy(source, target, sems.at[1 + place]))
    table_load = pltpu.make_async_copy(table_hbm, table_other, sems.at[11])
    table_load.start()
    for load in loads:
        load.start()
    _, ends = row_plan(len_ref, own_ref[0])
    row = lax.broadcasted_iota(jnp.int32, dk_ref.shape, 0)
    dk_ref[...] = sum((row >= end).astype(jnp.int32) for end in ends)
    lane = lax.broadcasted_iota(jnp.int32, dq_ref.shape, 1)
    dq_ref[...] = sum((lane >= end).astype(jnp.int32) for end in ends)
    bias_bands(buckets_ref, table_own, bias_ref, 0)
    table_load.wait()
    bias_bands(buckets_ref, table_other, bias_ref, heads)
    loads[0].wait()
    inputs = x_ref[...].astype(f32)
    scale = lax.rsqrt(jnp.mean(inputs * inputs, axis=1, keepdims=True) + eps_norm)
    x_ref[...] = (inputs * scale * gain_ref[...].reshape(1, D)).astype(bf16)
    for load in loads[1:]:
        load.wait()
    q_ref, k_ref, v_ref = (qkv_ref.at[place] for place in range(3))

    def project(place, carry):
        columns = pl.ds(pl.multiple_of(place * D, D), D)
        projected = nn(x_ref[...], w_ref[:, columns])
        qkv_ref[place] = (projected * jnp.where(place == 0, log2_e, 1.0)).astype(bf16)
        return carry

    lax.fori_loop(0, 3, project, 0)
    vt_ref[...] = v_ref[...].T
    stores = [
        pltpu.make_async_copy(q_ref, q_hbm, sems.at[7]),
        pltpu.make_async_copy(k_ref, k_hbm, sems.at[8]),
        pltpu.make_async_copy(v_ref, v_hbm, sems.at[9]),
    ]
    for store in stores:
        store.start()

    def prob_copy(it, count):
        slot, rows = lax.rem(it, 2), count * KB
        return pltpu.make_async_copy(
            prob_ref.at[slot, :, 0:rows, :],
            prob_hbm.at[lax.div(it, NQ), :, lax.rem(it, NQ), 0:rows, :],
            prob_sems.at[slot],
        )

    def ctx_copy(it):
        query_rows = pl.ds(pl.multiple_of(lax.rem(it, NQ) * QB, QB), QB)
        band = pl.ds(pl.multiple_of(lax.div(it, NQ) * half, half), half)
        return pltpu.make_async_copy(
            ctx_ref.at[band, query_rows], ctx_hbm.at[band, query_rows], ctx_sems.at[it]
        )

    def with_span(it, action):
        first_row = lax.rem(it, NQ) * QB
        begin, wide = key_window(ends, first_row, first_row + QB - 1)
        pl.when(wide)(functools.partial(action, it, begin, SEQ // KB))
        pl.when(jnp.logical_not(wide))(functools.partial(action, it, begin, MOST // KB))

    def drain(it, begin, count):
        prob_copy(it, count).wait()

    def attend(it, begin, count):
        rows = count * KB
        slot, group = lax.rem(it, 2), lax.div(it, NQ)
        first_row, first_key = lax.rem(it, NQ) * QB, pl.multiple_of(begin * KB, KB)
        key_rows = pl.ds(first_key, rows)
        query_rows = pl.ds(pl.multiple_of(first_row, QB), QB)
        doc_key = jnp.concatenate([dk_ref[key_rows, :]] * (QB // 128), axis=1)
        same = doc_key == dq_ref[0:1, query_rows]

        bands = []
        for part in range(rows // 128):
            lane = jnp.clip(first_row - first_key + (REACH - part * 128), 0, SPREAD - QB)
            bands.append(pl.ds(pl.multiple_of(lane, 128), QB))

        def some_heads(members):
            scores, totals, probs = [], [], []
            for head in members:
                lanes = places(group * half + head // 2 * PAIR, PAIR)
                scores.append(nt(k_ref[key_rows, lanes], one_head(q_ref[query_rows, lanes], len(scores) % 2)))
            for head, score in zip(members, scores):
                bias = jnp.concatenate(
                    [bias_ref[group * heads + head, :, lanes] for lanes in bands], axis=0
                )
                score = jnp.where(same, score + bias, masked_score)
                expo = jnp.exp2(score - jnp.max(score, axis=0, keepdims=True))
                totals.append(1.0 / jnp.sum(expo, axis=0, keepdims=True))
                probs.append(expo.astype(bf16))
                prob_ref[slot, head, 0:rows, :] = probs[-1]
            for head, total, prob in zip(members, totals, probs):
                band = places(group * half + head * DH, DH)
                context = nn(vt_ref[band, key_rows], prob)
                ctx_ref[band, query_rows] = (context * total).astype(bf16)
                shrink_ref[places(group * 8 + head, 1), query_rows] = total

        if rows <= MOST:
            some_heads(range(heads))
        else:

            def one_pair(pair, carry):
                some_heads((2 * pair, 2 * pair + 1))
                return carry

            lax.fori_loop(0, heads // 2, one_pair, 0)
        prob_copy(it, count).start()
        ctx_copy(it).start()

    def one_block(it, carry):
        @pl.when(it >= 2)
        def _drain():
            with_span(it - 2, drain)

        with_span(it, attend)
        return carry

    lax.fori_loop(0, 2 * NQ, one_block, 0)
    stores.append(pltpu.make_async_copy(shrink_ref, shrink_hbm, sems.at[10]))
    stores[-1].start()
    with_span(jnp.int32(2 * NQ - 2), drain)
    with_span(jnp.int32(2 * NQ - 1), drain)
    for it in range(2 * NQ):
        ctx_copy(it).wait()
    for copy in stores:
        copy.wait()


def attention_forward(own, lengths, x, weights, gain, buckets, table_own, table_other):
    heads = table_own.shape[0]
    any_space = pl.BlockSpec(memory_space=pl.ANY)
    vmem = pl.BlockSpec(memory_space=pltpu.VMEM)
    smem = pl.BlockSpec(memory_space=pltpu.SMEM)
    return pl.pallas_call(
        attention_kernel,
        in_specs=[smem, smem] + [any_space] * 8 + [vmem] * 3,
        out_specs=[any_space] * 6,
        out_shape=[
            jax.ShapeDtypeStruct((2, heads, NQ, SEQ, QB), bf16),
            jax.ShapeDtypeStruct((SEQ, D), bf16),
            jax.ShapeDtypeStruct((SEQ, D), bf16),
            jax.ShapeDtypeStruct((SEQ, D), bf16),
            jax.ShapeDtypeStruct((D, SEQ), bf16),
            jax.ShapeDtypeStruct((16, SEQ), f32),
        ],
        scratch_shapes=[
            pltpu.VMEM((SEQ, D), bf16),
            pltpu.VMEM((D, 3 * D), bf16),
            pltpu.VMEM((3, SEQ, D), bf16),
            pltpu.VMEM((D, SEQ), bf16),
            pltpu.VMEM((D, SEQ), bf16),
            pltpu.VMEM((16, SEQ), f32),
            pltpu.VMEM(table_own.shape, f32),
            pltpu.VMEM((2 * heads, 128, SPREAD), f32),
            pltpu.VMEM((SEQ, 128), jnp.int32),
            pltpu.VMEM((8, SEQ), jnp.int32),
            pltpu.VMEM((2, heads, SEQ, QB), bf16),
            pltpu.SemaphoreType.DMA((2,)),
            pltpu.SemaphoreType.DMA((2 * NQ,)),
            pltpu.SemaphoreType.DMA((12,)),
        ],
        compiler_params=pltpu.CompilerParams(vmem_limit_bytes=VMEM_BYTES),
        cost_estimate=pl.CostEstimate(flops=25 * 10**9, bytes_accessed=30 * 10**6, transcendentals=4 * 10**6),
        name="attention_forward",
    )(own, lengths, x, *weights, table_other, gain, buckets, table_own)


root_two_over_pi = 0.7978845608028654
cubic = 0.044715


def gelu_both(value):
    square = value * value
    slow = jnp.tanh(value * (root_two_over_pi + (root_two_over_pi * cubic) * square))
    half = 0.5 * value
    act = half + half * slow
    slope = (0.5 + 0.5 * slow) + half * (1.0 - slow * slow) * (
        root_two_over_pi + (3.0 * root_two_over_pi * cubic) * square
    )
    return act, slope


def block_of(index, width, blocks):
    return sum((index >= width * place).astype(jnp.int32) for place in range(1, blocks))


class Kronecker:
    def __init__(self, core, small, large, factor, swapped):
        terms, rows = KRON, KRON * KRON
        sub, leaf = BOTTLE // KRON, D // KRON
        self.factor = factor
        row = lax.broadcasted_iota(jnp.int32, (rows, rows * KRON), 0)
        item = lax.broadcasted_iota(jnp.int32, (rows, rows * KRON), 1)
        item_of = lax.broadcasted_iota(jnp.int32, (rows * KRON, BOTTLE), 0)
        lane_block = block_of(lax.broadcasted_iota(jnp.int32, (rows * KRON, BOTTLE), 1), sub, KRON)
        if swapped:
            self.holds = ((item >> 4) == (row >> 2)) & ((item & 3) == (row & 3))
            pick = ((item_of >> 2) & 3) == lane_block
        else:
            self.holds = (item >> 2) == row
            pick = (item_of & 3) == lane_block
        self.pick = pick.astype(f32)
        self.core = exact(jnp.where(self.holds, jnp.broadcast_to(core, self.holds.shape), 0.0), self.pick)
        self.small = jnp.concatenate(
            [
                jnp.broadcast_to(
                    jnp.concatenate([small[:, n * sub : n * sub + sub]] * KRON, axis=1), (KRON, BOTTLE)
                )
                for n in range(terms)
            ],
            axis=0,
        )
        large = jnp.concatenate(
            [
                jnp.broadcast_to(
                    jnp.concatenate([large[:, n * leaf : n * leaf + leaf]] * KRON, axis=1), (KRON, D)
                )
                for n in range(terms)
            ],
            axis=0,
        )
        row = lax.broadcasted_iota(jnp.int32, (rows, D), 0)
        lane = lax.broadcasted_iota(jnp.int32, (rows, D), 1)
        self.diagonal = (row & 3) == block_of(lane, leaf, KRON)
        self.large = jnp.where(self.diagonal, large, 0.0)
        self.mix = self.core * self.small

    def matrix(self):
        return exact(self.mix.T, self.large) * self.factor

    def gradient(self, grad):
        sub, leaf = BOTTLE // KRON, D // KRON
        inner = self.factor * lax.dot_general(
            self.large, grad, (((1,), (1,)), ((), ())), preferred_element_type=f32
        )
        core = lax.dot_general(
            self.small * inner, self.pick, (((1,), (1,)), ((), ())), preferred_element_type=f32
        )
        core = jnp.sum(jnp.where(self.holds, core, 0.0), axis=0, keepdims=True)
        by_term = self.core * inner
        outer = self.factor * jnp.where(self.diagonal, nn(self.mix, grad), 0.0)
        small, large = [], []
        for n in range(KRON):
            row = jnp.sum(by_term[n * KRON : n * KRON + KRON, :], axis=0, keepdims=True)
            small.append(sum(row[:, b * sub : b * sub + sub] for b in range(KRON)))
            row = jnp.sum(outer[n * KRON : n * KRON + KRON, :], axis=0, keepdims=True)
            large.append(sum(row[:, a * leaf : a * leaf + leaf] for a in range(KRON)))
        return core, jnp.concatenate(small, axis=1), jnp.concatenate(large, axis=1)


def both_adapters(flat):
    widths = (KRON * KRON * KRON, D, BOTTLE, BOTTLE, D, BOTTLE, D)
    pieces, place = [], 0
    for width in widths:
        pieces.append(flat[:, place : place + width])
        place = place + width
    core, down_left, down_right, up_left, up_right, bias_down, bias_up = pieces
    down = Kronecker(core, down_right, down_left, (KRON * D) ** (-0.5), False)
    up = Kronecker(core, up_left, up_right, BOTTLE ** (-0.5), True)
    return down, up, bias_down, bias_up


def feed_forward_kernel(
    own_ref,
    len_ref,
    prob_hbm,
    q_hbm,
    k_hbm,
    v_hbm,
    ctx_hbm,
    shrink_hbm,
    x_hbm,
    grad_hbm,
    wo_own,
    wo_other,
    win_own,
    win_other,
    wout_own,
    wout_other,
    wq_own,
    wk_own,
    wv_own,
    wq_other,
    wk_other,
    wv_other,
    gain_attn_ref,
    gain_ffn_ref,
    flat_ref,
    out_hbm,
    grad_in_hbm,
    flat_grad_ref,
    ctx_ref,
    x_ref,
    grad_ref,
    wo_ref,
    win_ref,
    wout_ref,
    slope_ref,
    res_ref,
    res_grad_ref,
    delta_ref,
    shrink_ref,
    dqt_ref,
    sums_ref,
    low_ref,
    prob_ref,
    prob_sems,
    sems,
):
    start, ends = row_plan(len_ref, own_ref[0])
    half = wo_own.shape[0]
    hidden = win_own.shape[1]
    heads = half // DH
    chunks = 2 * hidden // FCHUNK

    def load(source, target, place):
        return pltpu.make_async_copy(source, target, sems.at[place])

    first = [
        load(ctx_hbm, ctx_ref, 0),
        load(wo_own, wo_ref.at[0:half, :], 1),
        load(wo_other, wo_ref.at[half : 2 * half, :], 2),
        load(x_hbm, x_ref, 3),
    ]
    ffn_loads = [
        load(win_own, win_ref.at[:, 0:hidden], 4),
        load(wout_own, wout_ref.at[0:hidden, :], 5),
        load(win_other, win_ref.at[:, hidden : 2 * hidden], 6),
        load(wout_other, wout_ref.at[hidden : 2 * hidden, :], 7),
    ]
    base = 10
    grad_load = load(grad_hbm, grad_ref, base)
    v_ref, k_ref, q_ref = (wout_ref.at[place * SEQ : place * SEQ + SEQ, :] for place in range(3))
    late = [
        load(v_hbm, v_ref, base + 1),
        load(k_hbm, k_ref, base + 3),
        load(q_hbm, q_ref, base + 2),
    ]
    shrink_load = load(shrink_hbm, shrink_ref, base + 4)
    out_copy = load(res_grad_ref, out_hbm, base + 5)
    out_pieces = [
        load(
            res_ref.at[piece * QB : piece * QB + QB, :], grad_in_hbm.at[piece * QB : piece * QB + QB, :], piece
        )
        for piece in range(NQ)
    ]
    qkv_loads = [
        load(source, win_ref.at[:, place * half : place * half + half], 4 + place)
        for place, source in enumerate((wq_own, wq_other, wk_own, wk_other, wv_own, wv_other))
    ]
    for copy in first:
        copy.start()
    for copy in ffn_loads:
        copy.start()
    grad_load.start()
    shrink_load.start()

    def prob_copy(it, count):
        slot, rows = lax.rem(it, 2), count * KB
        return pltpu.make_async_copy(
            prob_hbm.at[lax.div(it, NQ), :, lax.rem(it, NQ), 0:rows, :],
            prob_ref.at[slot, :, 0:rows, :],
            prob_sems.at[slot],
        )

    def with_span(it, action):
        first_row = lax.rem(it, NQ) * QB
        _, wide = key_window(ends, first_row, first_row + QB - 1)
        pl.when(wide)(functools.partial(action, it, SEQ // KB))
        pl.when(jnp.logical_not(wide))(functools.partial(action, it, MOST // KB))

    def fetch(it, count):
        prob_copy(it, count).start()

    def arrive(it, count):
        prob_copy(it, count).wait()

    with_span(jnp.int32(0), fetch)
    flat = flat_ref[...].reshape(1, flat_ref.shape[0])
    down_maker, up_maker, bias_down, bias_up = both_adapters(flat)
    down, up = down_maker.matrix().astype(bf16), up_maker.matrix().astype(bf16)
    gain = gain_ffn_ref[...].reshape(1, D)
    for copy in first:
        copy.wait()
    residual = x_ref[...].astype(f32) + tn(ctx_ref[...], wo_ref[...])
    res_ref[...] = residual
    scale = lax.rsqrt(jnp.mean(residual * residual, axis=1, keepdims=True) + eps_norm)
    low = (residual * scale * gain).astype(bf16)

    for copy in ffn_loads[:2]:
        copy.wait()
    low_ref[...] = low
    sums_ref[...] = jnp.zeros_like(sums_ref)

    def halves_of(chunk):
        return [places(chunk * FCHUNK + part * (FCHUNK // 2), FCHUNK // 2) for part in range(2)]

    def forward_chunk(chunk, carry):
        @pl.when(chunk == hidden // FCHUNK)
        def _other_side():
            for copy in ffn_loads[2:]:
                copy.wait()

        halves = halves_of(chunk)
        pre_acts = [nn(low_ref[...], win_ref[:, cols]) for cols in halves]
        for pre_act, cols in zip(pre_acts, halves):
            act, slope = gelu_both(pre_act)
            slope_ref[:, cols] = slope.astype(bf16)
            sums_ref[...] += nn(act.astype(bf16), wout_ref[cols, :])
        return carry

    lax.fori_loop(0, chunks, forward_chunk, 0)
    mixed = sums_ref[...]
    grad_load.wait()
    out_grad_low = grad_ref[...]
    mixed_low = mixed.astype(bf16)
    bottle, bottle_slope = gelu_both(nt(mixed_low, down) + bias_down)
    bottle_low = bottle.astype(bf16)
    sums_ref[...] = res_ref[...] + mixed + nn(bottle_low, up) + bias_up
    rotate_rows(sums_ref, res_grad_ref, SEQ - start)
    out_copy.start()
    bottle_grad = (nt(out_grad_low, up) * bottle_slope).astype(bf16)
    mixed_grad = (out_grad_low.astype(f32) + nn(bottle_grad, down)).astype(bf16)
    up_grad = tn(bottle_low, out_grad_low)
    down_grad = tn(bottle_grad, mixed_low)
    core_down, right_down, left_down = down_maker.gradient(down_grad)
    core_up, left_up, right_up = up_maker.gradient(up_grad)
    flat_grad = jnp.concatenate(
        [
            core_down + core_up,
            left_down,
            right_down,
            left_up,
            right_up,
            jnp.sum(bottle_grad.astype(f32), axis=0, keepdims=True),
            jnp.sum(out_grad_low.astype(f32), axis=0, keepdims=True),
        ],
        axis=1,
    )
    flat_grad_ref[...] = flat_grad.reshape(flat_grad_ref.shape[0])
    low_ref[...] = mixed_grad
    sums_ref[...] = jnp.zeros_like(sums_ref)

    def backward_chunk(chunk, carry):
        halves = halves_of(chunk)
        hidden_grads = [nt(low_ref[...], wout_ref[cols, :]) for cols in halves]
        for hidden_grad, cols in zip(hidden_grads, halves):
            pre_grad = (hidden_grad * slope_ref[:, cols].astype(f32)).astype(bf16)
            sums_ref[...] += nt(pre_grad, win_ref[:, cols])
        return carry

    lax.fori_loop(0, chunks, backward_chunk, 0)
    for copy in late + qkv_loads:
        copy.start()
    residual = res_ref[...]
    weighted = sums_ref[...] * gain
    inner = jnp.mean(residual * weighted, axis=1, keepdims=True)
    res_grad = grad_ref[...].astype(f32) + scale * weighted - residual * (scale * scale * scale * inner)
    out_copy.wait()
    res_grad_ref[...] = res_grad
    shrink_load.wait()
    shrink = jnp.concatenate([shrink_ref[0:heads, :], shrink_ref[8 : 8 + heads, :]], axis=0)
    shrink_top = shrink.astype(bf16)
    shrink_rest = (shrink - shrink_top.astype(f32)).astype(bf16)
    head_row = lax.broadcasted_iota(jnp.int32, (2 * heads, D), 0)
    head_lane = lax.broadcasted_iota(jnp.int32, (2 * heads, D), 1) >> 6
    spread = (head_row == head_lane).astype(bf16)
    shrink_wide = tn(shrink_top, spread) + tn(shrink_rest, spread)
    dctx = (nt(res_grad.astype(bf16), wo_ref[...]) * shrink_wide).astype(bf16)
    grad_ref[...] = dctx
    product = dctx.T.astype(f32) * ctx_ref[...].astype(f32)
    delta_ref[0 : 2 * heads, :] = jnp.sum(product.reshape(2 * heads, DH, SEQ), axis=1)
    for copy in late:
        copy.wait()
    kt_ref, dctx_ref = ctx_ref, grad_ref
    kt_ref[...] = k_ref[...].T

    def attend(it, part, carry):
        slot, group = lax.rem(it, 2), lax.div(it, NQ)
        first_row = lax.rem(it, NQ) * QB
        begin, _ = key_window(ends, first_row, first_row + QB - 1)
        key_rows = pl.ds(pl.multiple_of(begin * KB + part * MOST, KB), MOST)
        rows = pl.ds(pl.multiple_of(part * MOST, MOST), MOST)
        query_rows = pl.ds(pl.multiple_of(first_row, QB), QB)

        def lanes(pair):
            return places(group * half + pair * PAIR, PAIR)

        grads, prob_grads, score_grads, probs = [], [], [], []
        for head in range(heads):
            grads.append(one_head(dctx_ref[query_rows, lanes(head // 2)], head % 2))
            prob_grads.append(nt(v_ref[key_rows, lanes(head // 2)], grads[head]))
        for head in range(heads):
            delta = delta_ref[places(group * heads + head, 1), query_rows]
            probs.append(prob_ref[slot, head, rows, :])
            score_grads.append((probs[head].astype(f32) * (prob_grads[head] - delta)).astype(bf16))
        for pair in range(heads // 2):
            dk = dv = None
            for head in (2 * pair, 2 * pair + 1):
                band = places(group * half + head * DH, DH)
                queries = one_head(q_ref[query_rows, lanes(pair)], head % 2)
                dv_part = nn(probs[head], grads[head])
                dk_part = nn(score_grads[head], queries)
                dv = dv_part if dv is None else dv + dv_part
                dk = dk_part if dk is None else dk + dk_part
                dq = nn(kt_ref[band, key_rows], score_grads[head])
                before = jnp.where(part > 0, dqt_ref[band, query_rows].astype(f32), 0.0)
                dqt_ref[band, query_rows] = (before + dq).astype(bf16)
            sums_ref[key_rows, pair * PAIR : pair * PAIR + PAIR] += dk
            sums_ref[key_rows, half + pair * PAIR : half + pair * PAIR + PAIR] += dv
        return carry

    def one_block(it, carry):
        @pl.when(it + 1 < 2 * NQ)
        def _ahead():
            with_span(it + 1, fetch)

        with_span(it, arrive)
        first_row = lax.rem(it, NQ) * QB
        _, wide = key_window(ends, first_row, first_row + QB - 1)
        lax.fori_loop(0, jnp.where(wide, SEQ // MOST, 1), functools.partial(attend, it), 0)
        return carry

    def one_group(group, carry):
        sums_ref[...] = jnp.zeros_like(sums_ref)
        lax.fori_loop(group * NQ, group * NQ + NQ, one_block, 0)
        slope_ref[:, places((2 + group) * half, half)] = (sums_ref[:, 0:half] * (1.0 / log2_e)).astype(bf16)
        slope_ref[:, places((4 + group) * half, half)] = sums_ref[:, half : 2 * half].astype(bf16)
        return carry

    lax.fori_loop(0, 2, one_group, 0)
    slope_ref[:, 0 : 2 * half] = dqt_ref[...].T
    for copy in qkv_loads:
        copy.wait()

    def input_columns(part, carry):
        rows = pl.ds(pl.multiple_of(part * KB, KB), KB)
        sums_ref[:, rows] = nt(slope_ref[:, 0 : 6 * half], win_ref[rows, 0 : 6 * half])
        return carry

    lax.fori_loop(0, D // KB, input_columns, 0)
    normed_grad = sums_ref[...]
    inputs = x_ref[...].astype(f32)
    scale = lax.rsqrt(jnp.mean(inputs * inputs, axis=1, keepdims=True) + eps_norm)
    weighted = normed_grad * gain_attn_ref[...].reshape(1, D)
    inner = jnp.mean(inputs * weighted, axis=1, keepdims=True)
    sums_ref[...] = res_grad_ref[...] + scale * weighted - inputs * (scale * scale * scale * inner)
    rotate_pieces(sums_ref, res_ref, SEQ - start, NQ, lambda piece: out_pieces[piece].start())
    for copy in out_pieces:
        copy.wait()


def feed_forward_and_back(own, lengths, kept, x, out_grad, frozen, weights, gain_attn, gain_ffn, flat):
    any_space = pl.BlockSpec(memory_space=pl.ANY)
    vmem = pl.BlockSpec(memory_space=pltpu.VMEM)
    smem = pl.BlockSpec(memory_space=pltpu.SMEM)
    hidden = 2 * frozen[2].shape[1]
    heads = kept[0].shape[1]
    half = heads * DH
    return pl.pallas_call(
        feed_forward_kernel,
        in_specs=[smem, smem] + [any_space] * 20 + [vmem] * 3,
        out_specs=[any_space, any_space, vmem],
        out_shape=[
            jax.ShapeDtypeStruct((SEQ, D), f32),
            jax.ShapeDtypeStruct((SEQ, D), f32),
            jax.ShapeDtypeStruct(flat.shape, f32),
        ],
        scratch_shapes=[
            pltpu.VMEM((D, SEQ), bf16),
            pltpu.VMEM((SEQ, D), bf16),
            pltpu.VMEM((SEQ, D), bf16),
            pltpu.VMEM((D, D), bf16),
            pltpu.VMEM((D, hidden), bf16),
            pltpu.VMEM((hidden, D), bf16),
            pltpu.VMEM((SEQ, hidden), bf16),
            pltpu.VMEM((SEQ, D), f32),
            pltpu.VMEM((SEQ, D), f32),
            pltpu.VMEM((16, SEQ), f32),
            pltpu.VMEM((16, SEQ), f32),
            pltpu.VMEM((D, SEQ), bf16),
            pltpu.VMEM((SEQ, D), f32),
            pltpu.VMEM((SEQ, D), bf16),
            pltpu.VMEM((2, heads, SEQ, QB), bf16),
            pltpu.SemaphoreType.DMA((2,)),
            pltpu.SemaphoreType.DMA((17,)),
        ],
        compiler_params=pltpu.CompilerParams(vmem_limit_bytes=VMEM_BYTES),
        cost_estimate=pl.CostEstimate(flops=60 * 10**9, bytes_accessed=40 * 10**6, transcendentals=4 * 10**6),
        name="feed_forward_and_back",
    )(own, lengths, *kept, x, out_grad, *frozen, *weights, gain_attn, gain_ffn, flat)


def sum_everywhere(value):
    for axis in ("head", "dp"):
        size = lax.axis_size(axis)
        step = 1
        while step < size:
            value = value + lax.ppermute(value, axis, [(place, place ^ step) for place in range(size)])
            step = 2 * step
    return value


def on_device(
    hidden_in,
    lengths,
    buckets,
    gain_attn,
    gain_ffn,
    w_query,
    w_key,
    w_value,
    w_attn_out,
    w_in,
    w_ffn_out,
    rel_bias,
    out_grad,
    adapter_weights,
    first_moment,
    second_moment,
    ema_weights,
):
    swap = [(0, 1), (1, 0)]
    own = lax.axis_index("head").astype(jnp.int32).reshape(1)

    def other(value):
        return lax.ppermute(value, "head", swap)

    table = rel_bias.T
    own_qkv = (w_query, w_key, w_value)
    other_qkv = tuple(other(weight) for weight in own_qkv)
    other_table = other(table)
    rest = (w_attn_out, w_in, w_ffn_out)
    frozen = tuple(piece for weight in rest for piece in (weight, other(weight)))
    packed, packed_grad = pack(own, lengths, hidden_in, out_grad)
    kept = attention_forward(
        own, lengths, packed, own_qkv + other_qkv, gain_attn, buckets, table, other_table
    )
    layer_out, grad_in, local_grad = feed_forward_and_back(
        own, lengths, kept, packed, packed_grad, frozen, own_qkv + other_qkv, gain_attn, gain_ffn, adapter_weights
    )
    total_grad = sum_everywhere(local_grad)
    new_first = beta_one * first_moment + (1.0 - beta_one) * total_grad
    new_second = beta_two * second_moment + (1.0 - beta_two) * total_grad * total_grad
    first_hat = new_first / (1.0 - beta_one**STEP)
    second_hat = new_second / (1.0 - beta_two**STEP)
    new_weights = adapter_weights - learn_rate * (
        first_hat / (jnp.sqrt(second_hat) + adam_eps) + weight_decay * adapter_weights
    )
    new_ema = ema_decay * ema_weights + (1.0 - ema_decay) * new_weights
    return (layer_out, grad_in, new_weights, new_first, new_second, new_ema)


def solution(mesh):
    placed = (
        P("dp", None),
        P("dp", None),
        P(),
        P(),
        P(),
        P(None, "head"),
        P(None, "head"),
        P(None, "head"),
        P("head", None),
        P(None, "head"),
        P("head", None),
        P(None, "head"),
        P(("dp", "head"), None),
        P(),
        P(),
        P(),
        P(),
    )
    return jax.shard_map(
        on_device,
        mesh=mesh,
        in_specs=placed,
        out_specs=(P(("dp", "head"), None), P(("dp", "head"), None), P(), P(), P(), P()),
        check_vma=False,
    )
```

```python
import functools

import jax
import jax.numpy as jnp
from jax import lax
from jax.experimental import pallas as pl
from jax.experimental.pallas import tpu as pltpu
from jax.sharding import PartitionSpec as P

D = 768
DH = 64
KRON = 4
BOTTLE = 48
SEQ = 1024
MOST = 512
STEP = 10
QB = 256
KB = 256
NQ = SEQ // QB
PAIR = 2 * DH
FCHUNK = 1024
REACH = QB + MOST - 128
SPREAD = REACH + MOST + QB
CODES = SPREAD + 128
VMEM_BYTES = 127 * 2**19

eps_norm = 1e-06
beta_one = 0.9
beta_two = 0.999
adam_eps = 1e-08
learn_rate = 0.6
weight_decay = 0.01
ema_decay = 0.9
masked_score = -1e30
log2_e = 1.4426950408889634
highest = lax.Precision.HIGHEST
f32 = jnp.float32
bf16 = jnp.bfloat16


def nn(left, right):
    return lax.dot_general(left, right, (((1,), (0,)), ((), ())), preferred_element_type=f32)


def nt(left, right):
    return lax.dot_general(left, right, (((1,), (1,)), ((), ())), preferred_element_type=f32)


def tn(left, right):
    return lax.dot_general(left, right, (((0,), (0,)), ((), ())), preferred_element_type=f32)


def row_plan(len_ref, own):
    docs = len_ref.shape[1]
    sizes = [len_ref[own, doc] for doc in range(docs)]
    longest, chosen = sizes[0], jnp.int32(0)
    for doc in range(1, docs):
        longer = sizes[doc] > longest
        chosen = jnp.where(longer, doc, chosen)
        longest = jnp.maximum(longest, sizes[doc])
    start = jnp.int32(0)
    for doc in range(docs):
        start = start + jnp.where(doc < chosen, sizes[doc], 0)
    ends, total = [], jnp.int32(0)
    for doc in range(docs):
        total = total + len_ref[own, lax.rem(chosen + doc, docs)]
        ends.append(total)
    return start, ends


def key_span(ends, first_row, last_row):
    begin, finish = jnp.int32(0), jnp.int32(SEQ)
    for end in ends:
        begin = jnp.where(end <= first_row, end, begin)
    for end in reversed(ends):
        finish = jnp.where(end > last_row, end, finish)
    return lax.div(begin, KB), lax.div(finish + (KB - 1), KB)


def rotate_rows(source_ref, target_ref, shift):
    groups = SEQ // 8
    fine, coarse = shift & 7, shift >> 3
    back = (8 - fine) & 7
    keep = lax.broadcasted_iota(jnp.int32, (8, target_ref.shape[1]), 0) < 8 - fine

    def turned(group):
        rows = source_ref[pl.ds(pl.multiple_of((group & (groups - 1)) * 8, 16), 16), :].astype(f32)
        return pltpu.roll(rows[0:8], back, 0), pltpu.roll(rows[8:16], back, 0)

    def some(part, carry):
        first, second = carry
        for pair in range(4):
            group = part * 8 + pair * 2
            third, fourth = turned(group + 2)
            for place, left, right in ((0, first, second), (1, second, third)):
                to = ((group + place - coarse) & (groups - 1)) * 8
                target_ref[pl.ds(pl.multiple_of(to, 8), 8), :] = jnp.where(keep, left, right)
            first, second = third, fourth
        return first, second

    lax.fori_loop(0, groups // 8, some, turned(jnp.int32(0)))


def rotate_pieces(source_ref, target_ref, shift, pieces, ready):
    groups = SEQ // 8
    fine, coarse = shift & 7, shift >> 3
    back = (8 - fine) & 7
    keep = lax.broadcasted_iota(jnp.int32, (8, target_ref.shape[1]), 0) < 8 - fine

    def turned(group):
        rows = source_ref[pl.ds(pl.multiple_of(((group + coarse) & (groups - 1)) * 8, 8), 8), :]
        return pltpu.roll(rows, back, 0)

    def some(part, before):
        for place in range(8):
            group = part * 8 + place
            after = turned(group + 1)
            target_ref[pl.ds(pl.multiple_of(group * 8, 8), 8), :] = jnp.where(keep, before, after)
            before = after
        return before

    steps = groups // 8 // pieces
    carry = turned(jnp.int32(0))
    for piece in range(pieces):
        carry = lax.fori_loop(piece * steps, piece * steps + steps, some, carry)
        ready(piece)


def one_head(pair, half):
    lane = lax.broadcasted_iota(jnp.int32, pair.shape, 1)
    keep = lane < DH if half == 0 else lane >= DH
    return jnp.where(keep, pair, jnp.zeros_like(pair))


def flip_lanes(value):
    tiles = value.shape[1] // 128
    row = lax.broadcasted_iota(jnp.int32, (128, 128), 0)
    lane = lax.broadcasted_iota(jnp.int32, (128, 128), 1)
    stacked = jnp.concatenate([value[:, tile * 128 : tile * 128 + 128] for tile in range(tiles)], axis=0)
    flipped = exact(stacked, (row + lane == 127).astype(f32))
    return jnp.concatenate([flipped[tile * 8 : tile * 8 + 8, :] for tile in reversed(range(tiles))], axis=1)


def exact(left, right):
    return lax.dot_general(
        left, right, (((1,), (0,)), ((), ())), precision=highest, preferred_element_type=f32
    )


def bias_rows(buckets_ref, table_ref, rows_ref, lead):
    heads = table_ref.shape[0]
    top = REACH + 128 + SEQ - 1
    codes = buckets_ref[...].reshape(1, 2 * SEQ - 1)[:, top - CODES + 1 : top + 1]
    bucket = lax.broadcasted_iota(jnp.int32, (table_ref.shape[1], CODES), 0)
    per_head = exact(table_ref[...] * log2_e, (bucket == codes).astype(f32))
    per_head = flip_lanes(jnp.concatenate([per_head, jnp.zeros((8 - heads, CODES), f32)], axis=0))
    rows_ref[lead : lead + heads, :] = per_head[0:heads, :]


def bias_band(rows_ref, bias_ref, head):
    spread = jnp.broadcast_to(rows_ref[pl.ds(head, 1), :], (128, CODES))
    spread = pltpu.roll(spread, CODES - 128, 1, stride=1, stride_axis=0)
    bias_ref[head] = spread[:, :SPREAD]


def places(first, width):
    return pl.ds(pl.multiple_of(first, width), width)


def key_window(ends, first_row, last_row):
    begin, finish = key_span(ends, first_row, last_row)
    wide = finish - begin > MOST // KB
    return jnp.where(wide, 0, jnp.minimum(begin, (SEQ - MOST) // KB)), wide


def pack_kernel(own_ref, len_ref, x_hbm, grad_hbm, packed_hbm, packed_grad_hbm, x_ref, grad_ref, turned_ref, sems):
    start, _ = row_plan(len_ref, own_ref[0])
    rows = pl.ds(pl.multiple_of(own_ref[0] * SEQ, SEQ), SEQ)
    loads = [
        pltpu.make_async_copy(x_hbm.at[rows, :], x_ref, sems.at[0]),
        pltpu.make_async_copy(grad_hbm, grad_ref, sems.at[1]),
    ]
    stores = [
        pltpu.make_async_copy(x_ref, packed_hbm, sems.at[2]),
        pltpu.make_async_copy(grad_ref, packed_grad_hbm, sems.at[3]),
    ]
    for load in loads:
        load.start()
    for load, store, ref in zip(loads, stores, (x_ref, grad_ref)):
        load.wait()
        rotate_rows(ref, turned_ref, start)
        ref[...] = turned_ref[...].astype(bf16)
        store.start()
    for store in stores:
        store.wait()


def pack(own, lengths, x, out_grad):
    any_space = pl.BlockSpec(memory_space=pl.ANY)
    smem = pl.BlockSpec(memory_space=pltpu.SMEM)
    return pl.pallas_call(
        pack_kernel,
        in_specs=[smem, smem, any_space, any_space],
        out_specs=[any_space, any_space],
        out_shape=[jax.ShapeDtypeStruct((SEQ, D), bf16)] * 2,
        scratch_shapes=[
            pltpu.VMEM((SEQ, D), bf16),
            pltpu.VMEM((SEQ, D), bf16),
            pltpu.VMEM((SEQ, D), f32),
            pltpu.SemaphoreType.DMA((4,)),
        ],
        compiler_params=pltpu.CompilerParams(vmem_limit_bytes=VMEM_BYTES),
        cost_estimate=pl.CostEstimate(flops=3 * 10**9, bytes_accessed=6 * 10**6, transcendentals=0),
        name="pack_rows",
    )(own, lengths, x, out_grad)


def attention_kernel(
    own_ref,
    len_ref,
    x_hbm,
    wq_own,
    wk_own,
    wv_own,
    wq_other,
    wk_other,
    wv_other,
    table_hbm,
    gain_ref,
    buckets_ref,
    table_own,
    prob_hbm,
    q_hbm,
    k_hbm,
    v_hbm,
    ctx_hbm,
    shrink_hbm,
    x_ref,
    w_ref,
    qkv_ref,
    vt_ref,
    ctx_ref,
    shrink_ref,
    table_other,
    rows_ref,
    bias_ref,
    dk_ref,
    dq_ref,
    prob_ref,
    prob_sems,
    ctx_sems,
    sems,
):
    heads = table_own.shape[0]
    half = heads * DH
    sources = (wq_own, wq_other, wk_own, wk_other, wv_own, wv_other)
    loads = [pltpu.make_async_copy(x_hbm, x_ref, sems.at[0])]
    for place, source in enumerate(sources):
        target = w_ref.at[:, place * half : place * half + half]
        loads.append(pltpu.make_async_copy(source, target, sems.at[1 + place]))
    table_load = pltpu.make_async_copy(table_hbm, table_other, sems.at[11])
    table_load.start()
    for load in loads:
        load.start()
    _, ends = row_plan(len_ref, own_ref[0])
    row = lax.broadcasted_iota(jnp.int32, dk_ref.shape, 0)
    dk_ref[...] = sum((row >= end).astype(jnp.int32) for end in ends)
    lane = lax.broadcasted_iota(jnp.int32, dq_ref.shape, 1)
    dq_ref[...] = sum((lane >= end).astype(jnp.int32) for end in ends)
    bias_rows(buckets_ref, table_own, rows_ref, 0)
    table_load.wait()
    bias_rows(buckets_ref, table_other, rows_ref, heads)
    loads[0].wait()
    inputs = x_ref[...].astype(f32)
    scale = lax.rsqrt(jnp.mean(inputs * inputs, axis=1, keepdims=True) + eps_norm)
    x_ref[...] = (inputs * scale * gain_ref[...].reshape(1, D)).astype(bf16)
    q_ref, k_ref, v_ref = (qkv_ref.at[place] for place in range(3))

    def project(place, carry):
        for part in range(3):

            @pl.when(place == part)
            def _arrive():
                loads[1 + 2 * part].wait()
                loads[2 + 2 * part].wait()

        columns = pl.ds(pl.multiple_of(place * D, D), D)
        projected = nn(x_ref[...], w_ref[:, columns])
        for head in range(2 * heads // 3):
            bias_band(rows_ref, bias_ref, place * (2 * heads // 3) + head)
        qkv_ref[place] = (projected * jnp.where(place == 0, log2_e, 1.0)).astype(bf16)
        return carry

    lax.fori_loop(0, 3, project, 0)
    vt_ref[...] = v_ref[...].T
    stores = [
        pltpu.make_async_copy(q_ref, q_hbm, sems.at[7]),
        pltpu.make_async_copy(k_ref, k_hbm, sems.at[8]),
        pltpu.make_async_copy(v_ref, v_hbm, sems.at[9]),
    ]
    for store in stores:
        store.start()

    def prob_copy(it, count):
        slot, rows = lax.rem(it, 2), count * KB
        return pltpu.make_async_copy(
            prob_ref.at[slot, :, 0:rows, :],
            prob_hbm.at[lax.div(it, NQ), :, lax.rem(it, NQ), 0:rows, :],
            prob_sems.at[slot],
        )

    def ctx_copy(it):
        query_rows = pl.ds(pl.multiple_of(lax.rem(it, NQ) * QB, QB), QB)
        band = pl.ds(pl.multiple_of(lax.div(it, NQ) * half, half), half)
        return pltpu.make_async_copy(
            ctx_ref.at[band, query_rows], ctx_hbm.at[band, query_rows], ctx_sems.at[it]
        )

    def with_span(it, action):
        first_row = lax.rem(it, NQ) * QB
        begin, wide = key_window(ends, first_row, first_row + QB - 1)
        pl.when(wide)(functools.partial(action, it, begin, SEQ // KB))
        pl.when(jnp.logical_not(wide))(functools.partial(action, it, begin, MOST // KB))

    def drain(it, begin, count):
        prob_copy(it, count).wait()

    def attend(it, begin, count):
        rows = count * KB
        slot, group = lax.rem(it, 2), lax.div(it, NQ)
        first_row, first_key = lax.rem(it, NQ) * QB, pl.multiple_of(begin * KB, KB)
        key_rows = pl.ds(first_key, rows)
        query_rows = pl.ds(pl.multiple_of(first_row, QB), QB)
        doc_key = jnp.concatenate([dk_ref[key_rows, :]] * (QB // 128), axis=1)
        same = doc_key == dq_ref[0:1, query_rows]

        bands = []
        for part in range(rows // 128):
            lane = jnp.clip(first_row - first_key + (REACH - part * 128), 0, SPREAD - QB)
            bands.append(pl.ds(pl.multiple_of(lane, 128), QB))

        def some_heads(members):
            scores, totals, probs = [], [], []
            for head in members:
                lanes = places(group * half + head // 2 * PAIR, PAIR)
                scores.append(nt(k_ref[key_rows, lanes], one_head(q_ref[query_rows, lanes], len(scores) % 2)))
            for head, score in zip(members, scores):
                bias = jnp.concatenate(
                    [bias_ref[group * heads + head, :, lanes] for lanes in bands], axis=0
                )
                score = jnp.where(same, score + bias, masked_score)
                expo = jnp.exp2(score - jnp.max(score, axis=0, keepdims=True))
                totals.append(1.0 / jnp.sum(expo, axis=0, keepdims=True))
                probs.append(expo.astype(bf16))
                prob_ref[slot, head, 0:rows, :] = probs[-1]
            for head, total, prob in zip(members, totals, probs):
                band = places(group * half + head * DH, DH)
                context = nn(vt_ref[band, key_rows], prob)
                ctx_ref[band, query_rows] = (context * total).astype(bf16)
                shrink_ref[places(group * 8 + head, 1), query_rows] = total

        if rows <= MOST:
            some_heads(range(heads))
        else:

            def one_pair(pair, carry):
                some_heads((2 * pair, 2 * pair + 1))
                return carry

            lax.fori_loop(0, heads // 2, one_pair, 0)
        prob_copy(it, count).start()
        ctx_copy(it).start()

    def one_block(it, carry):
        @pl.when(it >= 2)
        def _drain():
            with_span(it - 2, drain)

        with_span(it, attend)
        return carry

    lax.fori_loop(0, 2 * NQ, one_block, 0)
    stores.append(pltpu.make_async_copy(shrink_ref, shrink_hbm, sems.at[10]))
    stores[-1].start()
    with_span(jnp.int32(2 * NQ - 2), drain)
    with_span(jnp.int32(2 * NQ - 1), drain)
    for it in range(2 * NQ):
        ctx_copy(it).wait()
    for copy in stores:
        copy.wait()


def attention_forward(own, lengths, x, weights, gain, buckets, table_own, table_other):
    heads = table_own.shape[0]
    any_space = pl.BlockSpec(memory_space=pl.ANY)
    vmem = pl.BlockSpec(memory_space=pltpu.VMEM)
    smem = pl.BlockSpec(memory_space=pltpu.SMEM)
    return pl.pallas_call(
        attention_kernel,
        in_specs=[smem, smem] + [any_space] * 8 + [vmem] * 3,
        out_specs=[any_space] * 6,
        out_shape=[
            jax.ShapeDtypeStruct((2, heads, NQ, SEQ, QB), bf16),
            jax.ShapeDtypeStruct((SEQ, D), bf16),
            jax.ShapeDtypeStruct((SEQ, D), bf16),
            jax.ShapeDtypeStruct((SEQ, D), bf16),
            jax.ShapeDtypeStruct((D, SEQ), bf16),
            jax.ShapeDtypeStruct((16, SEQ), f32),
        ],
        scratch_shapes=[
            pltpu.VMEM((SEQ, D), bf16),
            pltpu.VMEM((D, 3 * D), bf16),
            pltpu.VMEM((3, SEQ, D), bf16),
            pltpu.VMEM((D, SEQ), bf16),
            pltpu.VMEM((D, SEQ), bf16),
            pltpu.VMEM((16, SEQ), f32),
            pltpu.VMEM(table_own.shape, f32),
            pltpu.VMEM((16, CODES), f32),
            pltpu.VMEM((2 * heads, 128, SPREAD), f32),
            pltpu.VMEM((SEQ, 128), jnp.int32),
            pltpu.VMEM((8, SEQ), jnp.int32),
            pltpu.VMEM((2, heads, SEQ, QB), bf16),
            pltpu.SemaphoreType.DMA((2,)),
            pltpu.SemaphoreType.DMA((2 * NQ,)),
            pltpu.SemaphoreType.DMA((12,)),
        ],
        compiler_params=pltpu.CompilerParams(vmem_limit_bytes=VMEM_BYTES),
        cost_estimate=pl.CostEstimate(flops=25 * 10**9, bytes_accessed=30 * 10**6, transcendentals=4 * 10**6),
        name="attention_forward",
    )(own, lengths, x, *weights, table_other, gain, buckets, table_own)


root_two_over_pi = 0.7978845608028654
cubic = 0.044715


def gelu_both(value):
    square = value * value
    slow = jnp.tanh(value * (root_two_over_pi + (root_two_over_pi * cubic) * square))
    half = 0.5 * value
    act = half + half * slow
    slope = (0.5 + 0.5 * slow) + half * (1.0 - slow * slow) * (
        root_two_over_pi + (3.0 * root_two_over_pi * cubic) * square
    )
    return act, slope


def block_of(index, width, blocks):
    return sum((index >= width * place).astype(jnp.int32) for place in range(1, blocks))


class Kronecker:
    def __init__(self, core, small, large, factor, swapped):
        terms, rows = KRON, KRON * KRON
        sub, leaf = BOTTLE // KRON, D // KRON
        self.factor = factor
        row = lax.broadcasted_iota(jnp.int32, (rows, rows * KRON), 0)
        item = lax.broadcasted_iota(jnp.int32, (rows, rows * KRON), 1)
        item_of = lax.broadcasted_iota(jnp.int32, (rows * KRON, BOTTLE), 0)
        lane_block = block_of(lax.broadcasted_iota(jnp.int32, (rows * KRON, BOTTLE), 1), sub, KRON)
        if swapped:
            self.holds = ((item >> 4) == (row >> 2)) & ((item & 3) == (row & 3))
            pick = ((item_of >> 2) & 3) == lane_block
        else:
            self.holds = (item >> 2) == row
            pick = (item_of & 3) == lane_block
        self.pick = pick.astype(f32)
        self.core = exact(jnp.where(self.holds, jnp.broadcast_to(core, self.holds.shape), 0.0), self.pick)
        self.small = jnp.concatenate(
            [
                jnp.broadcast_to(
                    jnp.concatenate([small[:, n * sub : n * sub + sub]] * KRON, axis=1), (KRON, BOTTLE)
                )
                for n in range(terms)
            ],
            axis=0,
        )
        large = jnp.concatenate(
            [
                jnp.broadcast_to(
                    jnp.concatenate([large[:, n * leaf : n * leaf + leaf]] * KRON, axis=1), (KRON, D)
                )
                for n in range(terms)
            ],
            axis=0,
        )
        row = lax.broadcasted_iota(jnp.int32, (rows, D), 0)
        lane = lax.broadcasted_iota(jnp.int32, (rows, D), 1)
        self.diagonal = (row & 3) == block_of(lane, leaf, KRON)
        self.large = jnp.where(self.diagonal, large, 0.0)
        self.mix = self.core * self.small

    def matrix(self):
        return exact(self.mix.T, self.large) * self.factor

    def gradient(self, grad):
        sub, leaf = BOTTLE // KRON, D // KRON
        inner = self.factor * lax.dot_general(
            self.large, grad, (((1,), (1,)), ((), ())), preferred_element_type=f32
        )
        core = lax.dot_general(
            self.small * inner, self.pick, (((1,), (1,)), ((), ())), preferred_element_type=f32
        )
        core = jnp.sum(jnp.where(self.holds, core, 0.0), axis=0, keepdims=True)
        by_term = self.core * inner
        outer = self.factor * jnp.where(self.diagonal, nn(self.mix, grad), 0.0)
        small, large = [], []
        for n in range(KRON):
            row = jnp.sum(by_term[n * KRON : n * KRON + KRON, :], axis=0, keepdims=True)
            small.append(sum(row[:, b * sub : b * sub + sub] for b in range(KRON)))
            row = jnp.sum(outer[n * KRON : n * KRON + KRON, :], axis=0, keepdims=True)
            large.append(sum(row[:, a * leaf : a * leaf + leaf] for a in range(KRON)))
        return core, jnp.concatenate(small, axis=1), jnp.concatenate(large, axis=1)


def both_adapters(flat):
    widths = (KRON * KRON * KRON, D, BOTTLE, BOTTLE, D, BOTTLE, D)
    pieces, place = [], 0
    for width in widths:
        pieces.append(flat[:, place : place + width])
        place = place + width
    core, down_left, down_right, up_left, up_right, bias_down, bias_up = pieces
    down = Kronecker(core, down_right, down_left, (KRON * D) ** (-0.5), False)
    up = Kronecker(core, up_left, up_right, BOTTLE ** (-0.5), True)
    return down, up, bias_down, bias_up


def feed_forward_kernel(
    own_ref,
    len_ref,
    prob_hbm,
    q_hbm,
    k_hbm,
    v_hbm,
    ctx_hbm,
    shrink_hbm,
    x_hbm,
    grad_hbm,
    wo_own,
    wo_other,
    win_own,
    win_other,
    wout_own,
    wout_other,
    wq_own,
    wk_own,
    wv_own,
    wq_other,
    wk_other,
    wv_other,
    gain_attn_ref,
    gain_ffn_ref,
    flat_ref,
    out_hbm,
    grad_in_hbm,
    flat_grad_ref,
    ctx_ref,
    x_ref,
    grad_ref,
    wo_ref,
    win_ref,
    wout_ref,
    slope_ref,
    res_ref,
    res_grad_ref,
    delta_ref,
    shrink_ref,
    dqt_ref,
    sums_ref,
    low_ref,
    prob_ref,
    prob_sems,
    sems,
):
    start, ends = row_plan(len_ref, own_ref[0])
    half = wo_own.shape[0]
    hidden = win_own.shape[1]
    heads = half // DH
    chunks = 2 * hidden // FCHUNK

    def load(source, target, place):
        return pltpu.make_async_copy(source, target, sems.at[place])

    first = [
        load(ctx_hbm, ctx_ref, 0),
        load(wo_own, wo_ref.at[0:half, :], 1),
        load(wo_other, wo_ref.at[half : 2 * half, :], 2),
        load(x_hbm, x_ref, 3),
    ]
    ffn_loads = [
        load(win_own, win_ref.at[:, 0:hidden], 4),
        load(wout_own, wout_ref.at[0:hidden, :], 5),
        load(win_other, win_ref.at[:, hidden : 2 * hidden], 6),
        load(wout_other, wout_ref.at[hidden : 2 * hidden, :], 7),
    ]
    base = 10
    grad_load = load(grad_hbm, grad_ref, base)
    v_ref, k_ref, q_ref = (wout_ref.at[place * SEQ : place * SEQ + SEQ, :] for place in range(3))
    late = [
        load(v_hbm, v_ref, base + 1),
        load(k_hbm, k_ref, base + 3),
        load(q_hbm, q_ref, base + 2),
    ]
    shrink_load = load(shrink_hbm, shrink_ref, base + 4)
    out_copy = load(res_grad_ref, out_hbm, base + 5)
    out_pieces = [
        load(
            res_ref.at[piece * QB : piece * QB + QB, :], grad_in_hbm.at[piece * QB : piece * QB + QB, :], piece
        )
        for piece in range(NQ)
    ]
    qkv_loads = [
        load(source, win_ref.at[:, place * half : place * half + half], 4 + place)
        for place, source in enumerate((wq_own, wq_other, wk_own, wk_other, wv_own, wv_other))
    ]
    for copy in first:
        copy.start()
    for copy in ffn_loads:
        copy.start()
    grad_load.start()
    shrink_load.start()

    def prob_copy(it, count):
        slot, rows = lax.rem(it, 2), count * KB
        return pltpu.make_async_copy(
            prob_hbm.at[lax.div(it, NQ), :, lax.rem(it, NQ), 0:rows, :],
            prob_ref.at[slot, :, 0:rows, :],
            prob_sems.at[slot],
        )

    def with_span(it, action):
        first_row = lax.rem(it, NQ) * QB
        _, wide = key_window(ends, first_row, first_row + QB - 1)
        pl.when(wide)(functools.partial(action, it, SEQ // KB))
        pl.when(jnp.logical_not(wide))(functools.partial(action, it, MOST // KB))

    def fetch(it, count):
        prob_copy(it, count).start()

    def arrive(it, count):
        prob_copy(it, count).wait()

    with_span(jnp.int32(0), fetch)
    flat = flat_ref[...].reshape(1, flat_ref.shape[0])
    down_maker, up_maker, bias_down, bias_up = both_adapters(flat)
    down, up = down_maker.matrix().astype(bf16), up_maker.matrix().astype(bf16)
    gain = gain_ffn_ref[...].reshape(1, D)
    for copy in first:
        copy.wait()
    residual = x_ref[...].astype(f32) + tn(ctx_ref[...], wo_ref[...])
    res_ref[...] = residual
    scale = lax.rsqrt(jnp.mean(residual * residual, axis=1, keepdims=True) + eps_norm)
    low = (residual * scale * gain).astype(bf16)

    for copy in ffn_loads[:2]:
        copy.wait()
    low_ref[...] = low
    sums_ref[...] = jnp.zeros_like(sums_ref)

    def halves_of(chunk):
        return [places(chunk * FCHUNK + part * (FCHUNK // 2), FCHUNK // 2) for part in range(2)]

    def forward_chunk(chunk, carry):
        @pl.when(chunk == hidden // FCHUNK)
        def _other_side():
            for copy in ffn_loads[2:]:
                copy.wait()

        halves = halves_of(chunk)
        pre_acts = [nn(low_ref[...], win_ref[:, cols]) for cols in halves]
        for pre_act, cols in zip(pre_acts, halves):
            act, slope = gelu_both(pre_act)
            slope_ref[:, cols] = slope.astype(bf16)
            sums_ref[...] += nn(act.astype(bf16), wout_ref[cols, :])
        return carry

    lax.fori_loop(0, chunks, forward_chunk, 0)
    mixed = sums_ref[...]
    grad_load.wait()
    out_grad_low = grad_ref[...]
    mixed_low = mixed.astype(bf16)
    bottle, bottle_slope = gelu_both(nt(mixed_low, down) + bias_down)
    bottle_low = bottle.astype(bf16)
    sums_ref[...] = res_ref[...] + mixed + nn(bottle_low, up) + bias_up
    rotate_rows(sums_ref, res_grad_ref, SEQ - start)
    out_copy.start()
    bottle_grad = (nt(out_grad_low, up) * bottle_slope).astype(bf16)
    mixed_grad = (out_grad_low.astype(f32) + nn(bottle_grad, down)).astype(bf16)
    up_grad = tn(bottle_low, out_grad_low)
    down_grad = tn(bottle_grad, mixed_low)
    core_down, right_down, left_down = down_maker.gradient(down_grad)
    core_up, left_up, right_up = up_maker.gradient(up_grad)
    flat_grad = jnp.concatenate(
        [
            core_down + core_up,
            left_down,
            right_down,
            left_up,
            right_up,
            jnp.sum(bottle_grad.astype(f32), axis=0, keepdims=True),
            jnp.sum(out_grad_low.astype(f32), axis=0, keepdims=True),
        ],
        axis=1,
    )
    flat_grad_ref[...] = flat_grad.reshape(flat_grad_ref.shape[0])
    low_ref[...] = mixed_grad
    sums_ref[...] = jnp.zeros_like(sums_ref)

    def backward_chunk(chunk, carry):
        halves = halves_of(chunk)
        hidden_grads = [nt(low_ref[...], wout_ref[cols, :]) for cols in halves]
        for hidden_grad, cols in zip(hidden_grads, halves):
            pre_grad = (hidden_grad * slope_ref[:, cols].astype(f32)).astype(bf16)
            sums_ref[...] += nt(pre_grad, win_ref[:, cols])
        return carry

    lax.fori_loop(0, chunks, backward_chunk, 0)
    for copy in late + qkv_loads:
        copy.start()
    residual = res_ref[...]
    weighted = sums_ref[...] * gain
    inner = jnp.mean(residual * weighted, axis=1, keepdims=True)
    res_grad = grad_ref[...].astype(f32) + scale * weighted - residual * (scale * scale * scale * inner)
    out_copy.wait()
    res_grad_ref[...] = res_grad
    shrink_load.wait()
    shrink = jnp.concatenate([shrink_ref[0:heads, :], shrink_ref[8 : 8 + heads, :]], axis=0)
    shrink_top = shrink.astype(bf16)
    shrink_rest = (shrink - shrink_top.astype(f32)).astype(bf16)
    head_row = lax.broadcasted_iota(jnp.int32, (2 * heads, D), 0)
    head_lane = lax.broadcasted_iota(jnp.int32, (2 * heads, D), 1) >> 6
    spread = (head_row == head_lane).astype(bf16)
    shrink_wide = tn(shrink_top, spread) + tn(shrink_rest, spread)
    dctx = (nt(res_grad.astype(bf16), wo_ref[...]) * shrink_wide).astype(bf16)
    grad_ref[...] = dctx
    product = dctx.T.astype(f32) * ctx_ref[...].astype(f32)
    delta_ref[0 : 2 * heads, :] = jnp.sum(product.reshape(2 * heads, DH, SEQ), axis=1)
    for copy in late:
        copy.wait()
    kt_ref, dctx_ref = ctx_ref, grad_ref
    kt_ref[...] = k_ref[...].T

    def attend(it, part, carry):
        slot, group = lax.rem(it, 2), lax.div(it, NQ)
        first_row = lax.rem(it, NQ) * QB
        begin, _ = key_window(ends, first_row, first_row + QB - 1)
        key_rows = pl.ds(pl.multiple_of(begin * KB + part * MOST, KB), MOST)
        rows = pl.ds(pl.multiple_of(part * MOST, MOST), MOST)
        query_rows = pl.ds(pl.multiple_of(first_row, QB), QB)

        def lanes(pair):
            return places(group * half + pair * PAIR, PAIR)

        grads, prob_grads, score_grads, probs = [], [], [], []
        for head in range(heads):
            grads.append(one_head(dctx_ref[query_rows, lanes(head // 2)], head % 2))
            prob_grads.append(nt(v_ref[key_rows, lanes(head // 2)], grads[head]))
        for head in range(heads):
            delta = delta_ref[places(group * heads + head, 1), query_rows]
            probs.append(prob_ref[slot, head, rows, :])
            score_grads.append((probs[head].astype(f32) * (prob_grads[head] - delta)).astype(bf16))
        for pair in range(heads // 2):
            dk = dv = None
            for head in (2 * pair, 2 * pair + 1):
                band = places(group * half + head * DH, DH)
                queries = one_head(q_ref[query_rows, lanes(pair)], head % 2)
                dv_part = nn(probs[head], grads[head])
                dk_part = nn(score_grads[head], queries)
                dv = dv_part if dv is None else dv + dv_part
                dk = dk_part if dk is None else dk + dk_part
                dq = nn(kt_ref[band, key_rows], score_grads[head])
                before = jnp.where(part > 0, dqt_ref[band, query_rows].astype(f32), 0.0)
                dqt_ref[band, query_rows] = (before + dq).astype(bf16)
            sums_ref[key_rows, pair * PAIR : pair * PAIR + PAIR] += dk
            sums_ref[key_rows, half + pair * PAIR : half + pair * PAIR + PAIR] += dv
        return carry

    def one_block(it, carry):
        @pl.when(it + 1 < 2 * NQ)
        def _ahead():
            with_span(it + 1, fetch)

        with_span(it, arrive)
        first_row = lax.rem(it, NQ) * QB
        _, wide = key_window(ends, first_row, first_row + QB - 1)
        lax.fori_loop(0, jnp.where(wide, SEQ // MOST, 1), functools.partial(attend, it), 0)
        return carry

    def one_group(group, carry):
        sums_ref[...] = jnp.zeros_like(sums_ref)
        lax.fori_loop(group * NQ, group * NQ + NQ, one_block, 0)
        slope_ref[:, places((2 + group) * half, half)] = (sums_ref[:, 0:half] * (1.0 / log2_e)).astype(bf16)
        slope_ref[:, places((4 + group) * half, half)] = sums_ref[:, half : 2 * half].astype(bf16)
        return carry

    lax.fori_loop(0, 2, one_group, 0)
    slope_ref[:, 0 : 2 * half] = dqt_ref[...].T
    for copy in qkv_loads:
        copy.wait()

    def input_columns(part, carry):
        rows = pl.ds(pl.multiple_of(part * KB, KB), KB)
        sums_ref[:, rows] = nt(slope_ref[:, 0 : 6 * half], win_ref[rows, 0 : 6 * half])
        return carry

    lax.fori_loop(0, D // KB, input_columns, 0)
    normed_grad = sums_ref[...]
    inputs = x_ref[...].astype(f32)
    scale = lax.rsqrt(jnp.mean(inputs * inputs, axis=1, keepdims=True) + eps_norm)
    weighted = normed_grad * gain_attn_ref[...].reshape(1, D)
    inner = jnp.mean(inputs * weighted, axis=1, keepdims=True)
    sums_ref[...] = res_grad_ref[...] + scale * weighted - inputs * (scale * scale * scale * inner)
    rotate_pieces(sums_ref, res_ref, SEQ - start, NQ, lambda piece: out_pieces[piece].start())
    for copy in out_pieces:
        copy.wait()


def feed_forward_and_back(own, lengths, kept, x, out_grad, frozen, weights, gain_attn, gain_ffn, flat):
    any_space = pl.BlockSpec(memory_space=pl.ANY)
    vmem = pl.BlockSpec(memory_space=pltpu.VMEM)
    smem = pl.BlockSpec(memory_space=pltpu.SMEM)
    hidden = 2 * frozen[2].shape[1]
    heads = kept[0].shape[1]
    half = heads * DH
    return pl.pallas_call(
        feed_forward_kernel,
        in_specs=[smem, smem] + [any_space] * 20 + [vmem] * 3,
        out_specs=[any_space, any_space, vmem],
        out_shape=[
            jax.ShapeDtypeStruct((SEQ, D), f32),
            jax.ShapeDtypeStruct((SEQ, D), f32),
            jax.ShapeDtypeStruct(flat.shape, f32),
        ],
        scratch_shapes=[
            pltpu.VMEM((D, SEQ), bf16),
            pltpu.VMEM((SEQ, D), bf16),
            pltpu.VMEM((SEQ, D), bf16),
            pltpu.VMEM((D, D), bf16),
            pltpu.VMEM((D, hidden), bf16),
            pltpu.VMEM((hidden, D), bf16),
            pltpu.VMEM((SEQ, hidden), bf16),
            pltpu.VMEM((SEQ, D), f32),
            pltpu.VMEM((SEQ, D), f32),
            pltpu.VMEM((16, SEQ), f32),
            pltpu.VMEM((16, SEQ), f32),
            pltpu.VMEM((D, SEQ), bf16),
            pltpu.VMEM((SEQ, D), f32),
            pltpu.VMEM((SEQ, D), bf16),
            pltpu.VMEM((2, heads, SEQ, QB), bf16),
            pltpu.SemaphoreType.DMA((2,)),
            pltpu.SemaphoreType.DMA((17,)),
        ],
        compiler_params=pltpu.CompilerParams(vmem_limit_bytes=VMEM_BYTES),
        cost_estimate=pl.CostEstimate(flops=60 * 10**9, bytes_accessed=40 * 10**6, transcendentals=4 * 10**6),
        name="feed_forward_and_back",
    )(own, lengths, *kept, x, out_grad, *frozen, *weights, gain_attn, gain_ffn, flat)


def sum_everywhere(value):
    for axis in ("head", "dp"):
        size = lax.axis_size(axis)
        step = 1
        while step < size:
            value = value + lax.ppermute(value, axis, [(place, place ^ step) for place in range(size)])
            step = 2 * step
    return value


def on_device(
    hidden_in,
    lengths,
    buckets,
    gain_attn,
    gain_ffn,
    w_query,
    w_key,
    w_value,
    w_attn_out,
    w_in,
    w_ffn_out,
    rel_bias,
    out_grad,
    adapter_weights,
    first_moment,
    second_moment,
    ema_weights,
):
    swap = [(0, 1), (1, 0)]
    own = lax.axis_index("head").astype(jnp.int32).reshape(1)

    def other(value):
        return lax.ppermute(value, "head", swap)

    table = rel_bias.T
    own_qkv = (w_query, w_key, w_value)
    other_qkv = tuple(other(weight) for weight in own_qkv)
    other_table = other(table)
    packed, packed_grad = pack(own, lengths, hidden_in, out_grad)
    rest = lax.optimization_barrier((w_attn_out, w_in, w_ffn_out, packed))[:3]
    frozen = tuple(piece for weight in rest for piece in (weight, other(weight)))
    kept = attention_forward(
        own, lengths, packed, own_qkv + other_qkv, gain_attn, buckets, table, other_table
    )
    layer_out, grad_in, local_grad = feed_forward_and_back(
        own, lengths, kept, packed, packed_grad, frozen, own_qkv + other_qkv, gain_attn, gain_ffn, adapter_weights
    )
    total_grad = sum_everywhere(local_grad)
    new_first = beta_one * first_moment + (1.0 - beta_one) * total_grad
    new_second = beta_two * second_moment + (1.0 - beta_two) * total_grad * total_grad
    first_hat = new_first / (1.0 - beta_one**STEP)
    second_hat = new_second / (1.0 - beta_two**STEP)
    new_weights = adapter_weights - learn_rate * (
        first_hat / (jnp.sqrt(second_hat) + adam_eps) + weight_decay * adapter_weights
    )
    new_ema = ema_decay * ema_weights + (1.0 - ema_decay) * new_weights
    return (layer_out, grad_in, new_weights, new_first, new_second, new_ema)


def solution(mesh):
    placed = (
        P("dp", None),
        P("dp", None),
        P(),
        P(),
        P(),
        P(None, "head"),
        P(None, "head"),
        P(None, "head"),
        P("head", None),
        P(None, "head"),
        P("head", None),
        P(None, "head"),
        P(("dp", "head"), None),
        P(),
        P(),
        P(),
        P(),
    )
    return jax.shard_map(
        on_device,
        mesh=mesh,
        in_specs=placed,
        out_specs=(P(("dp", "head"), None), P(("dp", "head"), None), P(), P(), P(), P()),
        check_vma=False,
    )
```

```python
import functools

import jax
import jax.numpy as jnp
from jax import lax
from jax.experimental import pallas as pl
from jax.experimental.pallas import tpu as pltpu
from jax.sharding import PartitionSpec as P

D = 768
DH = 64
KRON = 4
BOTTLE = 48
SEQ = 1024
MOST = 512
STEP = 10
QB = 256
KB = 256
NQ = SEQ // QB
PAIR = 2 * DH
FCHUNK = 1024
REACH = QB + MOST - 128
SPREAD = REACH + MOST + QB
CODES = SPREAD + 128
VMEM_BYTES = 127 * 2**19

eps_norm = 1e-06
beta_one = 0.9
beta_two = 0.999
adam_eps = 1e-08
learn_rate = 0.6
weight_decay = 0.01
ema_decay = 0.9
masked_score = -1e30
log2_e = 1.4426950408889634
highest = lax.Precision.HIGHEST
f32 = jnp.float32
bf16 = jnp.bfloat16


def nn(left, right):
    return lax.dot_general(left, right, (((1,), (0,)), ((), ())), preferred_element_type=f32)


def nt(left, right):
    return lax.dot_general(left, right, (((1,), (1,)), ((), ())), preferred_element_type=f32)


def tn(left, right):
    return lax.dot_general(left, right, (((0,), (0,)), ((), ())), preferred_element_type=f32)


def row_plan(len_ref, own):
    docs = len_ref.shape[1]
    sizes = [len_ref[own, doc] for doc in range(docs)]
    longest, chosen = sizes[0], jnp.int32(0)
    for doc in range(1, docs):
        longer = sizes[doc] > longest
        chosen = jnp.where(longer, doc, chosen)
        longest = jnp.maximum(longest, sizes[doc])
    start = jnp.int32(0)
    for doc in range(docs):
        start = start + jnp.where(doc < chosen, sizes[doc], 0)
    ends, total = [], jnp.int32(0)
    for doc in range(docs):
        total = total + len_ref[own, lax.rem(chosen + doc, docs)]
        ends.append(total)
    return start, ends


def key_span(ends, first_row, last_row):
    begin, finish = jnp.int32(0), jnp.int32(SEQ)
    for end in ends:
        begin = jnp.where(end <= first_row, end, begin)
    for end in reversed(ends):
        finish = jnp.where(end > last_row, end, finish)
    return lax.div(begin, KB), lax.div(finish + (KB - 1), KB)


def rotate_rows(source_ref, target_ref, shift):
    groups = SEQ // 8
    fine, coarse = shift & 7, shift >> 3
    back = (8 - fine) & 7
    keep = lax.broadcasted_iota(jnp.int32, (8, target_ref.shape[1]), 0) < 8 - fine

    def turned(group):
        rows = source_ref[pl.ds(pl.multiple_of((group & (groups - 1)) * 8, 16), 16), :].astype(f32)
        return pltpu.roll(rows[0:8], back, 0), pltpu.roll(rows[8:16], back, 0)

    def some(part, carry):
        first, second = carry
        for pair in range(4):
            group = part * 8 + pair * 2
            third, fourth = turned(group + 2)
            for place, left, right in ((0, first, second), (1, second, third)):
                to = ((group + place - coarse) & (groups - 1)) * 8
                target_ref[pl.ds(pl.multiple_of(to, 8), 8), :] = jnp.where(keep, left, right)
            first, second = third, fourth
        return first, second

    lax.fori_loop(0, groups // 8, some, turned(jnp.int32(0)))


def rotate_pieces(source_ref, target_ref, shift, pieces, ready):
    groups = SEQ // 8
    fine, coarse = shift & 7, shift >> 3
    back = (8 - fine) & 7
    keep = lax.broadcasted_iota(jnp.int32, (8, target_ref.shape[1]), 0) < 8 - fine

    def turned(group):
        rows = source_ref[pl.ds(pl.multiple_of(((group + coarse) & (groups - 1)) * 8, 8), 8), :]
        return pltpu.roll(rows, back, 0)

    def some(part, before):
        for place in range(8):
            group = part * 8 + place
            after = turned(group + 1)
            target_ref[pl.ds(pl.multiple_of(group * 8, 8), 8), :] = jnp.where(keep, before, after)
            before = after
        return before

    steps = groups // 8 // pieces
    carry = turned(jnp.int32(0))
    for piece in range(pieces):
        carry = lax.fori_loop(piece * steps, piece * steps + steps, some, carry)
        ready(piece)


def one_head(pair, half):
    lane = lax.broadcasted_iota(jnp.int32, pair.shape, 1)
    keep = lane < DH if half == 0 else lane >= DH
    return jnp.where(keep, pair, jnp.zeros_like(pair))


def flip_lanes(value):
    tiles = value.shape[1] // 128
    row = lax.broadcasted_iota(jnp.int32, (128, 128), 0)
    lane = lax.broadcasted_iota(jnp.int32, (128, 128), 1)
    stacked = jnp.concatenate([value[:, tile * 128 : tile * 128 + 128] for tile in range(tiles)], axis=0)
    flipped = exact(stacked, (row + lane == 127).astype(f32))
    return jnp.concatenate([flipped[tile * 8 : tile * 8 + 8, :] for tile in reversed(range(tiles))], axis=1)


def exact(left, right):
    return lax.dot_general(
        left, right, (((1,), (0,)), ((), ())), precision=highest, preferred_element_type=f32
    )


def bias_rows(buckets_ref, table_ref, rows_ref, lead):
    heads = table_ref.shape[0]
    top = REACH + 128 + SEQ - 1
    codes = buckets_ref[...].reshape(1, 2 * SEQ - 1)[:, top - CODES + 1 : top + 1]
    bucket = lax.broadcasted_iota(jnp.int32, (table_ref.shape[1], CODES), 0)
    per_head = exact(table_ref[...] * log2_e, (bucket == codes).astype(f32))
    per_head = flip_lanes(jnp.concatenate([per_head, jnp.zeros((8 - heads, CODES), f32)], axis=0))
    rows_ref[lead : lead + heads, :] = per_head[0:heads, :]


def bias_band(rows_ref, bias_ref, head):
    spread = jnp.broadcast_to(rows_ref[pl.ds(head, 1), :], (128, CODES))
    spread = pltpu.roll(spread, CODES - 128, 1, stride=1, stride_axis=0)
    bias_ref[head] = spread[:, :SPREAD]


def places(first, width):
    return pl.ds(pl.multiple_of(first, width), width)


def key_window(ends, first_row, last_row):
    begin, finish = key_span(ends, first_row, last_row)
    wide = finish - begin > MOST // KB
    return jnp.where(wide, 0, jnp.minimum(begin, (SEQ - MOST) // KB)), wide


def pack_kernel(own_ref, len_ref, x_hbm, grad_hbm, packed_hbm, packed_grad_hbm, x_ref, grad_ref, turned_ref, sems):
    start, _ = row_plan(len_ref, own_ref[0])
    rows = pl.ds(pl.multiple_of(own_ref[0] * SEQ, SEQ), SEQ)
    loads = [
        pltpu.make_async_copy(x_hbm.at[rows, :], x_ref, sems.at[0]),
        pltpu.make_async_copy(grad_hbm, grad_ref, sems.at[1]),
    ]
    stores = [
        pltpu.make_async_copy(x_ref, packed_hbm, sems.at[2]),
        pltpu.make_async_copy(grad_ref, packed_grad_hbm, sems.at[3]),
    ]
    for load in loads:
        load.start()
    for load, store, ref in zip(loads, stores, (x_ref, grad_ref)):
        load.wait()
        rotate_rows(ref, turned_ref, start)
        ref[...] = turned_ref[...].astype(bf16)
        store.start()
    for store in stores:
        store.wait()


def pack(own, lengths, x, out_grad):
    any_space = pl.BlockSpec(memory_space=pl.ANY)
    smem = pl.BlockSpec(memory_space=pltpu.SMEM)
    return pl.pallas_call(
        pack_kernel,
        in_specs=[smem, smem, any_space, any_space],
        out_specs=[any_space, any_space],
        out_shape=[jax.ShapeDtypeStruct((SEQ, D), bf16)] * 2,
        scratch_shapes=[
            pltpu.VMEM((SEQ, D), bf16),
            pltpu.VMEM((SEQ, D), bf16),
            pltpu.VMEM((SEQ, D), f32),
            pltpu.SemaphoreType.DMA((4,)),
        ],
        compiler_params=pltpu.CompilerParams(vmem_limit_bytes=VMEM_BYTES),
        cost_estimate=pl.CostEstimate(flops=3 * 10**9, bytes_accessed=6 * 10**6, transcendentals=0),
        name="pack_rows",
    )(own, lengths, x, out_grad)


def attention_kernel(
    own_ref,
    len_ref,
    x_hbm,
    wq_own,
    wk_own,
    wv_own,
    wq_other,
    wk_other,
    wv_other,
    table_hbm,
    gain_ref,
    buckets_ref,
    table_own,
    prob_hbm,
    q_hbm,
    k_hbm,
    v_hbm,
    ctx_hbm,
    shrink_hbm,
    x_ref,
    w_ref,
    qkv_ref,
    vt_ref,
    ctx_ref,
    shrink_ref,
    table_other,
    rows_ref,
    bias_ref,
    dk_ref,
    dq_ref,
    prob_ref,
    prob_sems,
    ctx_sems,
    sems,
):
    heads = table_own.shape[0]
    half = heads * DH
    sources = (wq_own, wq_other, wk_own, wk_other, wv_own, wv_other)
    loads = [pltpu.make_async_copy(x_hbm, x_ref, sems.at[0])]
    for place, source in enumerate(sources):
        target = w_ref.at[:, place * half : place * half + half]
        loads.append(pltpu.make_async_copy(source, target, sems.at[1 + place]))
    table_load = pltpu.make_async_copy(table_hbm, table_other, sems.at[11])
    table_load.start()
    for load in loads:
        load.start()
    _, ends = row_plan(len_ref, own_ref[0])
    row = lax.broadcasted_iota(jnp.int32, dk_ref.shape, 0)
    dk_ref[...] = sum((row >= end).astype(jnp.int32) for end in ends)
    lane = lax.broadcasted_iota(jnp.int32, dq_ref.shape, 1)
    dq_ref[...] = sum((lane >= end).astype(jnp.int32) for end in ends)
    bias_rows(buckets_ref, table_own, rows_ref, 0)
    table_load.wait()
    bias_rows(buckets_ref, table_other, rows_ref, heads)
    loads[0].wait()
    inputs = x_ref[...].astype(f32)
    scale = lax.rsqrt(jnp.mean(inputs * inputs, axis=1, keepdims=True) + eps_norm)
    x_ref[...] = (inputs * scale * gain_ref[...].reshape(1, D)).astype(bf16)
    q_ref, k_ref, v_ref = (qkv_ref.at[place] for place in range(3))

    def project(place, carry):
        for part in range(3):

            @pl.when(place == part)
            def _arrive():
                loads[1 + 2 * part].wait()
                loads[2 + 2 * part].wait()

        columns = pl.ds(pl.multiple_of(place * D, D), D)
        projected = nn(x_ref[...], w_ref[:, columns])
        for head in range(2 * heads // 3):
            bias_band(rows_ref, bias_ref, place * (2 * heads // 3) + head)
        qkv_ref[place] = (projected * jnp.where(place == 0, log2_e, 1.0)).astype(bf16)
        return carry

    lax.fori_loop(0, 3, project, 0)
    vt_ref[...] = v_ref[...].T
    stores = [
        pltpu.make_async_copy(q_ref, q_hbm, sems.at[7]),
        pltpu.make_async_copy(k_ref, k_hbm, sems.at[8]),
        pltpu.make_async_copy(v_ref, v_hbm, sems.at[9]),
    ]
    for store in stores:
        store.start()

    def prob_copy(it, count):
        slot, rows = lax.rem(it, 2), count * KB
        return pltpu.make_async_copy(
            prob_ref.at[slot, :, 0:rows, :],
            prob_hbm.at[lax.div(it, NQ), :, lax.rem(it, NQ), 0:rows, :],
            prob_sems.at[slot],
        )

    def ctx_copy(it):
        query_rows = pl.ds(pl.multiple_of(lax.rem(it, NQ) * QB, QB), QB)
        band = pl.ds(pl.multiple_of(lax.div(it, NQ) * half, half), half)
        return pltpu.make_async_copy(
            ctx_ref.at[band, query_rows], ctx_hbm.at[band, query_rows], ctx_sems.at[it]
        )

    def with_span(it, action):
        first_row = lax.rem(it, NQ) * QB
        begin, wide = key_window(ends, first_row, first_row + QB - 1)
        pl.when(wide)(functools.partial(action, it, begin, SEQ // KB))
        pl.when(jnp.logical_not(wide))(functools.partial(action, it, begin, MOST // KB))

    def drain(it, begin, count):
        prob_copy(it, count).wait()

    def attend(it, begin, count):
        rows = count * KB
        slot, group = lax.rem(it, 2), lax.div(it, NQ)
        first_row, first_key = lax.rem(it, NQ) * QB, pl.multiple_of(begin * KB, KB)
        key_rows = pl.ds(first_key, rows)
        query_rows = pl.ds(pl.multiple_of(first_row, QB), QB)
        doc_key = jnp.concatenate([dk_ref[key_rows, :]] * (QB // 128), axis=1)
        same = doc_key == dq_ref[0:1, query_rows]

        bands = []
        for part in range(rows // 128):
            lane = jnp.clip(first_row - first_key + (REACH - part * 128), 0, SPREAD - QB)
            bands.append(pl.ds(pl.multiple_of(lane, 128), QB))

        def some_heads(members):
            scores, totals, probs = [], [], []
            for head in members:
                lanes = places(group * half + head // 2 * PAIR, PAIR)
                scores.append(nt(k_ref[key_rows, lanes], one_head(q_ref[query_rows, lanes], len(scores) % 2)))
            for head, score in zip(members, scores):
                bias = jnp.concatenate(
                    [bias_ref[group * heads + head, :, lanes] for lanes in bands], axis=0
                )
                score = jnp.where(same, score + bias, masked_score)
                expo = jnp.exp2(score - jnp.max(score, axis=0, keepdims=True))
                totals.append(1.0 / jnp.sum(expo, axis=0, keepdims=True))
                probs.append(expo.astype(bf16))
                prob_ref[slot, head, 0:rows, :] = probs[-1]
            for head, total, prob in zip(members, totals, probs):
                band = places(group * half + head * DH, DH)
                context = nn(vt_ref[band, key_rows], prob)
                ctx_ref[band, query_rows] = (context * total).astype(bf16)
                shrink_ref[places(group * 8 + head, 1), query_rows] = total

        if rows <= MOST:
            some_heads(range(heads))
        else:

            def one_pair(pair, carry):
                some_heads((2 * pair, 2 * pair + 1))
                return carry

            lax.fori_loop(0, heads // 2, one_pair, 0)
        prob_copy(it, count).start()
        ctx_copy(it).start()

    def one_block(it, carry):
        @pl.when(it >= 2)
        def _drain():
            with_span(it - 2, drain)

        with_span(it, attend)
        return carry

    lax.fori_loop(0, 2 * NQ, one_block, 0)
    stores.append(pltpu.make_async_copy(shrink_ref, shrink_hbm, sems.at[10]))
    stores[-1].start()
    with_span(jnp.int32(2 * NQ - 2), drain)
    with_span(jnp.int32(2 * NQ - 1), drain)
    for it in range(2 * NQ):
        ctx_copy(it).wait()
    for copy in stores:
        copy.wait()


def attention_forward(own, lengths, x, weights, gain, buckets, table_own, table_other):
    heads = table_own.shape[0]
    any_space = pl.BlockSpec(memory_space=pl.ANY)
    vmem = pl.BlockSpec(memory_space=pltpu.VMEM)
    smem = pl.BlockSpec(memory_space=pltpu.SMEM)
    return pl.pallas_call(
        attention_kernel,
        in_specs=[smem, smem] + [any_space] * 8 + [vmem] * 3,
        out_specs=[any_space] * 6,
        out_shape=[
            jax.ShapeDtypeStruct((2, heads, NQ, SEQ, QB), bf16),
            jax.ShapeDtypeStruct((SEQ, D), bf16),
            jax.ShapeDtypeStruct((SEQ, D), bf16),
            jax.ShapeDtypeStruct((SEQ, D), bf16),
            jax.ShapeDtypeStruct((D, SEQ), bf16),
            jax.ShapeDtypeStruct((16, SEQ), f32),
        ],
        scratch_shapes=[
            pltpu.VMEM((SEQ, D), bf16),
            pltpu.VMEM((D, 3 * D), bf16),
            pltpu.VMEM((3, SEQ, D), bf16),
            pltpu.VMEM((D, SEQ), bf16),
            pltpu.VMEM((D, SEQ), bf16),
            pltpu.VMEM((16, SEQ), f32),
            pltpu.VMEM(table_own.shape, f32),
            pltpu.VMEM((16, CODES), f32),
            pltpu.VMEM((2 * heads, 128, SPREAD), f32),
            pltpu.VMEM((SEQ, 128), jnp.int32),
            pltpu.VMEM((8, SEQ), jnp.int32),
            pltpu.VMEM((2, heads, SEQ, QB), bf16),
            pltpu.SemaphoreType.DMA((2,)),
            pltpu.SemaphoreType.DMA((2 * NQ,)),
            pltpu.SemaphoreType.DMA((12,)),
        ],
        compiler_params=pltpu.CompilerParams(vmem_limit_bytes=VMEM_BYTES),
        cost_estimate=pl.CostEstimate(flops=25 * 10**9, bytes_accessed=30 * 10**6, transcendentals=4 * 10**6),
        name="attention_forward",
    )(own, lengths, x, *weights, table_other, gain, buckets, table_own)


root_two_over_pi = 0.7978845608028654
cubic = 0.044715


def gelu_both(value):
    square = value * value
    slow = jnp.tanh(value * (root_two_over_pi + (root_two_over_pi * cubic) * square))
    half = 0.5 * value
    act = half + half * slow
    slope = (0.5 + 0.5 * slow) + half * (1.0 - slow * slow) * (
        root_two_over_pi + (3.0 * root_two_over_pi * cubic) * square
    )
    return act, slope


def block_of(index, width, blocks):
    return sum((index >= width * place).astype(jnp.int32) for place in range(1, blocks))


class Kronecker:
    def __init__(self, core, small, large, factor, swapped):
        terms, rows = KRON, KRON * KRON
        sub, leaf = BOTTLE // KRON, D // KRON
        self.factor = factor
        row = lax.broadcasted_iota(jnp.int32, (rows, rows * KRON), 0)
        item = lax.broadcasted_iota(jnp.int32, (rows, rows * KRON), 1)
        item_of = lax.broadcasted_iota(jnp.int32, (rows * KRON, BOTTLE), 0)
        lane_block = block_of(lax.broadcasted_iota(jnp.int32, (rows * KRON, BOTTLE), 1), sub, KRON)
        if swapped:
            self.holds = ((item >> 4) == (row >> 2)) & ((item & 3) == (row & 3))
            pick = ((item_of >> 2) & 3) == lane_block
        else:
            self.holds = (item >> 2) == row
            pick = (item_of & 3) == lane_block
        self.pick = pick.astype(f32)
        self.core = exact(jnp.where(self.holds, jnp.broadcast_to(core, self.holds.shape), 0.0), self.pick)
        self.small = jnp.concatenate(
            [
                jnp.broadcast_to(
                    jnp.concatenate([small[:, n * sub : n * sub + sub]] * KRON, axis=1), (KRON, BOTTLE)
                )
                for n in range(terms)
            ],
            axis=0,
        )
        large = jnp.concatenate(
            [
                jnp.broadcast_to(
                    jnp.concatenate([large[:, n * leaf : n * leaf + leaf]] * KRON, axis=1), (KRON, D)
                )
                for n in range(terms)
            ],
            axis=0,
        )
        row = lax.broadcasted_iota(jnp.int32, (rows, D), 0)
        lane = lax.broadcasted_iota(jnp.int32, (rows, D), 1)
        self.diagonal = (row & 3) == block_of(lane, leaf, KRON)
        self.large = jnp.where(self.diagonal, large, 0.0)
        self.mix = self.core * self.small

    def matrix(self):
        return exact(self.mix.T, self.large) * self.factor

    def gradient(self, grad):
        sub, leaf = BOTTLE // KRON, D // KRON
        inner = self.factor * lax.dot_general(
            self.large, grad, (((1,), (1,)), ((), ())), preferred_element_type=f32
        )
        core = lax.dot_general(
            self.small * inner, self.pick, (((1,), (1,)), ((), ())), preferred_element_type=f32
        )
        core = jnp.sum(jnp.where(self.holds, core, 0.0), axis=0, keepdims=True)
        by_term = self.core * inner
        outer = self.factor * jnp.where(self.diagonal, nn(self.mix, grad), 0.0)
        small, large = [], []
        for n in range(KRON):
            row = jnp.sum(by_term[n * KRON : n * KRON + KRON, :], axis=0, keepdims=True)
            small.append(sum(row[:, b * sub : b * sub + sub] for b in range(KRON)))
            row = jnp.sum(outer[n * KRON : n * KRON + KRON, :], axis=0, keepdims=True)
            large.append(sum(row[:, a * leaf : a * leaf + leaf] for a in range(KRON)))
        return core, jnp.concatenate(small, axis=1), jnp.concatenate(large, axis=1)


def both_adapters(flat):
    widths = (KRON * KRON * KRON, D, BOTTLE, BOTTLE, D, BOTTLE, D)
    pieces, place = [], 0
    for width in widths:
        pieces.append(flat[:, place : place + width])
        place = place + width
    core, down_left, down_right, up_left, up_right, bias_down, bias_up = pieces
    down = Kronecker(core, down_right, down_left, (KRON * D) ** (-0.5), False)
    up = Kronecker(core, up_left, up_right, BOTTLE ** (-0.5), True)
    return down, up, bias_down, bias_up


def feed_forward_kernel(
    own_ref,
    len_ref,
    prob_hbm,
    q_hbm,
    k_hbm,
    v_hbm,
    ctx_hbm,
    shrink_hbm,
    x_hbm,
    grad_hbm,
    wo_own,
    wo_other,
    win_own,
    win_other,
    wout_own,
    wout_other,
    wq_own,
    wk_own,
    wv_own,
    wq_other,
    wk_other,
    wv_other,
    gain_attn_ref,
    gain_ffn_ref,
    flat_ref,
    out_hbm,
    grad_in_hbm,
    flat_grad_ref,
    ctx_ref,
    x_ref,
    grad_ref,
    wo_ref,
    win_ref,
    wout_ref,
    slope_ref,
    res_ref,
    res_grad_ref,
    delta_ref,
    shrink_ref,
    dqt_ref,
    sums_ref,
    low_ref,
    prob_ref,
    prob_sems,
    sems,
):
    start, ends = row_plan(len_ref, own_ref[0])
    half = wo_own.shape[0]
    hidden = win_own.shape[1]
    heads = half // DH
    chunks = 2 * hidden // FCHUNK

    def load(source, target, place):
        return pltpu.make_async_copy(source, target, sems.at[place])

    first = [
        load(ctx_hbm, ctx_ref, 0),
        load(wo_own, wo_ref.at[0:half, :], 1),
        load(wo_other, wo_ref.at[half : 2 * half, :], 2),
        load(x_hbm, x_ref, 3),
    ]
    ffn_loads = [
        load(win_own, win_ref.at[:, 0:hidden], 4),
        load(wout_own, wout_ref.at[0:hidden, :], 5),
        load(win_other, win_ref.at[:, hidden : 2 * hidden], 6),
        load(wout_other, wout_ref.at[hidden : 2 * hidden, :], 7),
    ]
    base = 10
    grad_load = load(grad_hbm, grad_ref, base)
    v_ref, k_ref, q_ref = (wout_ref.at[place * SEQ : place * SEQ + SEQ, :] for place in range(3))
    late = [
        load(v_hbm, v_ref, base + 1),
        load(k_hbm, k_ref, base + 3),
        load(q_hbm, q_ref, base + 2),
    ]
    shrink_load = load(shrink_hbm, shrink_ref, base + 4)
    out_copy = load(res_grad_ref, out_hbm, base + 5)
    out_pieces = [
        load(
            res_ref.at[piece * QB : piece * QB + QB, :], grad_in_hbm.at[piece * QB : piece * QB + QB, :], piece
        )
        for piece in range(NQ)
    ]
    qkv_loads = [
        load(source, win_ref.at[:, place * half : place * half + half], 4 + place)
        for place, source in enumerate((wq_own, wq_other, wk_own, wk_other, wv_own, wv_other))
    ]
    for copy in first:
        copy.start()
    for copy in ffn_loads:
        copy.start()
    grad_load.start()
    shrink_load.start()

    def prob_copy(it, count):
        slot, rows = lax.rem(it, 2), count * KB
        return pltpu.make_async_copy(
            prob_hbm.at[lax.div(it, NQ), :, lax.rem(it, NQ), 0:rows, :],
            prob_ref.at[slot, :, 0:rows, :],
            prob_sems.at[slot],
        )

    def with_span(it, action):
        first_row = lax.rem(it, NQ) * QB
        _, wide = key_window(ends, first_row, first_row + QB - 1)
        pl.when(wide)(functools.partial(action, it, SEQ // KB))
        pl.when(jnp.logical_not(wide))(functools.partial(action, it, MOST // KB))

    def fetch(it, count):
        prob_copy(it, count).start()

    def arrive(it, count):
        prob_copy(it, count).wait()

    with_span(jnp.int32(0), fetch)
    flat = flat_ref[...].reshape(1, flat_ref.shape[0])
    down_maker, up_maker, bias_down, bias_up = both_adapters(flat)
    down, up = down_maker.matrix().astype(bf16), up_maker.matrix().astype(bf16)
    gain = gain_ffn_ref[...].reshape(1, D)
    for copy in first:
        copy.wait()
    residual = x_ref[...].astype(f32) + tn(ctx_ref[...], wo_ref[...])
    res_ref[...] = residual
    scale = lax.rsqrt(jnp.mean(residual * residual, axis=1, keepdims=True) + eps_norm)
    low = (residual * scale * gain).astype(bf16)

    for copy in ffn_loads[:2]:
        copy.wait()
    low_ref[...] = low
    sums_ref[...] = jnp.zeros_like(sums_ref)

    def halves_of(chunk):
        return [places(chunk * FCHUNK + part * (FCHUNK // 2), FCHUNK // 2) for part in range(2)]

    def forward_chunk(chunk, carry):
        @pl.when(chunk == hidden // FCHUNK)
        def _other_side():
            for copy in ffn_loads[2:]:
                copy.wait()

        halves = halves_of(chunk)
        pre_acts = [nn(low_ref[...], win_ref[:, cols]) for cols in halves]
        for pre_act, cols in zip(pre_acts, halves):
            act, slope = gelu_both(pre_act)
            slope_ref[:, cols] = slope.astype(bf16)
            sums_ref[...] += nn(act.astype(bf16), wout_ref[cols, :])
        return carry

    lax.fori_loop(0, chunks, forward_chunk, 0)
    mixed = sums_ref[...]
    grad_load.wait()
    out_grad_low = grad_ref[...]
    mixed_low = mixed.astype(bf16)
    bottle, bottle_slope = gelu_both(nt(mixed_low, down) + bias_down)
    bottle_low = bottle.astype(bf16)
    sums_ref[...] = res_ref[...] + mixed + nn(bottle_low, up) + bias_up
    rotate_rows(sums_ref, res_grad_ref, SEQ - start)
    out_copy.start()
    bottle_grad = (nt(out_grad_low, up) * bottle_slope).astype(bf16)
    mixed_grad = (out_grad_low.astype(f32) + nn(bottle_grad, down)).astype(bf16)
    up_grad = tn(bottle_low, out_grad_low)
    down_grad = tn(bottle_grad, mixed_low)
    bias_down_grad = jnp.sum(bottle_grad.astype(f32), axis=0, keepdims=True)
    bias_up_grad = jnp.sum(out_grad_low.astype(f32), axis=0, keepdims=True)
    low_ref[...] = mixed_grad
    sums_ref[...] = jnp.zeros_like(sums_ref)

    def backward_chunk(chunk, carry):
        halves = halves_of(chunk)
        hidden_grads = [nt(low_ref[...], wout_ref[cols, :]) for cols in halves]
        for hidden_grad, cols in zip(hidden_grads, halves):
            pre_grad = (hidden_grad * slope_ref[:, cols].astype(f32)).astype(bf16)
            sums_ref[...] += nt(pre_grad, win_ref[:, cols])
        return carry

    lax.fori_loop(0, chunks, backward_chunk, 0)
    for copy in late + qkv_loads:
        copy.start()
    residual = res_ref[...]
    weighted = sums_ref[...] * gain
    inner = jnp.mean(residual * weighted, axis=1, keepdims=True)
    res_grad = grad_ref[...].astype(f32) + scale * weighted - residual * (scale * scale * scale * inner)
    out_copy.wait()
    res_grad_ref[...] = res_grad
    shrink_load.wait()
    shrink = jnp.concatenate([shrink_ref[0:heads, :], shrink_ref[8 : 8 + heads, :]], axis=0)
    shrink_top = shrink.astype(bf16)
    shrink_rest = (shrink - shrink_top.astype(f32)).astype(bf16)
    head_row = lax.broadcasted_iota(jnp.int32, (2 * heads, D), 0)
    head_lane = lax.broadcasted_iota(jnp.int32, (2 * heads, D), 1) >> 6
    spread = (head_row == head_lane).astype(bf16)
    shrink_wide = tn(shrink_top, spread) + tn(shrink_rest, spread)
    dctx = (nt(res_grad.astype(bf16), wo_ref[...]) * shrink_wide).astype(bf16)
    core_down, right_down, left_down = down_maker.gradient(down_grad)
    core_up, left_up, right_up = up_maker.gradient(up_grad)
    flat_grad = jnp.concatenate(
        [
            core_down + core_up,
            left_down,
            right_down,
            left_up,
            right_up,
            bias_down_grad,
            bias_up_grad,
        ],
        axis=1,
    )
    flat_grad_ref[...] = flat_grad.reshape(flat_grad_ref.shape[0])
    grad_ref[...] = dctx
    product = dctx.T.astype(f32) * ctx_ref[...].astype(f32)
    delta_ref[0 : 2 * heads, :] = jnp.sum(product.reshape(2 * heads, DH, SEQ), axis=1)
    for copy in late:
        copy.wait()
    kt_ref, dctx_ref = ctx_ref, grad_ref
    kt_ref[...] = k_ref[...].T

    def attend(it, part, carry):
        slot, group = lax.rem(it, 2), lax.div(it, NQ)
        first_row = lax.rem(it, NQ) * QB
        begin, _ = key_window(ends, first_row, first_row + QB - 1)
        key_rows = pl.ds(pl.multiple_of(begin * KB + part * MOST, KB), MOST)
        rows = pl.ds(pl.multiple_of(part * MOST, MOST), MOST)
        query_rows = pl.ds(pl.multiple_of(first_row, QB), QB)

        def lanes(pair):
            return places(group * half + pair * PAIR, PAIR)

        grads, prob_grads, score_grads, probs = [], [], [], []
        for head in range(heads):
            grads.append(one_head(dctx_ref[query_rows, lanes(head // 2)], head % 2))
            prob_grads.append(nt(v_ref[key_rows, lanes(head // 2)], grads[head]))
        for head in range(heads):
            delta = delta_ref[places(group * heads + head, 1), query_rows]
            probs.append(prob_ref[slot, head, rows, :])
            score_grads.append((probs[head].astype(f32) * (prob_grads[head] - delta)).astype(bf16))
        for pair in range(heads // 2):
            dk = dv = None
            for head in (2 * pair, 2 * pair + 1):
                band = places(group * half + head * DH, DH)
                queries = one_head(q_ref[query_rows, lanes(pair)], head % 2)
                dv_part = nn(probs[head], grads[head])
                dk_part = nn(score_grads[head], queries)
                dv = dv_part if dv is None else dv + dv_part
                dk = dk_part if dk is None else dk + dk_part
                dq = nn(kt_ref[band, key_rows], score_grads[head])
                before = jnp.where(part > 0, dqt_ref[band, query_rows].astype(f32), 0.0)
                dqt_ref[band, query_rows] = (before + dq).astype(bf16)
            sums_ref[key_rows, pair * PAIR : pair * PAIR + PAIR] += dk
            sums_ref[key_rows, half + pair * PAIR : half + pair * PAIR + PAIR] += dv
        return carry

    def one_block(it, carry):
        @pl.when(it + 1 < 2 * NQ)
        def _ahead():
            with_span(it + 1, fetch)

        with_span(it, arrive)
        first_row = lax.rem(it, NQ) * QB
        _, wide = key_window(ends, first_row, first_row + QB - 1)
        lax.fori_loop(0, jnp.where(wide, SEQ // MOST, 1), functools.partial(attend, it), 0)
        return carry

    def one_group(group, carry):
        sums_ref[...] = jnp.zeros_like(sums_ref)
        lax.fori_loop(group * NQ, group * NQ + NQ, one_block, 0)
        slope_ref[:, places((2 + group) * half, half)] = (sums_ref[:, 0:half] * (1.0 / log2_e)).astype(bf16)
        slope_ref[:, places((4 + group) * half, half)] = sums_ref[:, half : 2 * half].astype(bf16)
        return carry

    lax.fori_loop(0, 2, one_group, 0)
    slope_ref[:, 0 : 2 * half] = dqt_ref[...].T
    for copy in qkv_loads:
        copy.wait()

    def input_columns(part, carry):
        rows = pl.ds(pl.multiple_of(part * KB, KB), KB)
        sums_ref[:, rows] = nt(slope_ref[:, 0 : 6 * half], win_ref[rows, 0 : 6 * half])
        return carry

    lax.fori_loop(0, D // KB, input_columns, 0)
    normed_grad = sums_ref[...]
    inputs = x_ref[...].astype(f32)
    scale = lax.rsqrt(jnp.mean(inputs * inputs, axis=1, keepdims=True) + eps_norm)
    weighted = normed_grad * gain_attn_ref[...].reshape(1, D)
    inner = jnp.mean(inputs * weighted, axis=1, keepdims=True)
    sums_ref[...] = res_grad_ref[...] + scale * weighted - inputs * (scale * scale * scale * inner)
    rotate_pieces(sums_ref, res_ref, SEQ - start, NQ, lambda piece: out_pieces[piece].start())
    for copy in out_pieces:
        copy.wait()


def feed_forward_and_back(own, lengths, kept, x, out_grad, frozen, weights, gain_attn, gain_ffn, flat):
    any_space = pl.BlockSpec(memory_space=pl.ANY)
    vmem = pl.BlockSpec(memory_space=pltpu.VMEM)
    smem = pl.BlockSpec(memory_space=pltpu.SMEM)
    hidden = 2 * frozen[2].shape[1]
    heads = kept[0].shape[1]
    half = heads * DH
    return pl.pallas_call(
        feed_forward_kernel,
        in_specs=[smem, smem] + [any_space] * 20 + [vmem] * 3,
        out_specs=[any_space, any_space, vmem],
        out_shape=[
            jax.ShapeDtypeStruct((SEQ, D), f32),
            jax.ShapeDtypeStruct((SEQ, D), f32),
            jax.ShapeDtypeStruct(flat.shape, f32),
        ],
        scratch_shapes=[
            pltpu.VMEM((D, SEQ), bf16),
            pltpu.VMEM((SEQ, D), bf16),
            pltpu.VMEM((SEQ, D), bf16),
            pltpu.VMEM((D, D), bf16),
            pltpu.VMEM((D, hidden), bf16),
            pltpu.VMEM((hidden, D), bf16),
            pltpu.VMEM((SEQ, hidden), bf16),
            pltpu.VMEM((SEQ, D), f32),
            pltpu.VMEM((SEQ, D), f32),
            pltpu.VMEM((16, SEQ), f32),
            pltpu.VMEM((16, SEQ), f32),
            pltpu.VMEM((D, SEQ), bf16),
            pltpu.VMEM((SEQ, D), f32),
            pltpu.VMEM((SEQ, D), bf16),
            pltpu.VMEM((2, heads, SEQ, QB), bf16),
            pltpu.SemaphoreType.DMA((2,)),
            pltpu.SemaphoreType.DMA((17,)),
        ],
        compiler_params=pltpu.CompilerParams(vmem_limit_bytes=VMEM_BYTES),
        cost_estimate=pl.CostEstimate(flops=60 * 10**9, bytes_accessed=40 * 10**6, transcendentals=4 * 10**6),
        name="feed_forward_and_back",
    )(own, lengths, *kept, x, out_grad, *frozen, *weights, gain_attn, gain_ffn, flat)


def sum_everywhere(value):
    for axis in ("head", "dp"):
        size = lax.axis_size(axis)
        step = 1
        while step < size:
            value = value + lax.ppermute(value, axis, [(place, place ^ step) for place in range(size)])
            step = 2 * step
    return value


def on_device(
    hidden_in,
    lengths,
    buckets,
    gain_attn,
    gain_ffn,
    w_query,
    w_key,
    w_value,
    w_attn_out,
    w_in,
    w_ffn_out,
    rel_bias,
    out_grad,
    adapter_weights,
    first_moment,
    second_moment,
    ema_weights,
):
    swap = [(0, 1), (1, 0)]
    own = lax.axis_index("head").astype(jnp.int32).reshape(1)

    def other(value):
        return lax.ppermute(value, "head", swap)

    table = rel_bias.T
    own_qkv = (w_query, w_key, w_value)
    other_qkv = tuple(other(weight) for weight in own_qkv)
    other_table = other(table)
    packed, packed_grad = pack(own, lengths, hidden_in, out_grad)
    rest = lax.optimization_barrier((w_attn_out, w_in, w_ffn_out, packed))[:3]
    frozen = tuple(piece for weight in rest for piece in (weight, other(weight)))
    kept = attention_forward(
        own, lengths, packed, own_qkv + other_qkv, gain_attn, buckets, table, other_table
    )
    layer_out, grad_in, local_grad = feed_forward_and_back(
        own, lengths, kept, packed, packed_grad, frozen, own_qkv + other_qkv, gain_attn, gain_ffn, adapter_weights
    )
    total_grad = sum_everywhere(local_grad)
    new_first = beta_one * first_moment + (1.0 - beta_one) * total_grad
    new_second = beta_two * second_moment + (1.0 - beta_two) * total_grad * total_grad
    first_hat = new_first / (1.0 - beta_one**STEP)
    second_hat = new_second / (1.0 - beta_two**STEP)
    new_weights = adapter_weights - learn_rate * (
        first_hat / (jnp.sqrt(second_hat) + adam_eps) + weight_decay * adapter_weights
    )
    new_ema = ema_decay * ema_weights + (1.0 - ema_decay) * new_weights
    return (layer_out, grad_in, new_weights, new_first, new_second, new_ema)


def solution(mesh):
    placed = (
        P("dp", None),
        P("dp", None),
        P(),
        P(),
        P(),
        P(None, "head"),
        P(None, "head"),
        P(None, "head"),
        P("head", None),
        P(None, "head"),
        P("head", None),
        P(None, "head"),
        P(("dp", "head"), None),
        P(),
        P(),
        P(),
        P(),
    )
    return jax.shard_map(
        on_device,
        mesh=mesh,
        in_specs=placed,
        out_specs=(P(("dp", "head"), None), P(("dp", "head"), None), P(), P(), P(), P()),
        check_vma=False,
    )
```
